32 devices in a mesh: lat: 4 (over y, x), lon: 8 (over z, core).
Axes of the slice: x: 2, y: 2, z: 4, core: 2. Of those that a mesh axis runs over, the one named last changes fastest.
Arguments:
- field: float32 [32, 1024, 1024], P(None, 'lat', 'lon'), may hold values from -300 to 300
- lon_rate: float32 [1024], replicated, may hold values from 0.06 to 0.15
- lat_rate: float32 [1024], replicated, may hold values from 0.06 to 0.15
Outputs:
- basis_field: bfloat16 [32, 1024, 1024], P(None, 'lat', 'lon')
- factor: float32 [32, 32], replicated
The draws below stay inside these ranges and needn't reach their ends.
All inputs are finite; a program needn't handle non-finite values.
Results may differ from the reference program's by a relative error of at most 0.001.
Values sent between devices are 32-bit elements; how exact they have to be, the bound alone decides.
No kernel may reach another device: no remote copies, remote signals or barrier semaphores. Data moves between devices by JAX's collectives and lax.ppermute only.
A program may use at most 64 MiB of HBM per device.

```python
import math
import jax
import jax.numpy as jnp
from jax import lax

SNAPS = 32
NLAT = 1024
NLON = 1024


def second_difference(values):
    rows_done = values[:, :-2, :] - 2.0 * values[:, 1:-1, :] + values[:, 2:, :]
    both_done = rows_done[:, :, :-2] - 2.0 * rows_done[:, :, 1:-1] + rows_done[:, :, 2:]
    return both_done / 6.0


def draw_field(key, part):
    key = jax.random.fold_in(key, 11)
    key_cols, key_rows, key_noise = jax.random.split(key, 3)
    col_scale = jnp.exp(jax.random.uniform(key_cols, (SNAPS,), jnp.float32, 0.0, math.log(3.0)))
    row_scale = jnp.exp(jax.random.uniform(key_rows, (NLAT,), jnp.float32, 0.0, math.log(3.0)))
    ramp_scale = 1.0 + 2.0 * jnp.arange(NLON).astype(jnp.float32) / max(NLON - 1, 1)
    noise = jnp.clip(jax.random.normal(key_noise, (SNAPS, NLAT + 2, NLON + 2), jnp.float32), -4.0, 4.0)
    source = second_difference(noise)
    scaled = source * col_scale[:, None, None] * row_scale[None, :, None] * ramp_scale[None, None, :]
    return scaled.astype(jnp.float32)


def setup_inputs(seed: int = 0) -> dict:
    key_of = jax.random.split(jax.random.key(seed), 4)
    return {
        "field": draw_field(jax.random.fold_in(key_of[3], 71), 0),
        "lon_rate": jnp.clip(jnp.exp(jax.random.uniform(key_of[1], (NLAT,), jnp.float32, math.log(0.06), math.log(0.15))), 0.06, 0.15),
        "lat_rate": jnp.clip(jnp.exp(jax.random.uniform(key_of[2], (NLAT,), jnp.float32, math.log(0.06), math.log(0.15))), 0.06, 0.15),
    }


stencil_weights = (-205.0 / 72.0, 8.0 / 5.0, -1.0 / 5.0, 8.0 / 315.0, -1.0 / 560.0)

def smooth_once(grid_field, zonal_rate, merid_rate):
    row_count = grid_field.shape[0]
    padded = jnp.pad(grid_field, ((4, 4), (0, 0)))
    zonal_part = stencil_weights[0] * grid_field
    merid_part = stencil_weights[0] * grid_field
    for offset in range(1, 5):
        zonal_part = zonal_part + stencil_weights[offset] * (jnp.roll(grid_field, offset, axis=1) + jnp.roll(grid_field, -offset, axis=1))
        merid_part = merid_part + stencil_weights[offset] * (padded[4 + offset:4 + offset + row_count] + padded[4 - offset:4 - offset + row_count])
    return grid_field + zonal_rate[:, None] * zonal_part + merid_rate[:, None] * merid_part

def area_weight(first_row, row_count, total_rows):
    row_index = (jnp.arange(row_count) + first_row).astype(jnp.float32)
    latitude = (-90.0 + (row_index + 0.5) * (180.0 / total_rows)) * (math.pi / 180.0)
    return jnp.sqrt(jnp.cos(latitude))

def reference(field, lon_rate, lat_rate):
    weights = area_weight(0, NLAT, NLAT)

    def smooth_snapshot(snapshot):
        smoothed = smooth_once(smooth_once(snapshot, lon_rate, lat_rate), lon_rate, lat_rate)
        return smoothed * weights[:, None]
    weighted = lax.map(smooth_snapshot, field)
    flat_field = weighted.reshape(SNAPS, NLAT * NLON)
    gram_matrix = jnp.dot(flat_field.astype(jnp.float32), flat_field.T.astype(jnp.float32), precision=lax.Precision.HIGHEST, preferred_element_type=jnp.float32)
    lower_factor = jnp.linalg.cholesky(gram_matrix)
    inverse = jax.scipy.linalg.solve_triangular(lower_factor, jnp.eye(SNAPS, dtype=jnp.float32), lower=True)
    root_count = math.sqrt(NLAT * NLON)
    basis_field = jnp.dot(inverse.astype(jnp.float32), flat_field.astype(jnp.float32), precision=lax.Precision.HIGHEST, preferred_element_type=jnp.float32) * root_count
    basis_field = basis_field.astype(jnp.bfloat16).reshape(SNAPS, NLAT, NLON)
    factor = lower_factor.T / root_count
    return (basis_field, factor)
```

```python
import functools
import math

import jax
import jax.numpy as jnp
import numpy as np
from jax import lax
from jax.experimental import pallas as pl
from jax.experimental.pallas import tpu as pltpu
from jax.sharding import PartitionSpec as P

stencil_weights = (-205.0 / 72.0, 8.0 / 5.0, -1.0 / 5.0, 8.0 / 315.0, -1.0 / 560.0)

HALO = 8
STRIP = 2 * HALO
LANES = 128
GROUPS = LANES // STRIP
TILE = 16
VMEM_BYTES = 48 * 1024 * 1024


def area_weight(first_row, row_count, total_rows):
    row_index = (jnp.arange(row_count) + first_row).astype(jnp.float32)
    latitude = (-90.0 + (row_index + 0.5) * (180.0 / total_rows)) * (math.pi / 180.0)
    return jnp.sqrt(jnp.cos(latitude))


def hi_lo(values):
    hi = values.astype(jnp.bfloat16)
    lo = (values - hi.astype(jnp.float32)).astype(jnp.bfloat16)
    return hi, lo


def band(in_cols, out_cols):
    offset = np.abs(np.asarray(in_cols)[:, None] - np.asarray(out_cols)[None, :])
    table = np.asarray(stencil_weights, np.float32)
    return np.where(offset <= 4, table[np.minimum(offset, 4)], np.float32(0.0)).astype(np.float32)


def two_terms(matrix):
    hi = matrix.astype(jnp.bfloat16)
    lo = (matrix - hi.astype(np.float32)).astype(jnp.bfloat16)
    return np.concatenate([hi, lo], axis=1)


def zonal_matrices():
    own = np.arange(LANES)
    outer = np.concatenate([np.arange(-HALO, 0), LANES + np.arange(HALO)])
    inner = np.concatenate([np.arange(LANES - HALO, LANES), np.arange(HALO)])
    main = two_terms(band(own, own))
    side = two_terms(band(outer, own))
    near = band(outer, outer)
    far = band(inner, outer)
    near[:HALO, HALO:] = near[HALO:, :HALO] = 0.0
    far[:HALO, :HALO] = far[HALO:, HALO:] = 0.0
    strip_near = np.zeros((LANES, LANES), np.float32)
    strip_far = np.zeros((LANES, LANES), np.float32)
    for group in range(GROUPS):
        at = slice(group * STRIP, (group + 1) * STRIP)
        strip_near[at, at] = near
        strip_far[at, at] = far
    strip_near, strip_far = two_terms(strip_near), two_terms(strip_far)
    return (
        np.concatenate([main, main], axis=0),
        side,
        np.concatenate([strip_near, strip_near, strip_far, strip_far], axis=0),
    )


def strip_kernel(span, field_ref, turned_ref, strip_ref):
    rows = turned_ref.shape[0]
    group_of = lax.broadcasted_iota(jnp.int32, (TILE, LANES), 1) // STRIP

    def body(at, carry):
        packed = jnp.zeros((TILE, LANES), jnp.float32)
        for group in range(GROUPS):
            row = jnp.clip(group * span + at - HALO, 0, rows - 1)
            values = field_ref[pl.ds(row, TILE, stride=rows), :]
            turned_ref[row] = values
            moved = pltpu.roll(values, (HALO + STRIP * group) % LANES, 1)
            packed = jnp.where(group_of == group, moved, packed)
        strip_ref[at] = packed
        return carry

    lax.fori_loop(0, span, body, 0)


def message_kernel(span, strip_ref, low_ref, high_ref, full_ref, first_ref, second_ref):
    snaps = strip_ref.shape[1]
    half = span // 2
    lane = lax.broadcasted_iota(jnp.int32, (snaps, LANES), 1)
    lat_even = lax.axis_index("lat") % 2 == 0
    lon_even = lax.axis_index("lon") % 2 == 0
    full_ref[...] = strip_ref[...]
    for at in range(HALO):
        first = low_ref[pl.ds(at, snaps, stride=HALO), :]
        second = high_ref[pl.ds(at, snaps, stride=HALO), :]
        north = jnp.where(lat_even, second, first)
        south = jnp.where(lat_even, first, second)
        full_ref[at] = jnp.where(lane < STRIP, pltpu.roll(north, HALO, 1), full_ref[at])
        last = span - HALO + at
        full_ref[last] = jnp.where(
            lane >= LANES - STRIP, pltpu.roll(south, LANES - HALO, 1), full_ref[last]
        )
    left = lane % STRIP < HALO
    for at in range(half):
        upper, lower = full_ref[at], full_ref[at + half]
        eastward = jnp.where(left, upper, pltpu.roll(lower, HALO, 1))
        westward = jnp.where(left, pltpu.roll(lower, LANES - HALO, 1), upper)
        first_ref[at] = jnp.where(lon_even, eastward, westward)
        second_ref[at] = jnp.where(lon_even, westward, eastward)


def stencil_row(center, pairs, zonal, zonal_rate, merid_rate):
    merid = stencil_weights[1] * pairs[0]
    for offset in range(2, 5):
        merid = merid + stencil_weights[offset] * pairs[offset - 1]
    scale = 1.0 + stencil_weights[0] * merid_rate
    return scale * center + merid_rate * merid + zonal_rate * zonal


def smooth_kernel(
    span,
    rates_ref,
    turned_ref,
    strip_ref,
    first_ref,
    second_ref,
    low_ref,
    high_ref,
    main_ref,
    side_ref,
    edge_ref,
    split_ref,
    gram_ref,
    ext_ref,
    once_ref,
    both_ref,
    weights_ref,
    outer_ref,
    near_ref,
    inner_ref,
    zonal_ref,
    strip_rates_ref,
    in_sem,
    out_sem,
):
    rows, snaps, _ = turned_ref.shape
    half = span // 2
    total = span * GROUPS
    tiles = snaps // TILE
    lat_even = lax.axis_index("lat") % 2 == 0
    lon_even = lax.axis_index("lon") % 2 == 0
    lane = lax.broadcasted_iota(jnp.int32, (TILE, LANES), 1)
    left = lane % STRIP < HALO

    def load(tile):
        return pltpu.make_async_copy(
            turned_ref.at[:, tile * TILE : (tile + 1) * TILE, :],
            ext_ref.at[tile, 4 + HALO : 4 + HALO + rows],
            in_sem.at[tile],
        )

    for tile in range(tiles):
        load(tile).start()
    for group in range(GROUPS):
        weights_ref[group, : 2 * LANES] = main_ref[...]
        weights_ref[group, 2 * LANES :] = jnp.zeros((2 * LANES, 2 * LANES), jnp.bfloat16)
        for part in (2, 3):
            begin = part * LANES + group * STRIP
            weights_ref[group, begin : begin + STRIP] = side_ref[...]
    group_of = lax.broadcasted_iota(jnp.int32, (8, LANES), 1) // STRIP
    for at in range(span):
        for kind in range(2):
            value = jnp.zeros((8, LANES), jnp.float32)
            for group in range(GROUPS):
                value = jnp.where(group_of == group, rates_ref[kind, group * span + at], value)
            strip_rates_ref[kind, at] = value

    def zonal(values, packed, weights):
        hi, lo = hi_lo(values)
        product = jnp.dot(
            jnp.concatenate([hi, lo, packed], axis=1), weights, preferred_element_type=jnp.float32
        )
        return product[:, :LANES] + product[:, LANES:]

    for tile in range(tiles):
        snap = slice(tile * TILE, (tile + 1) * TILE)
        for at in range(HALO):
            first = low_ref[pl.ds(tile * TILE * HALO + at, TILE, stride=HALO), :]
            second = high_ref[pl.ds(tile * TILE * HALO + at, TILE, stride=HALO), :]
            ext_ref[tile, 4 + at] = jnp.where(lat_even, second, first)
            ext_ref[tile, 4 + HALO + rows + at] = jnp.where(lat_even, first, second)
        for at in range(4):
            ext_ref[tile, at] = jnp.zeros((TILE, LANES), jnp.float32)
            ext_ref[tile, total + 4 + at] = jnp.zeros((TILE, LANES), jnp.float32)
        for at in range(half):
            first, second = first_ref[at, snap], second_ref[at, snap]
            west = jnp.where(lon_even, second, first)
            east = jnp.where(lon_even, first, second)
            outer_ref[4 + at] = jnp.where(left, west, east)
            outer_ref[4 + half + at] = jnp.where(
                left, pltpu.roll(west, LANES - HALO, 1), pltpu.roll(east, HALO, 1)
            )
        for at in range(4):
            outer_ref[at] = pltpu.roll(outer_ref[span + at], STRIP, 1)
            outer_ref[span + 4 + at] = pltpu.roll(outer_ref[4 + at], LANES - STRIP, 1)
        outer = outer_ref[4 : 4 + span].reshape(span * TILE, LANES)
        hi, lo = hi_lo(outer)
        near_ref[...] = jnp.concatenate([hi, lo], axis=1)
        own_hi, own_lo = hi_lo(strip_ref[:, snap].reshape(span * TILE, LANES))
        product = jnp.dot(
            jnp.concatenate([hi, lo, own_hi, own_lo], axis=1),
            edge_ref[...],
            preferred_element_type=jnp.float32,
        )
        zonal_ref[...] = (product[:, :LANES] + product[:, LANES:]).reshape(span, TILE, LANES)

        def strip_row(at, carry):
            pairs = [
                outer_ref[4 + at + offset] + outer_ref[4 + at - offset] for offset in range(1, 5)
            ]
            rates = [
                jnp.concatenate([strip_rates_ref[kind, at]] * (TILE // 8), axis=0)
                for kind in range(2)
            ]
            value = stencil_row(outer_ref[4 + at], pairs, zonal_ref[at], rates[0], rates[1])
            hi, lo = hi_lo(value)
            begin = pl.multiple_of(at * TILE, TILE)
            inner_ref[pl.ds(begin, TILE), :LANES] = hi
            inner_ref[pl.ds(begin, TILE), LANES:] = lo
            return carry

        lax.fori_loop(0, span, strip_row, 0)
        load(tile).wait()

        def first_pass(group, carry):
            begin = group * span
            center = ext_ref[tile, pl.ds(4 + begin, span)].reshape(span * TILE, LANES)
            part = zonal(center, near_ref[...], weights_ref[group]).reshape(span, TILE, LANES)
            for at in range(span):
                here = 4 + begin + at
                pairs = [
                    ext_ref[tile, here + offset] + ext_ref[tile, here - offset]
                    for offset in range(1, 5)
                ]
                once_ref[here] = stencil_row(
                    ext_ref[tile, here],
                    pairs,
                    part[at],
                    rates_ref[0, begin + at],
                    rates_ref[1, begin + at],
                )
            return carry

        lax.fori_loop(0, GROUPS, first_pass, 0)
        for at in range(4):
            once_ref[at] = jnp.zeros((TILE, LANES), jnp.float32)
            once_ref[total + 4 + at] = jnp.zeros((TILE, LANES), jnp.float32)

        def second_pass(group, carry):
            begin = group * span
            center = once_ref[pl.ds(4 + begin, span)].reshape(span * TILE, LANES)
            part = zonal(center, inner_ref[...], weights_ref[group]).reshape(span, TILE, LANES)
            for at in range(span):
                here = 4 + begin + at
                pairs = [
                    once_ref[here + offset] + once_ref[here - offset] for offset in range(1, 5)
                ]
                value = rates_ref[2, begin + at] * stencil_row(
                    once_ref[here],
                    pairs,
                    part[at],
                    rates_ref[0, begin + at],
                    rates_ref[1, begin + at],
                )
                hi, lo = hi_lo(value)
                both_ref[begin + at, tile * TILE : (tile + 1) * TILE] = hi
                both_ref[begin + at, snaps + tile * TILE : snaps + (tile + 1) * TILE] = lo
            return carry

        lax.fori_loop(0, GROUPS, second_pass, 0)

    store = pltpu.make_async_copy(both_ref.at[HALO : HALO + rows], split_ref, out_sem)
    store.start()

    def product(at, total):
        two = jnp.concatenate([both_ref[HALO + 2 * at], both_ref[HALO + 2 * at + 1]], axis=1)
        return total + lax.dot_general(
            two, two, (((1,), (1,)), ((), ())), preferred_element_type=jnp.float32
        )

    grams = lax.fori_loop(
        0, rows // 2, product, jnp.zeros((2 * snaps, 2 * snaps), jnp.float32), unroll=8
    )
    gram_ref[...] = (
        grams[:snaps, :snaps]
        + grams[snaps:, snaps:]
        + (grams[:snaps, snaps:] + grams[snaps:, :snaps])
    )
    store.wait()


def basis_kernel(root_count, gram_ref, split_ref, basis_ref, factor_ref, left_ref, wide_ref):
    snaps = gram_ref.shape[0]
    rows = split_ref.shape[0]

    @pl.when(pl.program_id(0) == 0)
    def _():
        row = lax.broadcasted_iota(jnp.int32, (snaps, 2 * snaps), 0)
        col = lax.broadcasted_iota(jnp.int32, (snaps, 2 * snaps), 1)
        work = jnp.concatenate([gram_ref[...], jnp.zeros((snaps, snaps), jnp.float32)], axis=1)
        work = jnp.where(col == row + snaps, 1.0, work)
        for step in range(snaps):
            pivot_row = work[step : step + 1, :]
            ratio = work[:, step : step + 1] / work[step : step + 1, step : step + 1]
            work = work - jnp.where(row > step, ratio, 0.0) * pivot_row
        diagonal = jnp.sum(jnp.where(row == col, work, 0.0), axis=1, keepdims=True)
        work = work * lax.rsqrt(diagonal)
        upper = jnp.where(col >= row, work, 0.0)
        factor_ref[...] = upper[:, :snaps] / root_count
        hi, lo = hi_lo(work[:, snaps:] * root_count)
        left_ref[:snaps] = jnp.concatenate([hi, hi], axis=1)
        left_ref[snaps:] = jnp.concatenate([lo, jnp.zeros_like(lo)], axis=1)

    left = left_ref[...]

    def body(at, carry):
        two = jnp.concatenate([split_ref[2 * at], split_ref[2 * at + 1]], axis=1)
        product = jnp.dot(left, two, preferred_element_type=jnp.float32)
        value = product[:snaps] + product[snaps:]
        wide_ref[pl.ds(2 * at, snaps, stride=rows), :] = value[:, :LANES]
        wide_ref[pl.ds(2 * at + 1, snaps, stride=rows), :] = value[:, LANES:]
        return carry

    lax.fori_loop(0, rows // 2, body, 0, unroll=4)
    for snap in range(snaps):
        basis_ref[snap] = wide_ref[snap * rows : (snap + 1) * rows].astype(jnp.bfloat16)


def pair_permutes(values, axis, periodic):
    count = lax.axis_size(axis)
    inner = [(i, i ^ 1) for i in range(count)]
    outer = []
    for i in range(1, count, 2):
        if periodic or i + 1 < count:
            outer += [(i, (i + 1) % count), ((i + 1) % count, i)]
    return lax.ppermute(values[0], axis, inner), lax.ppermute(values[1], axis, outer)


def sum_all(values):
    for axis in ("lon", "lat"):
        count = lax.axis_size(axis)
        step = 1
        while step < count:
            values = values + lax.ppermute(values, axis, [(i, i ^ step) for i in range(count)])
            step *= 2
    return values


def whole(memory_space=pltpu.VMEM):
    return pl.BlockSpec(memory_space=memory_space)


def shards(field, lon_rate, lat_rate):
    snaps, rows, cols = field.shape
    lat, lon = lax.axis_index("lat"), lax.axis_index("lon")
    row_start = lat * rows
    total_rows = rows * lax.axis_size("lat")
    total_cells = total_rows * cols * lax.axis_size("lon")
    span = (rows + 2 * HALO) // GROUPS
    tiles = snaps // TILE
    f32 = jnp.float32
    limits = pltpu.CompilerParams(vmem_limit_bytes=VMEM_BYTES)

    lat_even = lat % 2 == 0
    start = jnp.where(lat_even, rows - HALO, 0)
    other = rows - HALO - start
    edges = [
        lax.dynamic_slice_in_dim(field, begin, HALO, axis=1).reshape(snaps * HALO, cols)
        for begin in (start, other)
    ]
    low, high = pair_permutes(edges, "lat", False)

    turned, strip = pl.pallas_call(
        functools.partial(strip_kernel, span),
        grid=(tiles,),
        in_specs=[pl.BlockSpec((TILE * rows, cols), lambda i: (i, 0))],
        out_specs=[
            pl.BlockSpec((rows, TILE, cols), lambda i: (0, i, 0)),
            pl.BlockSpec((span, TILE, cols), lambda i: (0, i, 0)),
        ],
        out_shape=[
            jax.ShapeDtypeStruct((rows, snaps, cols), f32),
            jax.ShapeDtypeStruct((span, snaps, cols), f32),
        ],
        compiler_params=limits,
        name="turn_and_pack",
    )(field.reshape(snaps * rows, cols))

    half = jax.ShapeDtypeStruct((span // 2, snaps, cols), f32)
    strip, first, second = pl.pallas_call(
        functools.partial(message_kernel, span),
        in_specs=[whole()] * 3,
        out_specs=[whole()] * 3,
        out_shape=[jax.ShapeDtypeStruct(strip.shape, f32), half, half],
        compiler_params=limits,
        name="lon_messages",
    )(strip, low, high)
    first, second = pair_permutes([first, second], "lon", True)

    pad = jnp.zeros((HALO,), f32)
    rates = [
        lax.dynamic_slice_in_dim(jnp.concatenate([pad, rate, pad]), row_start, rows + 2 * HALO)
        for rate in (lon_rate, lat_rate)
    ]
    weight = jnp.concatenate([pad, area_weight(row_start, rows, total_rows), pad])
    rates = jnp.stack([rates[0], rates[1], weight])

    main, side, edge = zonal_matrices()
    total = span * GROUPS
    bf16 = jnp.bfloat16
    split, gram = pl.pallas_call(
        functools.partial(smooth_kernel, span),
        in_specs=[whole(pltpu.SMEM), whole(pl.ANY)] + [whole()] * 8,
        out_specs=[whole(pl.ANY), whole()],
        out_shape=[
            jax.ShapeDtypeStruct((rows, 2 * snaps, cols), bf16),
            jax.ShapeDtypeStruct((snaps, snaps), f32),
        ],
        scratch_shapes=[
            pltpu.VMEM((tiles, total + 8, TILE, cols), f32),
            pltpu.VMEM((total + 8, TILE, cols), f32),
            pltpu.VMEM((total, 2 * snaps, cols), bf16),
            pltpu.VMEM((GROUPS, 4 * LANES, 2 * LANES), bf16),
            pltpu.VMEM((span + 8, TILE, cols), f32),
            pltpu.VMEM((span * TILE, 2 * LANES), bf16),
            pltpu.VMEM((span * TILE, 2 * LANES), bf16),
            pltpu.VMEM((span, TILE, cols), f32),
            pltpu.VMEM((2, span, 8, cols), f32),
            pltpu.SemaphoreType.DMA((tiles,)),
            pltpu.SemaphoreType.DMA,
        ],
        compiler_params=limits,
        name="smooth_and_gram",
    )(rates, turned, strip, first, second, low, high, main, side, edge)

    gram = sum_all(gram)
    block = 64
    basis, factor = pl.pallas_call(
        functools.partial(basis_kernel, math.sqrt(total_cells)),
        grid=(rows // block,),
        in_specs=[
            pl.BlockSpec((snaps, snaps), lambda i: (0, 0)),
            pl.BlockSpec((block, 2 * snaps, cols), lambda i: (i, 0, 0)),
        ],
        out_specs=[
            pl.BlockSpec((snaps, block, cols), lambda i: (0, i, 0)),
            pl.BlockSpec((snaps, snaps), lambda i: (0, 0)),
        ],
        out_shape=[
            jax.ShapeDtypeStruct((snaps, rows, cols), bf16),
            jax.ShapeDtypeStruct((snaps, snaps), f32),
        ],
        scratch_shapes=[
            pltpu.VMEM((2 * snaps, 2 * snaps), bf16),
            pltpu.VMEM((snaps * block, cols), f32),
        ],
        compiler_params=limits,
        name="factor_and_basis",
    )(gram, split)
    return (basis, factor)


def solution(mesh):
    return jax.shard_map(
        shards,
        mesh=mesh,
        in_specs=(P(None, "lat", "lon"), P(), P()),
        out_specs=(P(None, "lat", "lon"), P()),
        check_vma=False,
    )
```

```python
import functools
import math

import jax
import jax.numpy as jnp
import numpy as np
from jax import lax
from jax.experimental import pallas as pl
from jax.experimental.pallas import tpu as pltpu
from jax.sharding import PartitionSpec as P

stencil_weights = (-205.0 / 72.0, 8.0 / 5.0, -1.0 / 5.0, 8.0 / 315.0, -1.0 / 560.0)

HALO = 8
STRIP = 2 * HALO
LANES = 128
GROUPS = LANES // STRIP
TILE = 16
VMEM_BYTES = 40 * 1024 * 1024


def area_weight(first_row, row_count, total_rows):
    row_index = (jnp.arange(row_count) + first_row).astype(jnp.float32)
    latitude = (-90.0 + (row_index + 0.5) * (180.0 / total_rows)) * (math.pi / 180.0)
    return jnp.sqrt(jnp.cos(latitude))


def hi_lo(values):
    hi = values.astype(jnp.bfloat16)
    lo = (values - hi.astype(jnp.float32)).astype(jnp.bfloat16)
    return hi, lo


def band(in_cols, out_cols):
    offset = np.abs(np.asarray(in_cols)[:, None] - np.asarray(out_cols)[None, :])
    table = np.asarray(stencil_weights, np.float32)
    return np.where(offset <= 4, table[np.minimum(offset, 4)], np.float32(0.0)).astype(np.float32)


def two_terms(matrix):
    hi = matrix.astype(jnp.bfloat16)
    lo = (matrix - hi.astype(np.float32)).astype(jnp.bfloat16)
    return np.concatenate([hi, lo], axis=1)


def zonal_matrices():
    own = np.arange(LANES)
    outer = np.concatenate([np.arange(-HALO, 0), LANES + np.arange(HALO)])
    inner = np.concatenate([np.arange(LANES - HALO, LANES), np.arange(HALO)])
    main = two_terms(band(own, own))
    side = two_terms(band(outer, own))
    near = band(outer, outer)
    far = band(inner, outer)
    near[:HALO, HALO:] = near[HALO:, :HALO] = 0.0
    far[:HALO, :HALO] = far[HALO:, HALO:] = 0.0
    strip_near = np.zeros((LANES, LANES), np.float32)
    strip_far = np.zeros((LANES, LANES), np.float32)
    for group in range(GROUPS):
        at = slice(group * STRIP, (group + 1) * STRIP)
        strip_near[at, at] = near
        strip_far[at, at] = far
    strip_near, strip_far = two_terms(strip_near), two_terms(strip_far)
    return (
        np.concatenate([main, main], axis=0),
        side,
        np.concatenate([strip_near, strip_near, strip_far, strip_far], axis=0),
    )


def turn_rows(field_ref, rows, store):
    def body(at, carry):
        begin = pl.multiple_of(at * 8, 8)
        store(begin, jnp.swapaxes(field_ref[:, pl.ds(begin, 8), :], 0, 1))
        return carry

    lax.fori_loop(0, rows // 8, body, 0, unroll=4)


def strip_kernel(span, field_ref, strip_ref, first_ref, second_ref, turned_ref):
    tile, rows, _ = field_ref.shape
    lat_even = lax.axis_index("lat") % 2 == 0
    north = field_ref[:, :HALO].reshape(tile * HALO, LANES)
    south = field_ref[:, rows - HALO :].reshape(tile * HALO, LANES)
    first_ref[...] = jnp.where(lat_even, south, north)
    second_ref[...] = jnp.where(lat_even, north, south)
    group_of = lax.broadcasted_iota(jnp.int32, (tile, LANES), 1) // STRIP

    def store(begin, values):
        turned_ref[pl.ds(HALO + begin, 8)] = values

    turn_rows(field_ref, rows, store)
    for at in range(HALO):
        turned_ref[at] = jnp.zeros((tile, LANES), jnp.float32)
        turned_ref[HALO + rows + at] = jnp.zeros((tile, LANES), jnp.float32)

    def body(at, carry):
        packed = jnp.zeros((tile, LANES), jnp.float32)
        for group in range(GROUPS):
            values = turned_ref[group * span + at]
            moved = pltpu.roll(values, (HALO + STRIP * group) % LANES, 1)
            packed = jnp.where(group_of == group, moved, packed)
        strip_ref[at] = packed
        return carry

    lax.fori_loop(0, span, body, 0, unroll=2)


def message_kernel(span, strip_ref, low_ref, high_ref, full_ref, first_ref, second_ref):
    snaps = strip_ref.shape[1]
    half = span // 2
    lane = lax.broadcasted_iota(jnp.int32, (snaps, LANES), 1)
    lat_even = lax.axis_index("lat") % 2 == 0
    lon_even = lax.axis_index("lon") % 2 == 0
    full_ref[...] = strip_ref[...]
    for at in range(HALO):
        first = low_ref[pl.ds(at, snaps, stride=HALO), :]
        second = high_ref[pl.ds(at, snaps, stride=HALO), :]
        north = jnp.where(lat_even, second, first)
        south = jnp.where(lat_even, first, second)
        full_ref[at] = jnp.where(lane < STRIP, pltpu.roll(north, HALO, 1), full_ref[at])
        last = span - HALO + at
        full_ref[last] = jnp.where(
            lane >= LANES - STRIP, pltpu.roll(south, LANES - HALO, 1), full_ref[last]
        )
    left = lane % STRIP < HALO
    for at in range(half):
        upper, lower = full_ref[at], full_ref[at + half]
        eastward = jnp.where(left, upper, pltpu.roll(lower, HALO, 1))
        westward = jnp.where(left, pltpu.roll(lower, LANES - HALO, 1), upper)
        first_ref[at] = jnp.where(lon_even, eastward, westward)
        second_ref[at] = jnp.where(lon_even, westward, eastward)


def stencil_row(center, pairs, zonal, zonal_rate, merid_rate):
    merid = stencil_weights[1] * pairs[0]
    for offset in range(2, 5):
        merid = merid + stencil_weights[offset] * pairs[offset - 1]
    scale = 1.0 + stencil_weights[0] * merid_rate
    return scale * center + merid_rate * merid + zonal_rate * zonal


def zonal_terms(parts, weights):
    product = jnp.dot(
        jnp.concatenate(parts, axis=1), weights, preferred_element_type=jnp.float32
    )
    return product[:, :LANES] + product[:, LANES:]


def stencil_rows(source_ref, begin, span, part, rates_ref, store):
    loaded = {}

    def row(at):
        if at not in loaded:
            loaded[at] = source_ref[begin + at]
        return loaded[at]

    for at in range(span):
        here = at + 4
        pairs = [row(here + offset) + row(here - offset) for offset in range(1, 5)]
        store(
            at,
            stencil_row(
                row(here), pairs, part[at], rates_ref[0, begin + at], rates_ref[1, begin + at]
            ),
        )


def first_kernel(span, rates_ref, field_ref, low_ref, high_ref, main_ref, once_ref, ext_ref):
    rows = field_ref.shape[1]
    total = span * GROUPS
    lat_even = lax.axis_index("lat") % 2 == 0
    for at in range(HALO):
        first = low_ref[pl.ds(at, TILE, stride=HALO), :]
        second = high_ref[pl.ds(at, TILE, stride=HALO), :]
        ext_ref[4 + at] = jnp.where(lat_even, second, first)
        ext_ref[4 + HALO + rows + at] = jnp.where(lat_even, first, second)
    for at in range(4):
        ext_ref[at] = jnp.zeros((TILE, LANES), jnp.float32)
        ext_ref[total + 4 + at] = jnp.zeros((TILE, LANES), jnp.float32)
        once_ref[at] = jnp.zeros((TILE, LANES), jnp.float32)
        once_ref[total + 4 + at] = jnp.zeros((TILE, LANES), jnp.float32)

    def turn(begin, values):
        ext_ref[pl.ds(4 + HALO + begin, 8)] = values

    turn_rows(field_ref, rows, turn)

    def body(group, carry):
        begin = group * span
        center = ext_ref[pl.ds(4 + begin, span)].reshape(span * TILE, LANES)
        part = zonal_terms(hi_lo(center), main_ref[...]).reshape(span, TILE, LANES)

        def store(at, value):
            once_ref[4 + begin + at] = value

        stencil_rows(ext_ref, begin, span, part, rates_ref, store)
        return carry

    lax.fori_loop(0, GROUPS, body, 0)


def second_kernel(
    span,
    rates_ref,
    once_ref,
    strip_ref,
    first_ref,
    second_ref,
    main_ref,
    side_ref,
    edge_ref,
    split_ref,
    gram_ref,
    full_ref,
    weights_ref,
    outer_ref,
    near_ref,
    inner_ref,
    zonal_ref,
    strip_rates_ref,
):
    both = split_ref.shape[1]
    rows = split_ref.shape[0] - HALO
    snaps = both // 2
    half = span // 2
    tile = pl.program_id(0)
    lon_even = lax.axis_index("lon") % 2 == 0
    lane = lax.broadcasted_iota(jnp.int32, (TILE, LANES), 1)
    left = lane % STRIP < HALO

    @pl.when(tile == 0)
    def _():
        for group in range(GROUPS):
            weights_ref[group, : 2 * LANES] = main_ref[...]
            weights_ref[group, 2 * LANES :] = jnp.zeros((2 * LANES, 2 * LANES), jnp.bfloat16)
            for part in (2, 3):
                begin = part * LANES + group * STRIP
                weights_ref[group, begin : begin + STRIP] = side_ref[...]
        group_of = lax.broadcasted_iota(jnp.int32, (8, LANES), 1) // STRIP
        for at in range(span):
            for kind in range(2):
                value = jnp.zeros((8, LANES), jnp.float32)
                for group in range(GROUPS):
                    value = jnp.where(group_of == group, rates_ref[kind, group * span + at], value)
                strip_rates_ref[kind, at] = value

    for at in range(half):
        first, second = first_ref[at], second_ref[at]
        west = jnp.where(lon_even, second, first)
        east = jnp.where(lon_even, first, second)
        outer_ref[4 + at] = jnp.where(left, west, east)
        outer_ref[4 + half + at] = jnp.where(
            left, pltpu.roll(west, LANES - HALO, 1), pltpu.roll(east, HALO, 1)
        )
    for at in range(4):
        outer_ref[at] = pltpu.roll(outer_ref[span + at], STRIP, 1)
        outer_ref[span + 4 + at] = pltpu.roll(outer_ref[4 + at], LANES - STRIP, 1)
    hi, lo = hi_lo(outer_ref[4 : 4 + span].reshape(span * TILE, LANES))
    near_ref[...] = jnp.concatenate([hi, lo], axis=1)
    own_hi, own_lo = hi_lo(strip_ref[...].reshape(span * TILE, LANES))
    zonal_ref[...] = zonal_terms([hi, lo, own_hi, own_lo], edge_ref[...]).reshape(
        span, TILE, LANES
    )

    def strip_row(at, carry):
        pairs = [outer_ref[4 + at + offset] + outer_ref[4 + at - offset] for offset in range(1, 5)]
        rates = [
            jnp.concatenate([strip_rates_ref[kind, at]] * (TILE // 8), axis=0) for kind in range(2)
        ]
        value = stencil_row(outer_ref[4 + at], pairs, zonal_ref[at], rates[0], rates[1])
        hi, lo = hi_lo(value)
        begin = pl.multiple_of(at * TILE, TILE)
        inner_ref[pl.ds(begin, TILE), :LANES] = hi
        inner_ref[pl.ds(begin, TILE), LANES:] = lo
        return carry

    lax.fori_loop(0, span, strip_row, 0, unroll=2)

    def complete(group, carry):
        begin = group * span
        part = zonal_terms([near_ref[...]], weights_ref[group, 2 * LANES :]).reshape(
            span, TILE, LANES
        )
        for at in range(span):
            here = 4 + begin + at
            full_ref[here] = once_ref[here] + rates_ref[0, begin + at] * part[at]
        return carry

    lax.fori_loop(0, GROUPS, complete, 0)
    for at in range(4):
        full_ref[at] = once_ref[at]
        full_ref[span * GROUPS + 4 + at] = once_ref[span * GROUPS + 4 + at]

    def second_pass(group, carry):
        begin = group * span
        center = full_ref[pl.ds(4 + begin, span)].reshape(span * TILE, LANES)
        hi, lo = hi_lo(center)
        part = zonal_terms([hi, lo, inner_ref[...]], weights_ref[group]).reshape(
            span, TILE, LANES
        )

        def store(at, value):
            hi, lo = hi_lo(rates_ref[2, begin + at] * value)
            row = jnp.maximum(begin + at - HALO, 0)
            split_ref[row, pl.ds(pl.multiple_of(tile * TILE, TILE), TILE)] = hi
            split_ref[row, pl.ds(pl.multiple_of(snaps + tile * TILE, TILE), TILE)] = lo

        stencil_rows(full_ref, begin, span, part, rates_ref, store)
        return carry

    lax.fori_loop(0, GROUPS, second_pass, 0)

    @pl.when(tile == snaps // TILE - 1)
    def _():
        def product(at, total):
            two = jnp.concatenate([split_ref[2 * at], split_ref[2 * at + 1]], axis=1)
            return total + lax.dot_general(
                two, two, (((1,), (1,)), ((), ())), preferred_element_type=jnp.float32
            )

        grams = lax.fori_loop(
            0, rows // 2, product, jnp.zeros((both, both), jnp.float32), unroll=8
        )
        gram_ref[...] = (
            grams[:snaps, :snaps]
            + grams[snaps:, snaps:]
            + (grams[:snaps, snaps:] + grams[snaps:, :snaps])
        )


def basis_kernel(root_count, gram_ref, split_ref, basis_ref, factor_ref, left_ref):
    snaps = gram_ref.shape[0]

    @pl.when(pl.program_id(0) == 0)
    def _():
        row = lax.broadcasted_iota(jnp.int32, (snaps, 2 * snaps), 0)
        col = lax.broadcasted_iota(jnp.int32, (snaps, 2 * snaps), 1)
        work = jnp.concatenate([gram_ref[...], jnp.zeros((snaps, snaps), jnp.float32)], axis=1)
        work = jnp.where(col == row + snaps, 1.0, work)
        for step in range(snaps):
            pivot_row = work[step : step + 1, :]
            ratio = work[:, step : step + 1] / work[step : step + 1, step : step + 1]
            work = work - jnp.where(row > step, ratio, 0.0) * pivot_row
        diagonal = jnp.sum(jnp.where(row == col, work, 0.0), axis=1, keepdims=True)
        work = work * lax.rsqrt(diagonal)
        upper = jnp.where(col >= row, work, 0.0)
        factor_ref[...] = upper[:, :snaps] / root_count
        hi, lo = hi_lo(work[:, snaps:] * root_count)
        left_ref[:snaps] = jnp.concatenate([hi, hi], axis=1)
        left_ref[snaps:] = jnp.concatenate([lo, jnp.zeros_like(lo)], axis=1)

    left = left_ref[...]
    start = pl.program_id(0) * basis_ref.shape[1]

    def body(at, carry):
        begin = pl.multiple_of(at * 16, 16)
        values = []
        for pair in range(8):
            row = start + begin + 2 * pair
            two = jnp.concatenate([split_ref[row], split_ref[row + 1]], axis=1)
            product = jnp.dot(left, two, preferred_element_type=jnp.float32)
            value = product[:snaps] + product[snaps:]
            values += [value[:, :LANES], value[:, LANES:]]
        turned = jnp.swapaxes(jnp.stack(values, axis=0), 0, 1)
        basis_ref[:, pl.ds(begin, 16), :] = turned.astype(jnp.bfloat16)
        return carry

    lax.fori_loop(0, basis_ref.shape[1] // 16, body, 0)


def pair_permutes(values, axis, periodic):
    count = lax.axis_size(axis)
    inner = [(i, i ^ 1) for i in range(count)]
    outer = []
    for i in range(1, count, 2):
        if periodic or i + 1 < count:
            outer += [(i, (i + 1) % count), ((i + 1) % count, i)]
    return lax.ppermute(values[0], axis, inner), lax.ppermute(values[1], axis, outer)


def sum_all(values):
    for axis in ("lon", "lat"):
        count = lax.axis_size(axis)
        step = 1
        while step < count:
            values = values + lax.ppermute(values, axis, [(i, i ^ step) for i in range(count)])
            step *= 2
    return values


def whole(memory_space=pltpu.VMEM):
    return pl.BlockSpec(memory_space=memory_space)


def shards(field, lon_rate, lat_rate):
    snaps, rows, cols = field.shape
    row_start = lax.axis_index("lat") * rows
    total_rows = rows * lax.axis_size("lat")
    total_cells = total_rows * cols * lax.axis_size("lon")
    span = (rows + 2 * HALO) // GROUPS
    tiles = snaps // TILE
    f32 = jnp.float32
    limits = pltpu.CompilerParams(vmem_limit_bytes=VMEM_BYTES)

    edge_rows = pl.BlockSpec((8 * HALO, cols), lambda i: (i, 0))
    edges = jax.ShapeDtypeStruct((snaps * HALO, cols), f32)
    strip, first, second = pl.pallas_call(
        functools.partial(strip_kernel, span),
        grid=(snaps // 8,),
        in_specs=[pl.BlockSpec((8, rows, cols), lambda i: (i, 0, 0))],
        out_specs=[
            pl.BlockSpec((span, 8, cols), lambda i: (0, i, 0)),
            edge_rows,
            edge_rows,
        ],
        out_shape=[jax.ShapeDtypeStruct((span, snaps, cols), f32), edges, edges],
        scratch_shapes=[pltpu.VMEM((rows + 2 * HALO, 8, cols), f32)],
        compiler_params=pltpu.CompilerParams(vmem_limit_bytes=60 * 1024 * 1024),
        name="pack_edges",
    )(field)
    low, high = pair_permutes([first, second], "lat", False)

    half = jax.ShapeDtypeStruct((span // 2, snaps, cols), f32)
    strip, first, second = pl.pallas_call(
        functools.partial(message_kernel, span),
        in_specs=[whole()] * 3,
        out_specs=[whole()] * 3,
        out_shape=[jax.ShapeDtypeStruct(strip.shape, f32), half, half],
        compiler_params=limits,
        name="lon_messages",
    )(strip, low, high)
    first, second = pair_permutes([first, second], "lon", True)

    pad = jnp.zeros((HALO,), f32)
    rates = [
        lax.dynamic_slice_in_dim(jnp.concatenate([pad, rate, pad]), row_start, rows + 2 * HALO)
        for rate in (lon_rate, lat_rate)
    ]
    weight = jnp.concatenate([pad, area_weight(row_start, rows, total_rows), pad])
    rates = jnp.stack([rates[0], rates[1], weight])

    main, side, edge = zonal_matrices()
    total = span * GROUPS
    bf16 = jnp.bfloat16

    def tile_of(shape):
        return pl.BlockSpec((shape, TILE, cols), lambda i: (0, i, 0))

    once = pl.pallas_call(
        functools.partial(first_kernel, span),
        grid=(tiles,),
        in_specs=[
            whole(pltpu.SMEM),
            pl.BlockSpec((TILE, rows, cols), lambda i: (i, 0, 0)),
            pl.BlockSpec((TILE * HALO, cols), lambda i: (i, 0)),
            pl.BlockSpec((TILE * HALO, cols), lambda i: (i, 0)),
            whole(),
        ],
        out_specs=tile_of(total + 8),
        out_shape=jax.ShapeDtypeStruct((total + 8, snaps, cols), f32),
        scratch_shapes=[pltpu.VMEM((total + 8, TILE, cols), f32)],
        compiler_params=limits,
        cost_estimate=pl.CostEstimate(
            flops=100 * snaps * rows * cols, bytes_accessed=8 * snaps * rows * cols, transcendentals=0
        ),
        name="first_pass",
    )(rates, field, low, high, main)
    split, gram = pl.pallas_call(
        functools.partial(second_kernel, span),
        grid=(tiles,),
        in_specs=[
            whole(pltpu.SMEM),
            tile_of(total + 8),
            tile_of(span),
            tile_of(span // 2),
            tile_of(span // 2),
            whole(),
            whole(),
            whole(),
        ],
        out_specs=[whole(), whole()],
        out_shape=[
            jax.ShapeDtypeStruct((rows + HALO, 2 * snaps, cols), bf16),
            jax.ShapeDtypeStruct((snaps, snaps), f32),
        ],
        scratch_shapes=[
            pltpu.VMEM((total + 8, TILE, cols), f32),
            pltpu.VMEM((GROUPS, 4 * LANES, 2 * LANES), bf16),
            pltpu.VMEM((span + 8, TILE, cols), f32),
            pltpu.VMEM((span * TILE, 2 * LANES), bf16),
            pltpu.VMEM((span * TILE, 2 * LANES), bf16),
            pltpu.VMEM((span, TILE, cols), f32),
            pltpu.VMEM((2, span, 8, cols), f32),
        ],
        compiler_params=limits,
        name="second_pass_and_gram",
    )(rates, once, strip, first, second, main, side, edge)

    gram = sum_all(gram)
    block = 64
    basis, factor = pl.pallas_call(
        functools.partial(basis_kernel, math.sqrt(total_cells)),
        grid=(rows // block,),
        in_specs=[
            pl.BlockSpec((snaps, snaps), lambda i: (0, 0)),
            whole(),
        ],
        out_specs=[
            pl.BlockSpec((snaps, block, cols), lambda i: (0, i, 0)),
            pl.BlockSpec((snaps, snaps), lambda i: (0, 0)),
        ],
        out_shape=[
            jax.ShapeDtypeStruct((snaps, rows, cols), bf16),
            jax.ShapeDtypeStruct((snaps, snaps), f32),
        ],
        scratch_shapes=[
            pltpu.VMEM((2 * snaps, 2 * snaps), bf16),
        ],
        compiler_params=limits,
        name="factor_and_basis",
    )(gram, split)
    return (basis, factor)


def solution(mesh):
    return jax.shard_map(
        shards,
        mesh=mesh,
        in_specs=(P(None, "lat", "lon"), P(), P()),
        out_specs=(P(None, "lat", "lon"), P()),
        check_vma=False,
    )
```

```python
import functools
import math

import jax
import jax.numpy as jnp
import numpy as np
from jax import lax
from jax.experimental import pallas as pl
from jax.experimental.pallas import tpu as pltpu
from jax.sharding import PartitionSpec as P

stencil_weights = (-205.0 / 72.0, 8.0 / 5.0, -1.0 / 5.0, 8.0 / 315.0, -1.0 / 560.0)

HALO = 8
STRIP = 2 * HALO
LANES = 128
GROUPS = LANES // STRIP
TILE = 16
VMEM_BYTES = 24 * 1024 * 1024


def area_weight(first_row, row_count, total_rows):
    row_index = (jnp.arange(row_count) + first_row).astype(jnp.float32)
    latitude = (-90.0 + (row_index + 0.5) * (180.0 / total_rows)) * (math.pi / 180.0)
    return jnp.sqrt(jnp.cos(latitude))


def hi_lo(values):
    hi = values.astype(jnp.bfloat16)
    lo = (values - hi.astype(jnp.float32)).astype(jnp.bfloat16)
    return hi, lo


def band(in_cols, out_cols):
    offset = np.abs(np.asarray(in_cols)[:, None] - np.asarray(out_cols)[None, :])
    table = np.asarray(stencil_weights, np.float32)
    return np.where(offset <= 4, table[np.minimum(offset, 4)], np.float32(0.0)).astype(np.float32)


def two_terms(matrix):
    hi = matrix.astype(jnp.bfloat16)
    lo = (matrix - hi.astype(np.float32)).astype(jnp.bfloat16)
    return np.concatenate([hi, lo], axis=1)


def block_diagonal(matrix):
    return np.kron(np.eye(GROUPS, dtype=np.float32), matrix)


def zonal_matrices():
    own = np.arange(LANES)
    outer = np.concatenate([np.arange(-HALO, 0), LANES + np.arange(HALO)])
    inner = np.concatenate([np.arange(LANES - HALO, LANES), np.arange(HALO)])
    main = two_terms(band(own, own))
    near = band(outer, outer)
    far = band(inner, outer)
    inward = band(outer, inner)
    near[:HALO, HALO:] = near[HALO:, :HALO] = 0.0
    near, far, inward = [two_terms(block_diagonal(part)) for part in (near, far, inward)]
    edge = np.concatenate([near, near, far, far], axis=0)
    inward = np.concatenate([inward, inward], axis=0)
    inward_only = np.concatenate([inward, np.zeros_like(inward)], axis=0)
    return np.concatenate([main, main], axis=0), np.concatenate([edge, inward_only], axis=1), inward


def strip_kernel(span, field_ref, ext_ref, strip_ref, first_ref, second_ref):
    snaps, rows, _ = field_ref.shape
    lat_even = lax.axis_index("lat") % 2 == 0
    north = field_ref[:, :HALO].reshape(snaps * HALO, LANES)
    south = field_ref[:, rows - HALO :].reshape(snaps * HALO, LANES)
    first_ref[...] = jnp.where(lat_even, south, north)
    second_ref[...] = jnp.where(lat_even, north, south)

    def turn(at, carry):
        begin = pl.multiple_of(at * 8, 8)
        for tile in range(0, snaps, 8):
            ext_ref[pl.ds(4 + HALO + begin, 8), tile : tile + 8] = jnp.swapaxes(
                field_ref[tile : tile + 8, pl.ds(begin, 8), :], 0, 1
            )
        return carry

    lax.fori_loop(0, rows // 8, turn, 0, unroll=2)
    ends = jnp.zeros((4 + HALO, snaps, LANES), jnp.float32)
    ext_ref[: 4 + HALO] = ends
    ext_ref[4 + HALO + rows :] = ends
    group_of = lax.broadcasted_iota(jnp.int32, (snaps, LANES), 1) // STRIP

    def pack(at, carry):
        packed = jnp.zeros((snaps, LANES), jnp.float32)
        for group in range(GROUPS):
            values = ext_ref[4 + group * span + at]
            moved = pltpu.roll(values, (HALO + STRIP * group) % LANES, 1)
            packed = jnp.where(group_of == group, moved, packed)
        strip_ref[at] = packed
        return carry

    lax.fori_loop(0, span, pack, 0, unroll=2)


def message_kernel(
    span, ext_in_ref, strip_ref, low_ref, high_ref, ext_ref, full_ref, first_ref, second_ref
):
    snaps = strip_ref.shape[1]
    half = span // 2
    end = ext_ref.shape[0] - 4 - HALO
    lane = lax.broadcasted_iota(jnp.int32, (snaps, LANES), 1)
    lat_even = lax.axis_index("lat") % 2 == 0
    lon_even = lax.axis_index("lon") % 2 == 0
    full_ref[...] = strip_ref[...]
    for tile in range(0, snaps, 8):
        part = slice(tile * HALO, (tile + 8) * HALO)
        first = jnp.swapaxes(low_ref[part].reshape(8, HALO, LANES), 0, 1)
        second = jnp.swapaxes(high_ref[part].reshape(8, HALO, LANES), 0, 1)
        ext_ref[4 : 4 + HALO, tile : tile + 8] = jnp.where(lat_even, second, first)
        ext_ref[end : end + HALO, tile : tile + 8] = jnp.where(lat_even, first, second)
    for at in range(HALO):
        north, south = ext_ref[4 + at], ext_ref[end + at]
        full_ref[at] = jnp.where(lane < STRIP, pltpu.roll(north, HALO, 1), full_ref[at])
        last = span - HALO + at
        full_ref[last] = jnp.where(
            lane >= LANES - STRIP, pltpu.roll(south, LANES - HALO, 1), full_ref[last]
        )
    left = lane % STRIP < HALO
    for at in range(half):
        upper, lower = full_ref[at], full_ref[at + half]
        eastward = jnp.where(left, upper, pltpu.roll(lower, HALO, 1))
        westward = jnp.where(left, pltpu.roll(lower, LANES - HALO, 1), upper)
        first_ref[at] = jnp.where(lon_even, eastward, westward)
        second_ref[at] = jnp.where(lon_even, westward, eastward)


def stencil_row(center, pairs, zonal, zonal_rate, merid_rate):
    merid = stencil_weights[1] * pairs[0]
    for offset in range(2, 5):
        merid = merid + stencil_weights[offset] * pairs[offset - 1]
    scale = 1.0 + stencil_weights[0] * merid_rate
    return scale * center + merid_rate * merid + zonal_rate * zonal


def zonal_terms(parts, weights):
    product = jnp.dot(
        jnp.concatenate(parts, axis=1), weights, preferred_element_type=jnp.float32
    )
    return product[:, :LANES] + product[:, LANES:]


def stencil_rows(load, begin, span, part, rates_ref, store):
    loaded = {}

    def row(at):
        if at not in loaded:
            loaded[at] = load(begin + at)
        return loaded[at]

    for at in range(span):
        here = at + 4
        pairs = [row(here + offset) + row(here - offset) for offset in range(1, 5)]
        store(
            at,
            stencil_row(
                row(here), pairs, part[at], rates_ref[0, begin + at], rates_ref[1, begin + at]
            ),
        )


def first_kernel(span, rates_ref, ext_ref, main_ref, once_ref):
    snaps = ext_ref.shape[1]
    total = span * GROUPS
    ends = jnp.zeros((4, snaps, LANES), jnp.float32)
    once_ref[:4] = ends
    once_ref[total + 4 :] = ends
    for tile in range(0, snaps, TILE):
        snap = slice(tile, tile + TILE)

        def body(group, carry):
            begin = group * span
            center = ext_ref[pl.ds(4 + begin, span), snap].reshape(span * TILE, LANES)
            part = zonal_terms(hi_lo(center), main_ref[...]).reshape(span, TILE, LANES)

            def load(at):
                return ext_ref[at, snap]

            def store(at, value):
                once_ref[4 + begin + at, snap] = value

            stencil_rows(load, begin, span, part, rates_ref, store)
            return carry

        lax.fori_loop(0, GROUPS, body, 0)


def second_kernel(
    span,
    rates_ref,
    once_ref,
    strip_ref,
    first_ref,
    second_ref,
    main_ref,
    edge_ref,
    inward_ref,
    split_ref,
    gram_ref,
    full_ref,
    outer_ref,
    zonal_ref,
    add_ref,
    strip_rates_ref,
):
    both = split_ref.shape[1]
    rows = split_ref.shape[0] - HALO
    snaps = both // 2
    half = span // 2
    total = span * GROUPS
    lon_even = lax.axis_index("lon") % 2 == 0
    lane = lax.broadcasted_iota(jnp.int32, (TILE, LANES), 1)
    left = lane % STRIP < HALO
    rim = (lane < HALO) | (lane >= LANES - HALO)
    group_of = lax.broadcasted_iota(jnp.int32, (8, LANES), 1) // STRIP
    for at in range(span):
        for kind in range(3):
            value = jnp.zeros((8, LANES), jnp.float32)
            for group in range(GROUPS):
                value = jnp.where(group_of == group, rates_ref[kind, group * span + at], value)
            strip_rates_ref[kind, at] = value

    def strip_rate(kind, at):
        return jnp.concatenate([strip_rates_ref[kind, at]] * (TILE // 8), axis=0)

    for tile in range(0, snaps, TILE):
        snap = slice(tile, tile + TILE)
        for at in range(half):
            first, second = first_ref[at, snap], second_ref[at, snap]
            west = jnp.where(lon_even, second, first)
            east = jnp.where(lon_even, first, second)
            outer_ref[4 + at] = jnp.where(left, west, east)
            outer_ref[4 + half + at] = jnp.where(
                left, pltpu.roll(west, LANES - HALO, 1), pltpu.roll(east, HALO, 1)
            )
        for at in range(4):
            outer_ref[at] = pltpu.roll(outer_ref[span + at], STRIP, 1)
            outer_ref[span + 4 + at] = pltpu.roll(outer_ref[4 + at], LANES - STRIP, 1)
        hi, lo = hi_lo(outer_ref[4 : 4 + span].reshape(span * TILE, LANES))
        own_hi, own_lo = hi_lo(strip_ref[:, snap].reshape(span * TILE, LANES))
        product = jnp.dot(
            jnp.concatenate([hi, lo, own_hi, own_lo], axis=1),
            edge_ref[...],
            preferred_element_type=jnp.float32,
        ).reshape(span, TILE, 4 * LANES)
        for at in range(span):
            zonal = product[at, :, :LANES] + product[at, :, LANES : 2 * LANES]
            pairs = [
                outer_ref[4 + at + offset] + outer_ref[4 + at - offset] for offset in range(1, 5)
            ]
            zonal_rate = strip_rate(0, at)
            zonal_ref[at] = stencil_row(
                outer_ref[4 + at], pairs, zonal, zonal_rate, strip_rate(1, at)
            )
            add_ref[0, at] = zonal_rate * (
                product[at, :, 2 * LANES : 3 * LANES] + product[at, :, 3 * LANES :]
            )
        inner = zonal_ref[...].reshape(span * TILE, LANES)
        product = zonal_terms(hi_lo(inner), inward_ref[...]).reshape(span, TILE, LANES)
        for at in range(span):
            add_ref[1, at] = (strip_rate(2, at) * strip_rate(0, at)) * product[at]

        def added(kind, at, group):
            moved = pltpu.roll(add_ref[kind, at], LANES - HALO - STRIP * group, 1)
            return jnp.where(rim, moved, 0.0)

        def complete(group, carry):
            begin = group * span
            for at in range(span):
                here = 4 + begin + at
                full_ref[here] = once_ref[here, snap] + added(0, at, group)
            return carry

        lax.fori_loop(0, GROUPS, complete, 0)
        for at in range(4):
            full_ref[at] = once_ref[at, snap]
            full_ref[total + 4 + at] = once_ref[total + 4 + at, snap]

        def second_pass(group, carry):
            begin = group * span
            center = full_ref[pl.ds(4 + begin, span)].reshape(span * TILE, LANES)
            part = zonal_terms(hi_lo(center), main_ref[...]).reshape(span, TILE, LANES)

            def load(at):
                return full_ref[at]

            def store(at, value):
                hi, lo = hi_lo(rates_ref[2, begin + at] * value + added(1, at, group))
                row = jnp.maximum(begin + at - HALO, 0)
                split_ref[row, snap] = hi
                split_ref[row, snaps + tile : snaps + tile + TILE] = lo

            stencil_rows(load, begin, span, part, rates_ref, store)
            return carry

        lax.fori_loop(0, GROUPS, second_pass, 0)

    def square(at, total):
        two = jnp.concatenate([split_ref[2 * at], split_ref[2 * at + 1]], axis=1)
        return total + lax.dot_general(
            two, two, (((1,), (1,)), ((), ())), preferred_element_type=jnp.float32
        )

    grams = lax.fori_loop(0, rows // 2, square, jnp.zeros((both, both), jnp.float32), unroll=8)
    gram = (
        grams[:snaps, :snaps]
        + grams[snaps:, snaps:]
        + (grams[:snaps, snaps:] + grams[snaps:, :snaps])
    )
    gram_ref[...] = jnp.concatenate(
        [gram[at : at + 8] for at in range(0, snaps, 8)], axis=1
    )


def basis_kernel(root_count, gram_ref, split_ref, basis_ref, factor_ref, left_ref):
    snaps = basis_ref.shape[0]

    @pl.when(pl.program_id(0) == 0)
    def _():
        row = lax.broadcasted_iota(jnp.int32, (snaps, 2 * snaps), 0)
        col = lax.broadcasted_iota(jnp.int32, (snaps, 2 * snaps), 1)
        packed = jnp.sum(gram_ref[...], axis=0)
        gram = jnp.concatenate(
            [packed[:, at : at + snaps] for at in range(0, packed.shape[1], snaps)], axis=0
        )
        work = jnp.concatenate([gram, jnp.zeros((snaps, snaps), jnp.float32)], axis=1)
        work = jnp.where(col == row + snaps, 1.0, work)
        for step in range(snaps):
            pivot_row = work[step : step + 1, :]
            ratio = work[:, step : step + 1] / work[step : step + 1, step : step + 1]
            work = work - jnp.where(row > step, ratio, 0.0) * pivot_row
        diagonal = jnp.sum(jnp.where(row == col, work, 0.0), axis=1, keepdims=True)
        work = work * lax.rsqrt(diagonal)
        upper = jnp.where(col >= row, work, 0.0)
        factor_ref[...] = upper[:, :snaps] / root_count
        hi, lo = hi_lo(work[:, snaps:] * root_count)
        left_ref[:snaps] = jnp.concatenate([hi, hi], axis=1)
        left_ref[snaps:] = jnp.concatenate([lo, jnp.zeros_like(lo)], axis=1)

    left = left_ref[...]
    start = pl.program_id(0) * basis_ref.shape[1]

    def body(at, carry):
        begin = pl.multiple_of(at * 16, 16)
        values = []
        for pair in range(8):
            row = start + begin + 2 * pair
            two = jnp.concatenate([split_ref[row], split_ref[row + 1]], axis=1)
            product = jnp.dot(left, two, preferred_element_type=jnp.float32)
            value = product[:snaps] + product[snaps:]
            values += [value[:, :LANES], value[:, LANES:]]
        turned = jnp.swapaxes(jnp.stack(values, axis=0), 0, 1)
        basis_ref[:, pl.ds(begin, 16), :] = turned.astype(jnp.bfloat16)
        return carry

    lax.fori_loop(0, basis_ref.shape[1] // 16, body, 0)


def pair_permutes(values, axis, periodic):
    count = lax.axis_size(axis)
    inner = [(i, i ^ 1) for i in range(count)]
    outer = []
    for i in range(1, count, 2):
        if periodic or i + 1 < count:
            outer += [(i, (i + 1) % count), ((i + 1) % count, i)]
    return lax.ppermute(values[0], axis, inner), lax.ppermute(values[1], axis, outer)


def gather_all(values):
    axes = ("lat", "lon")
    count = lax.axis_size(axes)
    return lax.all_to_all(jnp.broadcast_to(values, (count,) + values.shape), axes, 0, 0)


def whole(memory_space=pltpu.VMEM):
    return pl.BlockSpec(memory_space=memory_space)


def shards(field, lon_rate, lat_rate):
    snaps, rows, cols = field.shape
    row_start = lax.axis_index("lat") * rows
    total_rows = rows * lax.axis_size("lat")
    total_cells = total_rows * cols * lax.axis_size("lon")
    span = (rows + 2 * HALO) // GROUPS
    f32 = jnp.float32
    limits = pltpu.CompilerParams(vmem_limit_bytes=VMEM_BYTES)

    total = span * GROUPS
    ext = jax.ShapeDtypeStruct((total + 8, snaps, cols), f32)
    strip = jax.ShapeDtypeStruct((span, snaps, cols), f32)
    half = jax.ShapeDtypeStruct((span // 2, snaps, cols), f32)
    edge_rows = jax.ShapeDtypeStruct((snaps * HALO, cols), f32)
    turned, packed, first, second = pl.pallas_call(
        functools.partial(strip_kernel, span),
        in_specs=[whole()],
        out_specs=[whole()] * 4,
        out_shape=[ext, strip, edge_rows, edge_rows],
        compiler_params=limits,
        name="turn_and_pack",
    )(field)
    low, high = pair_permutes([first, second], "lat", False)
    turned, packed, first, second = pl.pallas_call(
        functools.partial(message_kernel, span),
        in_specs=[whole()] * 4,
        out_specs=[whole()] * 4,
        out_shape=[ext, strip, half, half],
        input_output_aliases={0: 0},
        compiler_params=limits,
        name="lon_messages",
    )(turned, packed, low, high)
    first, second = pair_permutes([first, second], "lon", True)

    pad = jnp.zeros((HALO,), f32)
    rates = [
        lax.dynamic_slice_in_dim(jnp.concatenate([pad, rate, pad]), row_start, rows + 2 * HALO)
        for rate in (lon_rate, lat_rate)
    ]
    weight = jnp.concatenate([pad, area_weight(row_start, rows, total_rows), pad])
    rates = jnp.stack([rates[0], rates[1], weight])

    main, edge, inward = zonal_matrices()
    bf16 = jnp.bfloat16
    once = pl.pallas_call(
        functools.partial(first_kernel, span),
        in_specs=[whole(pltpu.SMEM), whole(), whole()],
        out_specs=whole(),
        out_shape=ext,
        compiler_params=limits,
        cost_estimate=pl.CostEstimate(
            flops=100 * snaps * rows * cols, bytes_accessed=8 * snaps * rows * cols, transcendentals=0
        ),
        name="first_pass",
    )(rates, turned, main)
    split, gram = pl.pallas_call(
        functools.partial(second_kernel, span),
        in_specs=[whole(pltpu.SMEM)] + [whole()] * 7,
        out_specs=[whole(), whole()],
        out_shape=[
            jax.ShapeDtypeStruct((rows + HALO, 2 * snaps, cols), bf16),
            jax.ShapeDtypeStruct((8, snaps // 8 * snaps), f32),
        ],
        scratch_shapes=[
            pltpu.VMEM((total + 8, TILE, cols), f32),
            pltpu.VMEM((span + 8, TILE, cols), f32),
            pltpu.VMEM((span, TILE, cols), f32),
            pltpu.VMEM((2, span, TILE, cols), f32),
            pltpu.VMEM((3, span, 8, cols), f32),
        ],
        compiler_params=limits,
        name="second_pass_and_gram",
    )(rates, once, packed, first, second, main, edge, inward)

    grams = gather_all(gram)
    block = 64
    basis, factor = pl.pallas_call(
        functools.partial(basis_kernel, math.sqrt(total_cells)),
        grid=(rows // block,),
        in_specs=[
            whole(),
            whole(),
        ],
        out_specs=[
            pl.BlockSpec((snaps, block, cols), lambda i: (0, i, 0)),
            pl.BlockSpec((snaps, snaps), lambda i: (0, 0)),
        ],
        out_shape=[
            jax.ShapeDtypeStruct((snaps, rows, cols), bf16),
            jax.ShapeDtypeStruct((snaps, snaps), f32),
        ],
        scratch_shapes=[
            pltpu.VMEM((2 * snaps, 2 * snaps), bf16),
        ],
        compiler_params=limits,
        name="factor_and_basis",
    )(grams, split)
    return (basis, factor)


def solution(mesh):
    return jax.shard_map(
        shards,
        mesh=mesh,
        in_specs=(P(None, "lat", "lon"), P(), P()),
        out_specs=(P(None, "lat", "lon"), P()),
        check_vma=False,
    )
```

```python
import functools
import math

import jax
import jax.numpy as jnp
import numpy as np
from jax import lax
from jax.experimental import pallas as pl
from jax.experimental.pallas import tpu as pltpu
from jax.sharding import PartitionSpec as P

stencil_weights = (-205.0 / 72.0, 8.0 / 5.0, -1.0 / 5.0, 8.0 / 315.0, -1.0 / 560.0)

HALO = 8
STRIP = 2 * HALO
LANES = 128
GROUPS = LANES // STRIP
TILE = 16
VMEM_BYTES = 24 * 1024 * 1024


def area_weight(first_row, row_count, total_rows):
    row_index = (jnp.arange(row_count) + first_row).astype(jnp.float32)
    latitude = (-90.0 + (row_index + 0.5) * (180.0 / total_rows)) * (math.pi / 180.0)
    return jnp.sqrt(jnp.cos(latitude))


def hi_lo(values):
    hi = values.astype(jnp.bfloat16)
    lo = (values - hi.astype(jnp.float32)).astype(jnp.bfloat16)
    return hi, lo


def band(in_cols, out_cols):
    offset = np.abs(np.asarray(in_cols)[:, None] - np.asarray(out_cols)[None, :])
    table = np.asarray(stencil_weights, np.float32)
    return np.where(offset <= 4, table[np.minimum(offset, 4)], np.float32(0.0)).astype(np.float32)


def two_terms(matrix):
    hi = matrix.astype(jnp.bfloat16)
    lo = (matrix - hi.astype(np.float32)).astype(jnp.bfloat16)
    return np.concatenate([hi, lo], axis=1)


def block_diagonal(matrix):
    return np.kron(np.eye(GROUPS, dtype=np.float32), matrix)


def zonal_matrices():
    own = np.arange(LANES)
    outer = np.concatenate([np.arange(-HALO, 0), LANES + np.arange(HALO)])
    inner = np.concatenate([np.arange(LANES - HALO, LANES), np.arange(HALO)])
    main = two_terms(band(own, own))
    near = band(outer, outer)
    far = band(inner, outer)
    inward = band(outer, inner)
    near[:HALO, HALO:] = near[HALO:, :HALO] = 0.0
    near, far, inward = [two_terms(block_diagonal(part)) for part in (near, far, inward)]
    edge = np.concatenate([near, near, far, far], axis=0)
    inward = np.concatenate([inward, inward], axis=0)
    inward_only = np.concatenate([inward, np.zeros_like(inward)], axis=0)
    return np.concatenate([main, main], axis=0), np.concatenate([edge, inward_only], axis=1), inward


def edge_kernel(field_ref, first_ref, second_ref, sems):
    rows = field_ref.shape[1]
    begin = (1 - lax.axis_index("lat") % 2) * (rows - HALO)
    copies = []
    for at, (start, target) in enumerate(
        [(begin, first_ref), (rows - HALO - begin, second_ref)]
    ):
        start = pl.multiple_of(start, HALO)
        copies.append(
            pltpu.make_async_copy(field_ref.at[:, pl.ds(start, HALO), :], target, sems.at[at])
        )
    for copy in copies:
        copy.start()
    for copy in copies:
        copy.wait()


def strip_kernel(span, field_ref, ext_ref, strip_ref):
    snaps, rows, _ = field_ref.shape

    def turn(at, carry):
        begin = pl.multiple_of(at * 8, 8)
        for tile in range(0, snaps, 8):
            ext_ref[pl.ds(4 + HALO + begin, 8), tile : tile + 8] = jnp.swapaxes(
                field_ref[tile : tile + 8, pl.ds(begin, 8), :], 0, 1
            )
        return carry

    lax.fori_loop(0, rows // 8, turn, 0, unroll=2)
    ends = jnp.zeros((4 + HALO, snaps, LANES), jnp.float32)
    ext_ref[: 4 + HALO] = ends
    ext_ref[4 + HALO + rows :] = ends
    group_of = lax.broadcasted_iota(jnp.int32, (snaps, LANES), 1) // STRIP

    def pack(at, carry):
        packed = jnp.zeros((snaps, LANES), jnp.float32)
        for group in range(GROUPS):
            values = ext_ref[4 + group * span + at]
            moved = pltpu.roll(values, (HALO + STRIP * group) % LANES, 1)
            packed = jnp.where(group_of == group, moved, packed)
        strip_ref[at] = packed
        return carry

    lax.fori_loop(0, span, pack, 0, unroll=2)


def message_kernel(
    span, ext_in_ref, strip_ref, low_ref, high_ref, ext_ref, full_ref, first_ref, second_ref
):
    snaps = strip_ref.shape[1]
    half = span // 2
    end = ext_ref.shape[0] - 4 - HALO
    lane = lax.broadcasted_iota(jnp.int32, (snaps, LANES), 1)
    lat_even = lax.axis_index("lat") % 2 == 0
    lon_even = lax.axis_index("lon") % 2 == 0
    full_ref[...] = strip_ref[...]
    for tile in range(0, snaps, 8):
        first = jnp.swapaxes(low_ref[tile : tile + 8], 0, 1)
        second = jnp.swapaxes(high_ref[tile : tile + 8], 0, 1)
        ext_ref[4 : 4 + HALO, tile : tile + 8] = jnp.where(lat_even, second, first)
        ext_ref[end : end + HALO, tile : tile + 8] = jnp.where(lat_even, first, second)
    for at in range(HALO):
        north, south = ext_ref[4 + at], ext_ref[end + at]
        full_ref[at] = jnp.where(lane < STRIP, pltpu.roll(north, HALO, 1), full_ref[at])
        last = span - HALO + at
        full_ref[last] = jnp.where(
            lane >= LANES - STRIP, pltpu.roll(south, LANES - HALO, 1), full_ref[last]
        )
    left = lane % STRIP < HALO
    for at in range(half):
        upper, lower = full_ref[at], full_ref[at + half]
        eastward = jnp.where(left, upper, pltpu.roll(lower, HALO, 1))
        westward = jnp.where(left, pltpu.roll(lower, LANES - HALO, 1), upper)
        first_ref[at] = jnp.where(lon_even, eastward, westward)
        second_ref[at] = jnp.where(lon_even, westward, eastward)


def stencil_row(center, pairs, zonal, zonal_rate, merid_rate):
    merid = stencil_weights[1] * pairs[0]
    for offset in range(2, 5):
        merid = merid + stencil_weights[offset] * pairs[offset - 1]
    scale = 1.0 + stencil_weights[0] * merid_rate
    return scale * center + merid_rate * merid + zonal_rate * zonal


def zonal_terms(parts, weights):
    product = jnp.dot(
        jnp.concatenate(parts, axis=1), weights, preferred_element_type=jnp.float32
    )
    return product[:, :LANES] + product[:, LANES:]


def rate_reader(rows, rates_refs):
    last = rows * lax.axis_size("lat") - 1
    origin = lax.axis_index("lat") * rows - HALO

    def read(at):
        row = jnp.clip(origin + at, 0, last)
        return [ref[row] for ref in rates_refs]

    return read


def stencil_rows(load, begin, span, part, rates, store):
    loaded = {}

    def row(at):
        if at not in loaded:
            loaded[at] = load(begin + at)
        return loaded[at]

    for at in range(span):
        here = at + 4
        pairs = [row(here + offset) + row(here - offset) for offset in range(1, 5)]
        values = rates(begin + at)
        store(at, stencil_row(row(here), pairs, part[at], values[0], values[1]), values)


def first_kernel(span, lon_ref, lat_ref, ext_ref, main_ref, once_ref):
    snaps = ext_ref.shape[1]
    total = span * GROUPS
    rows = total - 2 * HALO
    rates = rate_reader(rows, (lon_ref, lat_ref))
    for tile in range(0, snaps, TILE):
        snap = slice(tile, tile + TILE)

        def body(group, carry):
            begin = group * span
            center = ext_ref[pl.ds(4 + begin, span), snap].reshape(span * TILE, LANES)
            part = zonal_terms(hi_lo(center), main_ref[...]).reshape(span, TILE, LANES)

            def load(at):
                return ext_ref[at, snap]

            def store(at, value, _):
                once_ref[4 + begin + at, snap] = value

            stencil_rows(load, begin, span, part, rates, store)
            return carry

        lax.fori_loop(0, GROUPS, body, 0)
    ends = jnp.zeros((4, snaps, LANES), jnp.float32)
    once_ref[:4] = ends
    once_ref[total + 4 :] = ends


def second_kernel(
    span,
    lon_ref,
    lat_ref,
    weight_ref,
    once_ref,
    strip_ref,
    first_ref,
    second_ref,
    main_ref,
    edge_ref,
    inward_ref,
    split_ref,
    gram_ref,
    full_ref,
    outer_ref,
    zonal_ref,
    add_ref,
    strip_rates_ref,
):
    both = split_ref.shape[1]
    rows = split_ref.shape[0] - HALO
    snaps = both // 2
    half = span // 2
    total = span * GROUPS
    lon_even = lax.axis_index("lon") % 2 == 0
    lane = lax.broadcasted_iota(jnp.int32, (TILE, LANES), 1)
    left = lane % STRIP < HALO
    rim = (lane < HALO) | (lane >= LANES - HALO)
    group_of = lax.broadcasted_iota(jnp.int32, (8, LANES), 1) // STRIP
    rates = rate_reader(rows, (lon_ref, lat_ref, weight_ref))
    for at in range(span):
        packed = [jnp.zeros((8, LANES), jnp.float32)] * 3
        for group in range(GROUPS):
            here = group_of == group
            packed = [
                jnp.where(here, value, old)
                for value, old in zip(rates(group * span + at), packed)
            ]
        for kind in range(3):
            strip_rates_ref[kind, at] = packed[kind]

    def strip_rate(kind, at):
        return jnp.concatenate([strip_rates_ref[kind, at]] * (TILE // 8), axis=0)

    for tile in range(0, snaps, TILE):
        snap = slice(tile, tile + TILE)
        for at in range(half):
            first, second = first_ref[at, snap], second_ref[at, snap]
            west = jnp.where(lon_even, second, first)
            east = jnp.where(lon_even, first, second)
            outer_ref[4 + at] = jnp.where(left, west, east)
            outer_ref[4 + half + at] = jnp.where(
                left, pltpu.roll(west, LANES - HALO, 1), pltpu.roll(east, HALO, 1)
            )
        for at in range(4):
            outer_ref[at] = pltpu.roll(outer_ref[span + at], STRIP, 1)
            outer_ref[span + 4 + at] = pltpu.roll(outer_ref[4 + at], LANES - STRIP, 1)
        hi, lo = hi_lo(outer_ref[4 : 4 + span].reshape(span * TILE, LANES))
        own_hi, own_lo = hi_lo(strip_ref[:, snap].reshape(span * TILE, LANES))
        product = jnp.dot(
            jnp.concatenate([hi, lo, own_hi, own_lo], axis=1),
            edge_ref[...],
            preferred_element_type=jnp.float32,
        ).reshape(span, TILE, 4 * LANES)
        for at in range(span):
            zonal = product[at, :, :LANES] + product[at, :, LANES : 2 * LANES]
            pairs = [
                outer_ref[4 + at + offset] + outer_ref[4 + at - offset] for offset in range(1, 5)
            ]
            zonal_rate = strip_rate(0, at)
            zonal_ref[at] = stencil_row(
                outer_ref[4 + at], pairs, zonal, zonal_rate, strip_rate(1, at)
            )
            add_ref[0, at] = zonal_rate * (
                product[at, :, 2 * LANES : 3 * LANES] + product[at, :, 3 * LANES :]
            )
        inner = zonal_ref[...].reshape(span * TILE, LANES)
        product = zonal_terms(hi_lo(inner), inward_ref[...]).reshape(span, TILE, LANES)
        for at in range(span):
            add_ref[1, at] = (strip_rate(2, at) * strip_rate(0, at)) * product[at]

        def added(kind, at, group):
            moved = pltpu.roll(add_ref[kind, at], LANES - HALO - STRIP * group, 1)
            return jnp.where(rim, moved, 0.0)

        def complete(group, carry):
            begin = group * span
            for at in range(span):
                here = 4 + begin + at
                full_ref[here] = once_ref[here, snap] + added(0, at, group)
            return carry

        lax.fori_loop(0, GROUPS, complete, 0)
        outside = jnp.zeros((HALO, TILE, LANES), jnp.float32)

        @pl.when(lax.axis_index("lat") == 0)
        def _():
            full_ref[4 : 4 + HALO] = outside

        @pl.when(lax.axis_index("lat") == lax.axis_size("lat") - 1)
        def _():
            full_ref[4 + HALO + rows : 4 + total] = outside

        for at in range(4):
            full_ref[at] = once_ref[at, snap]
            full_ref[total + 4 + at] = once_ref[total + 4 + at, snap]

        def second_pass(group, carry):
            begin = group * span
            center = full_ref[pl.ds(4 + begin, span)].reshape(span * TILE, LANES)
            part = zonal_terms(hi_lo(center), main_ref[...]).reshape(span, TILE, LANES)

            def load(at):
                return full_ref[at]

            def store(at, value, values):
                hi, lo = hi_lo(values[2] * value + added(1, at, group))
                row = jnp.maximum(begin + at - HALO, 0)
                split_ref[row, snap] = hi
                split_ref[row, snaps + tile : snaps + tile + TILE] = lo

            stencil_rows(load, begin, span, part, rates, store)
            return carry

        lax.fori_loop(0, GROUPS, second_pass, 0)

    def square(at, total):
        two = jnp.concatenate([split_ref[2 * at], split_ref[2 * at + 1]], axis=1)
        return total + lax.dot_general(
            two, two, (((1,), (1,)), ((), ())), preferred_element_type=jnp.float32
        )

    grams = lax.fori_loop(0, rows // 2, square, jnp.zeros((both, both), jnp.float32), unroll=8)
    gram = (
        grams[:snaps, :snaps]
        + grams[snaps:, snaps:]
        + (grams[:snaps, snaps:] + grams[snaps:, :snaps])
    )
    gram_ref[...] = jnp.concatenate(
        [gram[at : at + 8] for at in range(0, snaps, 8)], axis=1
    )


def basis_kernel(root_count, gram_ref, split_ref, basis_ref, factor_ref, left_ref):
    snaps = basis_ref.shape[0]

    @pl.when(pl.program_id(0) == 0)
    def _():
        row = lax.broadcasted_iota(jnp.int32, (snaps, 2 * snaps), 0)
        col = lax.broadcasted_iota(jnp.int32, (snaps, 2 * snaps), 1)
        packed = jnp.sum(gram_ref[...], axis=0)
        gram = jnp.concatenate(
            [packed[:, at : at + snaps] for at in range(0, packed.shape[1], snaps)], axis=0
        )
        work = jnp.concatenate([gram, jnp.zeros((snaps, snaps), jnp.float32)], axis=1)
        work = jnp.where(col == row + snaps, 1.0, work)
        for step in range(snaps):
            pivot_row = work[step : step + 1, :]
            ratio = work[:, step : step + 1] / work[step : step + 1, step : step + 1]
            work = work - jnp.where(row > step, ratio, 0.0) * pivot_row
        diagonal = jnp.sum(jnp.where(row == col, work, 0.0), axis=1, keepdims=True)
        work = work * lax.rsqrt(diagonal)
        upper = jnp.where(col >= row, work, 0.0)
        factor_ref[...] = upper[:, :snaps] / root_count
        hi, lo = hi_lo(work[:, snaps:] * root_count)
        left_ref[:snaps] = jnp.concatenate([hi, hi], axis=1)
        left_ref[snaps:] = jnp.concatenate([lo, jnp.zeros_like(lo)], axis=1)

    left = left_ref[...]
    start = pl.program_id(0) * basis_ref.shape[1]

    def body(at, carry):
        begin = pl.multiple_of(at * 16, 16)
        values = []
        for pair in range(8):
            row = start + begin + 2 * pair
            two = jnp.concatenate([split_ref[row], split_ref[row + 1]], axis=1)
            product = jnp.dot(left, two, preferred_element_type=jnp.float32)
            value = product[:snaps] + product[snaps:]
            values += [value[:, :LANES], value[:, LANES:]]
        turned = jnp.swapaxes(jnp.stack(values, axis=0), 0, 1)
        basis_ref[:, pl.ds(begin, 16), :] = turned.astype(jnp.bfloat16)
        return carry

    lax.fori_loop(0, basis_ref.shape[1] // 16, body, 0)


def pair_permutes(values, axis, periodic):
    count = lax.axis_size(axis)
    inner = [(i, i ^ 1) for i in range(count)]
    outer = []
    for i in range(1, count, 2):
        if periodic or i + 1 < count:
            outer += [(i, (i + 1) % count), ((i + 1) % count, i)]
    return lax.ppermute(values[0], axis, inner), lax.ppermute(values[1], axis, outer)


def gather_all(values):
    axes = ("lat", "lon")
    count = lax.axis_size(axes)
    return lax.all_to_all(jnp.broadcast_to(values, (count,) + values.shape), axes, 0, 0)


def whole(memory_space=pltpu.VMEM):
    return pl.BlockSpec(memory_space=memory_space)


def shards(field, lon_rate, lat_rate):
    snaps, rows, cols = field.shape
    total_rows = rows * lax.axis_size("lat")
    total_cells = total_rows * cols * lax.axis_size("lon")
    span = (rows + 2 * HALO) // GROUPS
    f32 = jnp.float32
    limits = pltpu.CompilerParams(vmem_limit_bytes=VMEM_BYTES)

    total = span * GROUPS
    ext = jax.ShapeDtypeStruct((total + 8, snaps, cols), f32)
    strip = jax.ShapeDtypeStruct((span, snaps, cols), f32)
    half = jax.ShapeDtypeStruct((span // 2, snaps, cols), f32)
    edge_rows = jax.ShapeDtypeStruct((snaps, HALO, cols), f32)
    first, second = pl.pallas_call(
        edge_kernel,
        in_specs=[whole(pl.ANY)],
        out_specs=[whole()] * 2,
        out_shape=[edge_rows, edge_rows],
        scratch_shapes=[pltpu.SemaphoreType.DMA((2,))],
        compiler_params=pltpu.CompilerParams(vmem_limit_bytes=60 * 1024 * 1024),
        name="lat_messages",
    )(field)
    low, high = pair_permutes([first, second], "lat", False)
    turned, packed = pl.pallas_call(
        functools.partial(strip_kernel, span),
        in_specs=[whole()],
        out_specs=[whole()] * 2,
        out_shape=[ext, strip],
        compiler_params=limits,
        name="turn_and_pack",
    )(field)
    turned, packed, first, second = pl.pallas_call(
        functools.partial(message_kernel, span),
        in_specs=[whole()] * 4,
        out_specs=[whole()] * 4,
        out_shape=[ext, strip, half, half],
        input_output_aliases={0: 0},
        compiler_params=limits,
        name="lon_messages",
    )(turned, packed, low, high)
    first, second = pair_permutes([first, second], "lon", True)

    weight = area_weight(0, total_rows, total_rows)

    main, edge, inward = zonal_matrices()
    bf16 = jnp.bfloat16
    once = pl.pallas_call(
        functools.partial(first_kernel, span),
        in_specs=[whole(pltpu.SMEM)] * 2 + [whole()] * 2,
        out_specs=whole(),
        out_shape=ext,
        compiler_params=limits,
        cost_estimate=pl.CostEstimate(
            flops=100 * snaps * rows * cols, bytes_accessed=8 * snaps * rows * cols, transcendentals=0
        ),
        name="first_pass",
    )(lon_rate, lat_rate, turned, main)
    split, gram = pl.pallas_call(
        functools.partial(second_kernel, span),
        in_specs=[whole(pltpu.SMEM)] * 3 + [whole()] * 7,
        out_specs=[whole(), whole()],
        out_shape=[
            jax.ShapeDtypeStruct((rows + HALO, 2 * snaps, cols), bf16),
            jax.ShapeDtypeStruct((8, snaps // 8 * snaps), f32),
        ],
        scratch_shapes=[
            pltpu.VMEM((total + 8, TILE, cols), f32),
            pltpu.VMEM((span + 8, TILE, cols), f32),
            pltpu.VMEM((span, TILE, cols), f32),
            pltpu.VMEM((2, span, TILE, cols), f32),
            pltpu.VMEM((3, span, 8, cols), f32),
        ],
        compiler_params=limits,
        name="second_pass_and_gram",
    )(lon_rate, lat_rate, weight, once, packed, first, second, main, edge, inward)

    grams = gather_all(gram)
    block = 64
    basis, factor = pl.pallas_call(
        functools.partial(basis_kernel, math.sqrt(total_cells)),
        grid=(rows // block,),
        in_specs=[
            whole(),
            whole(),
        ],
        out_specs=[
            pl.BlockSpec((snaps, block, cols), lambda i: (0, i, 0)),
            pl.BlockSpec((snaps, snaps), lambda i: (0, 0)),
        ],
        out_shape=[
            jax.ShapeDtypeStruct((snaps, rows, cols), bf16),
            jax.ShapeDtypeStruct((snaps, snaps), f32),
        ],
        scratch_shapes=[
            pltpu.VMEM((2 * snaps, 2 * snaps), bf16),
        ],
        compiler_params=limits,
        name="factor_and_basis",
    )(grams, split)
    return (basis, factor)


def solution(mesh):
    return jax.shard_map(
        shards,
        mesh=mesh,
        in_specs=(P(None, "lat", "lon"), P(), P()),
        out_specs=(P(None, "lat", "lon"), P()),
        check_vma=False,
    )
```

```python
import functools
import math

import jax
import jax.numpy as jnp
import numpy as np
from jax import lax
from jax.experimental import pallas as pl
from jax.experimental.pallas import tpu as pltpu
from jax.sharding import PartitionSpec as P

stencil_weights = (-205.0 / 72.0, 8.0 / 5.0, -1.0 / 5.0, 8.0 / 315.0, -1.0 / 560.0)

HALO = 8
STRIP = 2 * HALO
LANES = 128
GROUPS = LANES // STRIP
TILE = 16
VMEM_BYTES = 24 * 1024 * 1024


def area_weight(first_row, row_count, total_rows):
    row_index = (jnp.arange(row_count) + first_row).astype(jnp.float32)
    latitude = (-90.0 + (row_index + 0.5) * (180.0 / total_rows)) * (math.pi / 180.0)
    return jnp.sqrt(jnp.cos(latitude))


def hi_lo(values):
    hi = values.astype(jnp.bfloat16)
    lo = (values - hi.astype(jnp.float32)).astype(jnp.bfloat16)
    return hi, lo


def band(in_cols, out_cols):
    offset = np.abs(np.asarray(in_cols)[:, None] - np.asarray(out_cols)[None, :])
    table = np.asarray(stencil_weights, np.float32)
    return np.where(offset <= 4, table[np.minimum(offset, 4)], np.float32(0.0)).astype(np.float32)


def two_terms(matrix):
    hi = matrix.astype(jnp.bfloat16)
    lo = (matrix - hi.astype(np.float32)).astype(jnp.bfloat16)
    return np.concatenate([hi, lo], axis=1)


def block_diagonal(matrix):
    return np.kron(np.eye(GROUPS, dtype=np.float32), matrix)


def zonal_matrices():
    own = np.arange(LANES)
    outer = np.concatenate([np.arange(-HALO, 0), LANES + np.arange(HALO)])
    inner = np.concatenate([np.arange(LANES - HALO, LANES), np.arange(HALO)])
    main = two_terms(band(own, own))
    near = band(outer, outer)
    far = band(inner, outer)
    inward = band(outer, inner)
    near[:HALO, HALO:] = near[HALO:, :HALO] = 0.0
    within = band(inner, inner)
    within[:HALO, HALO:] = within[HALO:, :HALO] = 0.0
    near, far, inward, within = [
        two_terms(block_diagonal(part)) for part in (near, far, inward, within)
    ]
    edge = np.concatenate([near, near, far, far], axis=0)
    again = np.concatenate([inward, inward, within, within], axis=0)
    inward = np.concatenate([inward, inward], axis=0)
    inward_only = np.concatenate([inward, np.zeros_like(inward)], axis=0)
    return np.concatenate([main, main], axis=0), np.concatenate([edge, inward_only], axis=1), again


def edge_kernel(field_ref, first_ref, second_ref, sems):
    rows = field_ref.shape[1]
    begin = (1 - lax.axis_index("lat") % 2) * (rows - HALO)
    copies = []
    for at, (start, target) in enumerate(
        [(begin, first_ref), (rows - HALO - begin, second_ref)]
    ):
        start = pl.multiple_of(start, HALO)
        copies.append(
            pltpu.make_async_copy(field_ref.at[:, pl.ds(start, HALO), :], target, sems.at[at])
        )
    for copy in copies:
        copy.start()
    for copy in copies:
        copy.wait()


def strip_kernel(span, field_ref, ext_ref, strip_ref):
    snaps, rows, _ = field_ref.shape

    def turn(at, carry):
        begin = pl.multiple_of(at * 8, 8)
        for tile in range(0, snaps, 8):
            ext_ref[pl.ds(4 + HALO + begin, 8), tile : tile + 8] = jnp.swapaxes(
                field_ref[tile : tile + 8, pl.ds(begin, 8), :], 0, 1
            )
        return carry

    lax.fori_loop(0, rows // 8, turn, 0, unroll=2)
    ends = jnp.zeros((4 + HALO, snaps, LANES), jnp.float32)
    ext_ref[: 4 + HALO] = ends
    ext_ref[4 + HALO + rows :] = ends
    group_of = lax.broadcasted_iota(jnp.int32, (snaps, LANES), 1) // STRIP

    def pack(at, carry):
        packed = jnp.zeros((snaps, LANES), jnp.float32)
        for group in range(GROUPS):
            values = ext_ref[4 + group * span + at]
            moved = pltpu.roll(values, (HALO + STRIP * group) % LANES, 1)
            packed = jnp.where(group_of == group, moved, packed)
        strip_ref[at] = packed
        return carry

    lax.fori_loop(0, span, pack, 0, unroll=2)


def message_kernel(
    span, ext_in_ref, strip_ref, low_ref, high_ref, ext_ref, full_ref, first_ref, second_ref
):
    snaps = strip_ref.shape[1]
    half = span // 2
    end = ext_ref.shape[0] - 4 - HALO
    lane = lax.broadcasted_iota(jnp.int32, (snaps, LANES), 1)
    lat_even = lax.axis_index("lat") % 2 == 0
    lon_even = lax.axis_index("lon") % 2 == 0
    full_ref[...] = strip_ref[...]
    for tile in range(0, snaps, 8):
        first = jnp.swapaxes(low_ref[tile : tile + 8], 0, 1)
        second = jnp.swapaxes(high_ref[tile : tile + 8], 0, 1)
        ext_ref[4 : 4 + HALO, tile : tile + 8] = jnp.where(lat_even, second, first)
        ext_ref[end : end + HALO, tile : tile + 8] = jnp.where(lat_even, first, second)
    for at in range(HALO):
        north, south = ext_ref[4 + at], ext_ref[end + at]
        full_ref[at] = jnp.where(lane < STRIP, pltpu.roll(north, HALO, 1), full_ref[at])
        last = span - HALO + at
        full_ref[last] = jnp.where(
            lane >= LANES - STRIP, pltpu.roll(south, LANES - HALO, 1), full_ref[last]
        )
    left = lane % STRIP < HALO
    for at in range(half):
        upper, lower = full_ref[at], full_ref[at + half]
        eastward = jnp.where(left, upper, pltpu.roll(lower, HALO, 1))
        westward = jnp.where(left, pltpu.roll(lower, LANES - HALO, 1), upper)
        first_ref[at] = jnp.where(lon_even, eastward, westward)
        second_ref[at] = jnp.where(lon_even, westward, eastward)


def stencil_row(center, pairs, zonal, zonal_rate, merid_rate):
    merid = stencil_weights[1] * pairs[0]
    for offset in range(2, 5):
        merid = merid + stencil_weights[offset] * pairs[offset - 1]
    scale = 1.0 + stencil_weights[0] * merid_rate
    return scale * center + merid_rate * merid + zonal_rate * zonal


def zonal_terms(parts, weights):
    product = jnp.dot(
        jnp.concatenate(parts, axis=1), weights, preferred_element_type=jnp.float32
    )
    return product[:, :LANES] + product[:, LANES:]


def rate_reader(rows, rates_refs):
    last = rows * lax.axis_size("lat") - 1
    origin = lax.axis_index("lat") * rows - HALO

    def read(at):
        row = jnp.clip(origin + at, 0, last)
        return [ref[row] for ref in rates_refs]

    return read


def stencil_rows(load, begin, span, part, rates, store):
    loaded = {}

    def row(at):
        if at not in loaded:
            loaded[at] = load(begin + at)
        return loaded[at]

    for at in range(span):
        here = at + 4
        pairs = [row(here + offset) + row(here - offset) for offset in range(1, 5)]
        values = rates(begin + at)
        store(at, stencil_row(row(here), pairs, part[at], values[0], values[1]), values)


def tile_kernel(span, lon_ref, lat_ref, weight_ref, ext_ref, main_ref, twice_ref, once_ref):
    snaps = ext_ref.shape[1]
    total = span * GROUPS
    rows = total - 2 * HALO
    rates = rate_reader(rows, (lon_ref, lat_ref, weight_ref))
    for tile in range(0, snaps, TILE):
        snap = slice(tile, tile + TILE)

        def first_pass(group, carry):
            begin = group * span
            center = ext_ref[pl.ds(4 + begin, span), snap].reshape(span * TILE, LANES)
            part = zonal_terms(hi_lo(center), main_ref[...]).reshape(span, TILE, LANES)

            def load(at):
                return ext_ref[at, snap]

            def store(at, value, _):
                once_ref[4 + begin + at] = value

            stencil_rows(load, begin, span, part, rates, store)
            return carry

        def second_pass(group, carry):
            begin = group * span
            center = once_ref[pl.ds(4 + begin, span)].reshape(span * TILE, LANES)
            part = zonal_terms(hi_lo(center), main_ref[...]).reshape(span, TILE, LANES)

            def load(at):
                return once_ref[at]

            def store(at, value, values):
                twice_ref[begin + at, snap] = values[2] * value

            stencil_rows(load, begin, span, part, rates, store)
            return carry

        lax.fori_loop(0, GROUPS, first_pass, 0)
        ends = jnp.zeros((4, TILE, LANES), jnp.float32)
        once_ref[:4] = ends
        once_ref[total + 4 :] = ends
        outside = jnp.zeros((HALO, TILE, LANES), jnp.float32)

        @pl.when(lax.axis_index("lat") == 0)
        def _():
            once_ref[4 : 4 + HALO] = outside

        @pl.when(lax.axis_index("lat") == lax.axis_size("lat") - 1)
        def _():
            once_ref[4 + HALO + rows : 4 + total] = outside

        lax.fori_loop(0, GROUPS, second_pass, 0)
    outside = jnp.zeros((HALO, snaps, LANES), jnp.float32)
    twice_ref[:HALO] = outside
    twice_ref[HALO + rows :] = outside


def close_ends(strip_ref, span):
    for at in range(4):
        strip_ref[at] = pltpu.roll(strip_ref[span + at], STRIP, 1)
        strip_ref[span + 4 + at] = pltpu.roll(strip_ref[4 + at], LANES - STRIP, 1)


def rim_kernel(
    span,
    lon_ref,
    lat_ref,
    weight_ref,
    twice_ref,
    strip_ref,
    first_ref,
    second_ref,
    edge_ref,
    again_ref,
    split_ref,
    gram_ref,
    outer_ref,
    side_ref,
    added_ref,
    rim_ref,
    strip_rates_ref,
):
    total, both, _ = split_ref.shape
    rows = total - 2 * HALO
    snaps = both // 2
    half = span // 2
    lon_even = lax.axis_index("lon") % 2 == 0
    lane = lax.broadcasted_iota(jnp.int32, (TILE, LANES), 1)
    left = lane % STRIP < HALO
    rim = (lane < HALO) | (lane >= LANES - HALO)
    group_of = lax.broadcasted_iota(jnp.int32, (8, LANES), 1) // STRIP
    rates = rate_reader(rows, (lon_ref, lat_ref, weight_ref))
    for at in range(span):
        packed = [jnp.zeros((8, LANES), jnp.float32)] * 3
        for group in range(GROUPS):
            here = group_of == group
            row = group * span + at
            values = rates(row)
            if row < HALO or row >= HALO + rows:
                values[2] = 0.0
            packed = [jnp.where(here, value, old) for value, old in zip(values, packed)]
        for kind in range(3):
            strip_rates_ref[kind, at] = packed[kind]

    def strip_rate(kind, at):
        return jnp.concatenate([strip_rates_ref[kind, at]] * (TILE // 8), axis=0)

    def strip_stencil(source_ref, at, zonal):
        pairs = [
            source_ref[4 + at + offset] + source_ref[4 + at - offset] for offset in range(1, 5)
        ]
        return stencil_row(
            source_ref[4 + at], pairs, zonal, strip_rate(0, at), strip_rate(1, at)
        )

    for tile in range(0, snaps, TILE):
        snap = slice(tile, tile + TILE)
        for at in range(half):
            first, second = first_ref[at, snap], second_ref[at, snap]
            west = jnp.where(lon_even, second, first)
            east = jnp.where(lon_even, first, second)
            outer_ref[4 + at] = jnp.where(left, west, east)
            outer_ref[4 + half + at] = jnp.where(
                left, pltpu.roll(west, LANES - HALO, 1), pltpu.roll(east, HALO, 1)
            )
        close_ends(outer_ref, span)
        hi, lo = hi_lo(outer_ref[4 : 4 + span].reshape(span * TILE, LANES))
        own_hi, own_lo = hi_lo(strip_ref[:, snap].reshape(span * TILE, LANES))
        product = jnp.dot(
            jnp.concatenate([hi, lo, own_hi, own_lo], axis=1),
            edge_ref[...],
            preferred_element_type=jnp.float32,
        ).reshape(span, TILE, 4 * LANES)
        for at in range(span):
            zonal = product[at, :, :LANES] + product[at, :, LANES : 2 * LANES]
            side_ref[at] = strip_stencil(outer_ref, at, zonal)
            added_ref[4 + at] = strip_rate(0, at) * (
                product[at, :, 2 * LANES : 3 * LANES] + product[at, :, 3 * LANES :]
            )
        close_ends(added_ref, span)
        hi, lo = hi_lo(side_ref[...].reshape(span * TILE, LANES))
        own_hi, own_lo = hi_lo(added_ref[4 : 4 + span].reshape(span * TILE, LANES))
        part = zonal_terms([hi, lo, own_hi, own_lo], again_ref[...]).reshape(span, TILE, LANES)
        for at in range(span):
            rim_ref[at, snap] = strip_rate(2, at) * strip_stencil(added_ref, at, part[at])

    def finish(group, grams):
        begin = group * span
        shift = LANES - HALO - STRIP * group
        for pair in range(0, span, 2):
            rows_done = []
            for at in (pair, pair + 1):
                terms = []
                for tile in range(0, snaps, TILE):
                    snap = slice(tile, tile + TILE)
                    moved = pltpu.roll(rim_ref[at, snap], shift, 1)
                    value = twice_ref[begin + at, snap] + jnp.where(rim, moved, 0.0)
                    terms.append(hi_lo(value))
                row = jnp.concatenate(
                    [term[0] for term in terms] + [term[1] for term in terms], axis=0
                )
                split_ref[begin + at] = row
                rows_done.append(row)
            two = jnp.concatenate(rows_done, axis=1)
            grams = grams + lax.dot_general(
                two, two, (((1,), (1,)), ((), ())), preferred_element_type=jnp.float32
            )
        return grams

    grams = lax.fori_loop(0, GROUPS, finish, jnp.zeros((both, both), jnp.float32))
    gram = (
        grams[:snaps, :snaps]
        + grams[snaps:, snaps:]
        + (grams[:snaps, snaps:] + grams[snaps:, :snaps])
    )
    gram_ref[...] = jnp.concatenate([gram[at : at + 8] for at in range(0, snaps, 8)], axis=1)


def basis_kernel(root_count, gram_ref, split_ref, basis_ref, factor_ref, left_ref):
    snaps = basis_ref.shape[0]

    @pl.when(pl.program_id(0) == 0)
    def _():
        row = lax.broadcasted_iota(jnp.int32, (snaps, 2 * snaps), 0)
        col = lax.broadcasted_iota(jnp.int32, (snaps, 2 * snaps), 1)
        packed = jnp.sum(gram_ref[...], axis=0)
        gram = jnp.concatenate(
            [packed[:, at : at + snaps] for at in range(0, packed.shape[1], snaps)], axis=0
        )
        work = jnp.concatenate([gram, jnp.zeros((snaps, snaps), jnp.float32)], axis=1)
        work = jnp.where(col == row + snaps, 1.0, work)
        for step in range(snaps):
            pivot_row = work[step : step + 1, :]
            ratio = work[:, step : step + 1] / work[step : step + 1, step : step + 1]
            work = work - jnp.where(row > step, ratio, 0.0) * pivot_row
        diagonal = jnp.sum(jnp.where(row == col, work, 0.0), axis=1, keepdims=True)
        work = work * lax.rsqrt(diagonal)
        upper = jnp.where(col >= row, work, 0.0)
        factor_ref[...] = upper[:, :snaps] / root_count
        hi, lo = hi_lo(work[:, snaps:] * root_count)
        left_ref[:snaps] = jnp.concatenate([hi, hi], axis=1)
        left_ref[snaps:] = jnp.concatenate([lo, jnp.zeros_like(lo)], axis=1)

    left = left_ref[...]
    start = pl.program_id(0) * basis_ref.shape[1] + HALO

    def body(at, carry):
        begin = pl.multiple_of(at * 16, 16)
        values = []
        for pair in range(8):
            row = start + begin + 2 * pair
            two = jnp.concatenate([split_ref[row], split_ref[row + 1]], axis=1)
            product = jnp.dot(left, two, preferred_element_type=jnp.float32)
            value = product[:snaps] + product[snaps:]
            values += [value[:, :LANES], value[:, LANES:]]
        turned = jnp.swapaxes(jnp.stack(values, axis=0), 0, 1)
        basis_ref[:, pl.ds(begin, 16), :] = turned.astype(jnp.bfloat16)
        return carry

    lax.fori_loop(0, basis_ref.shape[1] // 16, body, 0)


def pair_permutes(values, axis, periodic):
    count = lax.axis_size(axis)
    inner = [(i, i ^ 1) for i in range(count)]
    outer = []
    for i in range(1, count, 2):
        if periodic or i + 1 < count:
            outer += [(i, (i + 1) % count), ((i + 1) % count, i)]
    return lax.ppermute(values[0], axis, inner), lax.ppermute(values[1], axis, outer)


def gather_all(values):
    axes = ("lat", "lon")
    count = lax.axis_size(axes)
    return lax.all_to_all(jnp.broadcast_to(values, (count,) + values.shape), axes, 0, 0)


def whole(memory_space=pltpu.VMEM):
    return pl.BlockSpec(memory_space=memory_space)


def shards(field, lon_rate, lat_rate):
    snaps, rows, cols = field.shape
    total_rows = rows * lax.axis_size("lat")
    total_cells = total_rows * cols * lax.axis_size("lon")
    span = (rows + 2 * HALO) // GROUPS
    f32 = jnp.float32
    limits = pltpu.CompilerParams(vmem_limit_bytes=VMEM_BYTES)

    total = span * GROUPS
    ext = jax.ShapeDtypeStruct((total + 8, snaps, cols), f32)
    strip = jax.ShapeDtypeStruct((span, snaps, cols), f32)
    half = jax.ShapeDtypeStruct((span // 2, snaps, cols), f32)
    edge_rows = jax.ShapeDtypeStruct((snaps, HALO, cols), f32)
    first, second = pl.pallas_call(
        edge_kernel,
        in_specs=[whole(pl.ANY)],
        out_specs=[whole()] * 2,
        out_shape=[edge_rows, edge_rows],
        scratch_shapes=[pltpu.SemaphoreType.DMA((2,))],
        compiler_params=pltpu.CompilerParams(vmem_limit_bytes=60 * 1024 * 1024),
        name="lat_messages",
    )(field)
    low, high = pair_permutes([first, second], "lat", False)
    turned, packed = pl.pallas_call(
        functools.partial(strip_kernel, span),
        in_specs=[whole()],
        out_specs=[whole()] * 2,
        out_shape=[ext, strip],
        compiler_params=limits,
        name="turn_and_pack",
    )(field)
    turned, packed, first, second = pl.pallas_call(
        functools.partial(message_kernel, span),
        in_specs=[whole()] * 4,
        out_specs=[whole()] * 4,
        out_shape=[ext, strip, half, half],
        input_output_aliases={0: 0},
        compiler_params=limits,
        name="lon_messages",
    )(turned, packed, low, high)
    first, second = pair_permutes([first, second], "lon", True)

    weight = area_weight(0, total_rows, total_rows)

    main, edge, again = zonal_matrices()
    bf16 = jnp.bfloat16
    twice = pl.pallas_call(
        functools.partial(tile_kernel, span),
        in_specs=[whole(pltpu.SMEM)] * 3 + [whole()] * 2,
        out_specs=whole(),
        out_shape=jax.ShapeDtypeStruct((total, snaps, cols), f32),
        scratch_shapes=[pltpu.VMEM((total + 8, TILE, cols), f32)],
        compiler_params=limits,
        cost_estimate=pl.CostEstimate(
            flops=100 * snaps * rows * cols, bytes_accessed=8 * snaps * rows * cols, transcendentals=0
        ),
        name="both_passes",
    )(lon_rate, lat_rate, weight, turned, main)
    split, gram = pl.pallas_call(
        functools.partial(rim_kernel, span),
        in_specs=[whole(pltpu.SMEM)] * 3 + [whole()] * 6,
        out_specs=[whole(), whole()],
        out_shape=[
            jax.ShapeDtypeStruct((total, 2 * snaps, cols), bf16),
            jax.ShapeDtypeStruct((8, snaps // 8 * snaps), f32),
        ],
        scratch_shapes=[
            pltpu.VMEM((span + 8, TILE, cols), f32),
            pltpu.VMEM((span, TILE, cols), f32),
            pltpu.VMEM((span + 8, TILE, cols), f32),
            pltpu.VMEM((span, snaps, cols), f32),
            pltpu.VMEM((3, span, 8, cols), f32),
        ],
        compiler_params=limits,
        name="rim_and_gram",
    )(lon_rate, lat_rate, weight, twice, packed, first, second, edge, again)

    grams = gather_all(gram)
    block = 64
    basis, factor = pl.pallas_call(
        functools.partial(basis_kernel, math.sqrt(total_cells)),
        grid=(rows // block,),
        in_specs=[
            whole(),
            whole(),
        ],
        out_specs=[
            pl.BlockSpec((snaps, block, cols), lambda i: (0, i, 0)),
            pl.BlockSpec((snaps, snaps), lambda i: (0, 0)),
        ],
        out_shape=[
            jax.ShapeDtypeStruct((snaps, rows, cols), bf16),
            jax.ShapeDtypeStruct((snaps, snaps), f32),
        ],
        scratch_shapes=[
            pltpu.VMEM((2 * snaps, 2 * snaps), bf16),
        ],
        compiler_params=limits,
        name="factor_and_basis",
    )(grams, split)
    return (basis, factor)


def solution(mesh):
    return jax.shard_map(
        shards,
        mesh=mesh,
        in_specs=(P(None, "lat", "lon"), P(), P()),
        out_specs=(P(None, "lat", "lon"), P()),
        check_vma=False,
    )
```

```python
import functools
import math

import jax
import jax.numpy as jnp
import numpy as np
from jax import lax
from jax.experimental import pallas as pl
from jax.experimental.pallas import tpu as pltpu
from jax.sharding import PartitionSpec as P

stencil_weights = (-205.0 / 72.0, 8.0 / 5.0, -1.0 / 5.0, 8.0 / 315.0, -1.0 / 560.0)

HALO = 8
STRIP = 2 * HALO
LANES = 128
GROUPS = LANES // STRIP
TILE = 16
PIVOTS = 8
VMEM_BYTES = 24 * 1024 * 1024


def area_weight(first_row, row_count, total_rows):
    row_index = (jnp.arange(row_count) + first_row).astype(jnp.float32)
    latitude = (-90.0 + (row_index + 0.5) * (180.0 / total_rows)) * (math.pi / 180.0)
    return jnp.sqrt(jnp.cos(latitude))


def hi_lo(values):
    hi = values.astype(jnp.bfloat16)
    lo = (values - hi.astype(jnp.float32)).astype(jnp.bfloat16)
    return hi, lo


def band(in_cols, out_cols):
    offset = np.abs(np.asarray(in_cols)[:, None] - np.asarray(out_cols)[None, :])
    table = np.asarray(stencil_weights, np.float32)
    return np.where(offset <= 4, table[np.minimum(offset, 4)], np.float32(0.0)).astype(np.float32)


def two_terms(matrix):
    hi = matrix.astype(jnp.bfloat16)
    lo = (matrix - hi.astype(np.float32)).astype(jnp.bfloat16)
    return np.concatenate([hi, lo], axis=1)


def block_diagonal(matrix):
    return np.kron(np.eye(GROUPS, dtype=np.float32), matrix)


def zonal_matrices():
    own = np.arange(LANES)
    outer = np.concatenate([np.arange(-HALO, 0), LANES + np.arange(HALO)])
    inner = np.concatenate([np.arange(LANES - HALO, LANES), np.arange(HALO)])
    main = two_terms(band(own, own))
    near = band(outer, outer)
    far = band(inner, outer)
    inward = band(outer, inner)
    near[:HALO, HALO:] = near[HALO:, :HALO] = 0.0
    within = band(inner, inner)
    within[:HALO, HALO:] = within[HALO:, :HALO] = 0.0
    near, far, inward, within = [
        two_terms(block_diagonal(part)) for part in (near, far, inward, within)
    ]
    edge = np.concatenate([near, near, far, far], axis=0)
    again = np.concatenate([inward, inward, within, within], axis=0)
    inward = np.concatenate([inward, inward], axis=0)
    inward_only = np.concatenate([inward, np.zeros_like(inward)], axis=0)
    return np.concatenate([main, main], axis=0), np.concatenate([edge, inward_only], axis=1), again


def edge_kernel(field_ref, first_ref, second_ref):
    rows = field_ref.shape[1]
    lat_even = lax.axis_index("lat") % 2 == 0
    north, south = field_ref[:, :HALO], field_ref[:, rows - HALO :]
    first_ref[...] = jnp.where(lat_even, south, north)
    second_ref[...] = jnp.where(lat_even, north, south)


def strip_kernel(span, field_ref, ext_ref, strip_ref):
    snaps, rows, _ = field_ref.shape

    def turn(at, carry):
        begin = pl.multiple_of(at * 8, 8)
        for tile in range(0, snaps, 8):
            ext_ref[pl.ds(4 + HALO + begin, 8), tile : tile + 8] = jnp.swapaxes(
                field_ref[tile : tile + 8, pl.ds(begin, 8), :], 0, 1
            )
        return carry

    lax.fori_loop(0, rows // 8, turn, 0, unroll=4)
    ends = jnp.zeros((4 + HALO, snaps, LANES), jnp.float32)
    ext_ref[: 4 + HALO] = ends
    ext_ref[4 + HALO + rows :] = ends
    group_of = lax.broadcasted_iota(jnp.int32, (snaps, LANES), 1) // STRIP

    def pack(at, carry):
        packed = jnp.zeros((snaps, LANES), jnp.float32)
        for group in range(GROUPS):
            values = ext_ref[4 + group * span + at]
            moved = pltpu.roll(values, (HALO + STRIP * group) % LANES, 1)
            packed = jnp.where(group_of == group, moved, packed)
        strip_ref[at] = packed
        return carry

    lax.fori_loop(0, span, pack, 0, unroll=span // 2)


def message_kernel(
    span, ext_in_ref, strip_ref, low_ref, high_ref, ext_ref, full_ref, first_ref, second_ref
):
    snaps = strip_ref.shape[1]
    half = span // 2
    end = ext_ref.shape[0] - 4 - HALO
    lane = lax.broadcasted_iota(jnp.int32, (snaps, LANES), 1)
    lat_even = lax.axis_index("lat") % 2 == 0
    lon_even = lax.axis_index("lon") % 2 == 0
    full_ref[...] = strip_ref[...]
    for tile in range(0, snaps, 8):
        first = jnp.swapaxes(low_ref[tile : tile + 8], 0, 1)
        second = jnp.swapaxes(high_ref[tile : tile + 8], 0, 1)
        ext_ref[4 : 4 + HALO, tile : tile + 8] = jnp.where(lat_even, second, first)
        ext_ref[end : end + HALO, tile : tile + 8] = jnp.where(lat_even, first, second)
    for at in range(HALO):
        north, south = ext_ref[4 + at], ext_ref[end + at]
        full_ref[at] = jnp.where(lane < STRIP, pltpu.roll(north, HALO, 1), full_ref[at])
        last = span - HALO + at
        full_ref[last] = jnp.where(
            lane >= LANES - STRIP, pltpu.roll(south, LANES - HALO, 1), full_ref[last]
        )
    left = lane % STRIP < HALO
    for at in range(half):
        upper, lower = full_ref[at], full_ref[at + half]
        eastward = jnp.where(left, upper, pltpu.roll(lower, HALO, 1))
        westward = jnp.where(left, pltpu.roll(lower, LANES - HALO, 1), upper)
        first_ref[at] = jnp.where(lon_even, eastward, westward)
        second_ref[at] = jnp.where(lon_even, westward, eastward)


def stencil_row(center, pairs, zonal, zonal_rate, merid_rate):
    merid = stencil_weights[1] * pairs[0]
    for offset in range(2, 5):
        merid = merid + stencil_weights[offset] * pairs[offset - 1]
    scale = 1.0 + stencil_weights[0] * merid_rate
    return scale * center + merid_rate * merid + zonal_rate * zonal


def zonal_terms(parts, weights):
    product = jnp.dot(
        jnp.concatenate(parts, axis=1), weights, preferred_element_type=jnp.float32
    )
    return product[:, :LANES] + product[:, LANES:]


def rate_reader(rows, rates_refs):
    last = rows * lax.axis_size("lat") - 1
    origin = lax.axis_index("lat") * rows - HALO

    def read(at):
        row = jnp.clip(origin + at, 0, last)
        return [ref[row] for ref in rates_refs]

    return read


def stencil_rows(load, begin, span, part, rates, store):
    loaded = {}

    def row(at):
        if at not in loaded:
            loaded[at] = load(begin + at)
        return loaded[at]

    for at in range(span):
        here = at + 4
        pairs = [row(here + offset) + row(here - offset) for offset in range(1, 5)]
        values = rates(begin + at)
        store(at, stencil_row(row(here), pairs, part[at], values[0], values[1]), values)


def tile_kernel(span, lon_ref, lat_ref, weight_ref, ext_ref, main_ref, twice_ref, once_ref):
    snaps = ext_ref.shape[1]
    total = span * GROUPS
    rows = total - 2 * HALO
    rates = rate_reader(rows, (lon_ref, lat_ref, weight_ref))
    chunk = total // 2
    ends = jnp.zeros((4, TILE, LANES), jnp.float32)
    once_ref[:4] = ends
    once_ref[total + 4 :] = ends

    def one_tile(tile, carry):
        snap = pl.ds(pl.multiple_of(tile * TILE, TILE), TILE)

        def first_pass(part, carry):
            begin = part * chunk
            center = ext_ref[pl.ds(4 + begin, chunk), snap].reshape(chunk * TILE, LANES)
            part = zonal_terms(hi_lo(center), main_ref[...]).reshape(chunk, TILE, LANES)

            def load(at):
                return ext_ref[at, snap]

            def store(at, value, _):
                once_ref[4 + begin + at] = value

            stencil_rows(load, begin, chunk, part, rates, store)
            return carry

        def second_pass(part, carry):
            begin = part * chunk
            center = once_ref[pl.ds(4 + begin, chunk)].reshape(chunk * TILE, LANES)
            part = zonal_terms(hi_lo(center), main_ref[...]).reshape(chunk, TILE, LANES)

            def load(at):
                return once_ref[at]

            def store(at, value, values):
                twice_ref[begin + at, snap] = values[2] * value

            stencil_rows(load, begin, chunk, part, rates, store)
            return carry

        lax.fori_loop(0, 2, first_pass, 0)
        outside = jnp.zeros((HALO, TILE, LANES), jnp.float32)

        @pl.when(lax.axis_index("lat") == 0)
        def _():
            once_ref[4 : 4 + HALO] = outside

        @pl.when(lax.axis_index("lat") == lax.axis_size("lat") - 1)
        def _():
            once_ref[4 + HALO + rows : 4 + total] = outside

        lax.fori_loop(0, 2, second_pass, 0)
        return carry

    lax.fori_loop(0, snaps // TILE, one_tile, 0)
    outside = jnp.zeros((HALO, snaps, LANES), jnp.float32)
    twice_ref[:HALO] = outside
    twice_ref[HALO + rows :] = outside


def close_ends(strip_ref, span):
    for at in range(4):
        strip_ref[at] = pltpu.roll(strip_ref[span + at], STRIP, 1)
        strip_ref[span + 4 + at] = pltpu.roll(strip_ref[4 + at], LANES - STRIP, 1)


def rim_kernel(
    span,
    lon_ref,
    lat_ref,
    weight_ref,
    twice_ref,
    strip_ref,
    first_ref,
    second_ref,
    edge_ref,
    again_ref,
    split_ref,
    gram_ref,
    outer_ref,
    side_ref,
    added_ref,
    rim_ref,
    strip_rates_ref,
):
    total, both, _ = split_ref.shape
    rows = total - 2 * HALO
    snaps = both // 2
    half = span // 2
    lon_even = lax.axis_index("lon") % 2 == 0
    lane = lax.broadcasted_iota(jnp.int32, (TILE, LANES), 1)
    left = lane % STRIP < HALO
    rim = (lane < HALO) | (lane >= LANES - HALO)
    group_of = lax.broadcasted_iota(jnp.int32, (8, LANES), 1) // STRIP
    rates = rate_reader(rows, (lon_ref, lat_ref, weight_ref))
    for at in range(span):
        packed = [jnp.zeros((8, LANES), jnp.float32)] * 3
        for group in range(GROUPS):
            here = group_of == group
            row = group * span + at
            values = rates(row)
            if row < HALO or row >= HALO + rows:
                values[2] = 0.0
            packed = [jnp.where(here, value, old) for value, old in zip(values, packed)]
        for kind in range(3):
            strip_rates_ref[kind, at] = packed[kind]

    def strip_rate(kind, at):
        return jnp.concatenate([strip_rates_ref[kind, at]] * (TILE // 8), axis=0)

    def strip_stencil(source_ref, at, zonal):
        pairs = [
            source_ref[4 + at + offset] + source_ref[4 + at - offset] for offset in range(1, 5)
        ]
        return stencil_row(
            source_ref[4 + at], pairs, zonal, strip_rate(0, at), strip_rate(1, at)
        )

    for tile in range(0, snaps, TILE):
        snap = slice(tile, tile + TILE)
        for at in range(half):
            first, second = first_ref[at, snap], second_ref[at, snap]
            west = jnp.where(lon_even, second, first)
            east = jnp.where(lon_even, first, second)
            outer_ref[4 + at] = jnp.where(left, west, east)
            outer_ref[4 + half + at] = jnp.where(
                left, pltpu.roll(west, LANES - HALO, 1), pltpu.roll(east, HALO, 1)
            )
        close_ends(outer_ref, span)
        hi, lo = hi_lo(outer_ref[4 : 4 + span].reshape(span * TILE, LANES))
        own_hi, own_lo = hi_lo(strip_ref[:, snap].reshape(span * TILE, LANES))
        product = jnp.dot(
            jnp.concatenate([hi, lo, own_hi, own_lo], axis=1),
            edge_ref[...],
            preferred_element_type=jnp.float32,
        ).reshape(span, TILE, 4 * LANES)
        for at in range(span):
            zonal = product[at, :, :LANES] + product[at, :, LANES : 2 * LANES]
            side_ref[at] = strip_stencil(outer_ref, at, zonal)
            added_ref[4 + at] = strip_rate(0, at) * (
                product[at, :, 2 * LANES : 3 * LANES] + product[at, :, 3 * LANES :]
            )
        close_ends(added_ref, span)
        hi, lo = hi_lo(side_ref[...].reshape(span * TILE, LANES))
        own_hi, own_lo = hi_lo(added_ref[4 : 4 + span].reshape(span * TILE, LANES))
        part = zonal_terms([hi, lo, own_hi, own_lo], again_ref[...]).reshape(span, TILE, LANES)
        for at in range(span):
            rim_ref[at, snap] = strip_rate(2, at) * strip_stencil(added_ref, at, part[at])

    def finish(group, grams):
        begin = group * span
        shift = LANES - HALO - STRIP * group
        for pair in range(0, span, 2):
            rows_done = []
            for at in (pair, pair + 1):
                terms = []
                for tile in range(0, snaps, TILE):
                    snap = slice(tile, tile + TILE)
                    moved = pltpu.roll(rim_ref[at, snap], shift, 1)
                    value = twice_ref[begin + at, snap] + jnp.where(rim, moved, 0.0)
                    terms.append(hi_lo(value))
                row = jnp.concatenate(
                    [term[0] for term in terms] + [term[1] for term in terms], axis=0
                )
                split_ref[begin + at] = row
                rows_done.append(row)
            two = jnp.concatenate(rows_done, axis=1)
            grams = grams + lax.dot_general(
                two, two, (((1,), (1,)), ((), ())), preferred_element_type=jnp.float32
            )
        return grams

    grams = lax.fori_loop(0, GROUPS, finish, jnp.zeros((both, both), jnp.float32))
    gram = (
        grams[:snaps, :snaps]
        + grams[snaps:, snaps:]
        + (grams[:snaps, snaps:] + grams[snaps:, :snaps])
    )
    gram_ref[...] = jnp.concatenate([gram[at : at + 8] for at in range(0, snaps, 8)], axis=1)


def basis_kernel(root_count, gram_ref, split_ref, basis_ref, factor_ref, left_ref):
    snaps = basis_ref.shape[0]

    @pl.when(pl.program_id(0) == 0)
    def _():
        row = lax.broadcasted_iota(jnp.int32, (snaps, 2 * snaps), 0)
        col = lax.broadcasted_iota(jnp.int32, (snaps, 2 * snaps), 1)
        packed = jnp.sum(gram_ref[...], axis=0)
        gram = jnp.concatenate(
            [packed[:, at : at + snaps] for at in range(0, packed.shape[1], snaps)], axis=0
        )
        work = jnp.concatenate([gram, jnp.zeros((snaps, snaps), jnp.float32)], axis=1)
        work = jnp.where(col == row + snaps, 1.0, work)
        for step in range(0, snaps, PIVOTS):
            below = [
                jnp.broadcast_to(work[:, pivot : pivot + 1], work.shape)
                for pivot in range(step, step + PIVOTS)
            ]
            across = [work[pivot : pivot + 1, :] for pivot in range(step, step + PIVOTS)]
            for at in range(PIVOTS):
                pivot = step + at
                ratio = 1.0 / below[at][pivot : pivot + 1, :]
                rest = jnp.where(row > pivot, below[at], 0.0)
                work = work - (rest * ratio) * across[at]
                for later in range(at + 1, PIVOTS):
                    factor = below[later][pivot : pivot + 1, :] * ratio
                    below[later] = below[later] - rest * factor
                    across[later] = across[later] - factor * across[at]
        diagonal = jnp.sum(jnp.where(row == col, work, 0.0), axis=1, keepdims=True)
        work = work * lax.rsqrt(diagonal)
        upper = jnp.where(col >= row, work, 0.0)
        factor_ref[...] = upper[:, :snaps] / root_count
        hi, lo = hi_lo(work[:, snaps:] * root_count)
        left_ref[:snaps] = jnp.concatenate([hi, hi], axis=1)
        left_ref[snaps:] = jnp.concatenate([lo, jnp.zeros_like(lo)], axis=1)

    left = left_ref[...]
    start = pl.program_id(0) * basis_ref.shape[1] + HALO

    def body(at, carry):
        begin = pl.multiple_of(at * 16, 16)
        values = []
        for pair in range(8):
            row = start + begin + 2 * pair
            two = jnp.concatenate([split_ref[row], split_ref[row + 1]], axis=1)
            product = jnp.dot(left, two, preferred_element_type=jnp.float32)
            value = product[:snaps] + product[snaps:]
            values += [value[:, :LANES], value[:, LANES:]]
        turned = jnp.swapaxes(jnp.stack(values, axis=0), 0, 1)
        basis_ref[:, pl.ds(begin, 16), :] = turned.astype(jnp.bfloat16)
        return carry

    lax.fori_loop(0, basis_ref.shape[1] // 16, body, 0)


def pair_permutes(values, axis, periodic):
    count = lax.axis_size(axis)
    inner = [(i, i ^ 1) for i in range(count)]
    outer = []
    for i in range(1, count, 2):
        if periodic or i + 1 < count:
            outer += [(i, (i + 1) % count), ((i + 1) % count, i)]
    return lax.ppermute(values[0], axis, inner), lax.ppermute(values[1], axis, outer)


def gather_all(values):
    axes = ("lat", "lon")
    count = lax.axis_size(axes)
    return lax.all_to_all(jnp.broadcast_to(values, (count,) + values.shape), axes, 0, 0)


def whole(memory_space=pltpu.VMEM):
    return pl.BlockSpec(memory_space=memory_space)


def shards(field, lon_rate, lat_rate):
    snaps, rows, cols = field.shape
    total_rows = rows * lax.axis_size("lat")
    total_cells = total_rows * cols * lax.axis_size("lon")
    span = (rows + 2 * HALO) // GROUPS
    f32 = jnp.float32
    limits = pltpu.CompilerParams(vmem_limit_bytes=VMEM_BYTES)

    total = span * GROUPS
    ext = jax.ShapeDtypeStruct((total + 8, snaps, cols), f32)
    strip = jax.ShapeDtypeStruct((span, snaps, cols), f32)
    half = jax.ShapeDtypeStruct((span // 2, snaps, cols), f32)
    edge_rows = jax.ShapeDtypeStruct((snaps, HALO, cols), f32)
    first, second = pl.pallas_call(
        edge_kernel,
        in_specs=[whole()],
        out_specs=[whole()] * 2,
        out_shape=[edge_rows, edge_rows],
        compiler_params=limits,
        name="lat_messages",
    )(field)
    low, high = pair_permutes([first, second], "lat", False)
    turned, packed = pl.pallas_call(
        functools.partial(strip_kernel, span),
        in_specs=[whole()],
        out_specs=[whole()] * 2,
        out_shape=[ext, strip],
        compiler_params=limits,
        name="turn_and_pack",
    )(field)
    turned, packed, first, second = pl.pallas_call(
        functools.partial(message_kernel, span),
        in_specs=[whole()] * 4,
        out_specs=[whole()] * 4,
        out_shape=[ext, strip, half, half],
        input_output_aliases={0: 0},
        compiler_params=limits,
        name="lon_messages",
    )(turned, packed, low, high)
    first, second = pair_permutes([first, second], "lon", True)

    weight = area_weight(0, total_rows, total_rows)

    main, edge, again = zonal_matrices()
    bf16 = jnp.bfloat16
    twice = pl.pallas_call(
        functools.partial(tile_kernel, span),
        in_specs=[whole(pltpu.SMEM)] * 3 + [whole()] * 2,
        out_specs=whole(),
        out_shape=jax.ShapeDtypeStruct((total, snaps, cols), f32),
        scratch_shapes=[pltpu.VMEM((total + 8, TILE, cols), f32)],
        compiler_params=limits,
        cost_estimate=pl.CostEstimate(
            flops=100 * snaps * rows * cols, bytes_accessed=8 * snaps * rows * cols, transcendentals=0
        ),
        name="both_passes",
    )(lon_rate, lat_rate, weight, turned, main)
    split, gram = pl.pallas_call(
        functools.partial(rim_kernel, span),
        in_specs=[whole(pltpu.SMEM)] * 3 + [whole()] * 6,
        out_specs=[whole(), whole()],
        out_shape=[
            jax.ShapeDtypeStruct((total, 2 * snaps, cols), bf16),
            jax.ShapeDtypeStruct((8, snaps // 8 * snaps), f32),
        ],
        scratch_shapes=[
            pltpu.VMEM((span + 8, TILE, cols), f32),
            pltpu.VMEM((span, TILE, cols), f32),
            pltpu.VMEM((span + 8, TILE, cols), f32),
            pltpu.VMEM((span, snaps, cols), f32),
            pltpu.VMEM((3, span, 8, cols), f32),
        ],
        compiler_params=limits,
        name="rim_and_gram",
    )(lon_rate, lat_rate, weight, twice, packed, first, second, edge, again)

    grams = gather_all(gram)
    block = 64
    basis, factor = pl.pallas_call(
        functools.partial(basis_kernel, math.sqrt(total_cells)),
        grid=(rows // block,),
        in_specs=[
            whole(),
            whole(),
        ],
        out_specs=[
            pl.BlockSpec((snaps, block, cols), lambda i: (0, i, 0)),
            pl.BlockSpec((snaps, snaps), lambda i: (0, 0)),
        ],
        out_shape=[
            jax.ShapeDtypeStruct((snaps, rows, cols), bf16),
            jax.ShapeDtypeStruct((snaps, snaps), f32),
        ],
        scratch_shapes=[
            pltpu.VMEM((2 * snaps, 2 * snaps), bf16),
        ],
        compiler_params=limits,
        name="factor_and_basis",
    )(grams, split)
    return (basis, factor)


def solution(mesh):
    return jax.shard_map(
        shards,
        mesh=mesh,
        in_specs=(P(None, "lat", "lon"), P(), P()),
        out_specs=(P(None, "lat", "lon"), P()),
        check_vma=False,
    )
```

```python
import functools
import math

import jax
import jax.numpy as jnp
import numpy as np
from jax import lax
from jax.experimental import pallas as pl
from jax.experimental.pallas import tpu as pltpu
from jax.sharding import PartitionSpec as P

stencil_weights = (-205.0 / 72.0, 8.0 / 5.0, -1.0 / 5.0, 8.0 / 315.0, -1.0 / 560.0)

HALO = 8
STRIP = 2 * HALO
LANES = 128
GROUPS = LANES // STRIP
TILE = 16
PIVOTS = 8
VMEM_BYTES = 24 * 1024 * 1024


def area_weight(total_rows):
    row_index = np.arange(total_rows).astype(np.float32)
    step = np.float32(180.0 / total_rows)
    latitude = np.float32(-90.0) + (row_index + np.float32(0.5)) * step
    return np.sqrt(np.cos(latitude * np.float32(math.pi / 180.0))).astype(np.float32)


def hi_lo(values):
    hi = values.astype(jnp.bfloat16)
    lo = (values - hi.astype(jnp.float32)).astype(jnp.bfloat16)
    return hi, lo


def band(in_cols, out_cols):
    offset = np.abs(np.asarray(in_cols)[:, None] - np.asarray(out_cols)[None, :])
    table = np.asarray(stencil_weights, np.float32)
    return np.where(offset <= 4, table[np.minimum(offset, 4)], np.float32(0.0)).astype(np.float32)


def two_terms(matrix):
    hi = matrix.astype(jnp.bfloat16)
    lo = (matrix - hi.astype(np.float32)).astype(jnp.bfloat16)
    return np.concatenate([hi, lo], axis=1)


def block_diagonal(matrix):
    return np.kron(np.eye(GROUPS, dtype=np.float32), matrix)


def zonal_matrices():
    own = np.arange(LANES)
    outer = np.concatenate([np.arange(-HALO, 0), LANES + np.arange(HALO)])
    inner = np.concatenate([np.arange(LANES - HALO, LANES), np.arange(HALO)])
    main = two_terms(band(own, own))
    near = band(outer, outer)
    far = band(inner, outer)
    inward = band(outer, inner)
    near[:HALO, HALO:] = near[HALO:, :HALO] = 0.0
    within = band(inner, inner)
    within[:HALO, HALO:] = within[HALO:, :HALO] = 0.0
    near, far, inward, within = [
        two_terms(block_diagonal(part)) for part in (near, far, inward, within)
    ]
    edge = np.concatenate([near, near, far, far], axis=0)
    again = np.concatenate([inward, inward, within, within], axis=0)
    inward = np.concatenate([inward, inward], axis=0)
    inward_only = np.concatenate([inward, np.zeros_like(inward)], axis=0)
    return np.concatenate([main, main], axis=0), np.concatenate([edge, inward_only], axis=1), again


def edge_kernel(field_ref, first_ref, second_ref):
    rows = field_ref.shape[1]
    lat_even = lax.axis_index("lat") % 2 == 0
    north, south = field_ref[:, :HALO], field_ref[:, rows - HALO :]
    first_ref[...] = jnp.where(lat_even, south, north)
    second_ref[...] = jnp.where(lat_even, north, south)


def strip_kernel(
    span, lon_ref, lat_ref, weight_ref, field_ref, ext_ref, strip_ref, strip_rates_ref
):
    snaps, rows, _ = field_ref.shape

    def turn(at, carry):
        begin = pl.multiple_of(at * 8, 8)
        for tile in range(0, snaps, 8):
            ext_ref[pl.ds(4 + HALO + begin, 8), tile : tile + 8] = jnp.swapaxes(
                field_ref[tile : tile + 8, pl.ds(begin, 8), :], 0, 1
            )
        return carry

    lax.fori_loop(0, rows // 8, turn, 0, unroll=4)
    ends = jnp.zeros((4 + HALO, snaps, LANES), jnp.float32)
    ext_ref[: 4 + HALO] = ends
    ext_ref[4 + HALO + rows :] = ends
    group_of = lax.broadcasted_iota(jnp.int32, (snaps, LANES), 1) // STRIP

    def pack(at, carry):
        packed = jnp.zeros((snaps, LANES), jnp.float32)
        for group in range(GROUPS):
            values = ext_ref[4 + group * span + at]
            moved = pltpu.roll(values, (HALO + STRIP * group) % LANES, 1)
            packed = jnp.where(group_of == group, moved, packed)
        strip_ref[at] = packed
        return carry

    lax.fori_loop(0, span, pack, 0, unroll=span // 2)
    lane_group = lax.broadcasted_iota(jnp.int32, (8, LANES), 1) // STRIP
    rates = rate_reader(rows, (lon_ref, lat_ref, weight_ref))
    for at in range(span):
        values_at = [jnp.zeros((8, LANES), jnp.float32)] * 3
        for group in range(GROUPS):
            here = lane_group == group
            row = group * span + at
            values = rates(row)
            if row < HALO or row >= HALO + rows:
                values[2] = 0.0
            values_at = [jnp.where(here, value, old) for value, old in zip(values, values_at)]
        for kind in range(3):
            strip_rates_ref[kind, at] = values_at[kind]


def message_kernel(
    span, ext_in_ref, strip_ref, low_ref, high_ref, ext_ref, full_ref, first_ref, second_ref
):
    snaps = strip_ref.shape[1]
    half = span // 2
    end = ext_ref.shape[0] - 4 - HALO
    lane = lax.broadcasted_iota(jnp.int32, (snaps, LANES), 1)
    lat_even = lax.axis_index("lat") % 2 == 0
    lon_even = lax.axis_index("lon") % 2 == 0
    full_ref[...] = strip_ref[...]
    for tile in range(0, snaps, 8):
        first = jnp.swapaxes(low_ref[tile : tile + 8], 0, 1)
        second = jnp.swapaxes(high_ref[tile : tile + 8], 0, 1)
        ext_ref[4 : 4 + HALO, tile : tile + 8] = jnp.where(lat_even, second, first)
        ext_ref[end : end + HALO, tile : tile + 8] = jnp.where(lat_even, first, second)
    for at in range(HALO):
        north, south = ext_ref[4 + at], ext_ref[end + at]
        full_ref[at] = jnp.where(lane < STRIP, pltpu.roll(north, HALO, 1), full_ref[at])
        last = span - HALO + at
        full_ref[last] = jnp.where(
            lane >= LANES - STRIP, pltpu.roll(south, LANES - HALO, 1), full_ref[last]
        )
    left = lane % STRIP < HALO
    for at in range(half):
        upper, lower = full_ref[at], full_ref[at + half]
        eastward = jnp.where(left, upper, pltpu.roll(lower, HALO, 1))
        westward = jnp.where(left, pltpu.roll(lower, LANES - HALO, 1), upper)
        first_ref[at] = jnp.where(lon_even, eastward, westward)
        second_ref[at] = jnp.where(lon_even, westward, eastward)


def stencil_row(center, pairs, zonal, zonal_rate, merid_rate, weight=None):
    merid = stencil_weights[1] * pairs[0]
    for offset in range(2, 5):
        merid = merid + stencil_weights[offset] * pairs[offset - 1]
    scale = 1.0 + stencil_weights[0] * merid_rate
    if weight is not None:
        scale, merid_rate, zonal_rate = scale * weight, merid_rate * weight, zonal_rate * weight
    return scale * center + merid_rate * merid + zonal_rate * zonal


def zonal_terms(parts, weights):
    product = jnp.dot(
        jnp.concatenate(parts, axis=1), weights, preferred_element_type=jnp.float32
    )
    return product[:, :LANES] + product[:, LANES:]


def rate_reader(rows, rates_refs):
    last = rows * lax.axis_size("lat") - 1
    origin = lax.axis_index("lat") * rows - HALO

    def read(at):
        row = jnp.clip(origin + at, 0, last)
        return [ref[row] for ref in rates_refs]

    return read


def stencil_rows(load, begin, span, part, rates, store):
    loaded = {}

    def row(at):
        if at not in loaded:
            loaded[at] = load(begin + at)
        return loaded[at]

    for at in range(span):
        here = at + 4
        pairs = [row(here + offset) + row(here - offset) for offset in range(1, 5)]
        store(at, stencil_row(row(here), pairs, part[at], *rates(begin + at)))


def tile_kernel(span, lon_ref, lat_ref, weight_ref, ext_ref, main_ref, twice_ref, once_ref):
    snaps = ext_ref.shape[1]
    total = span * GROUPS
    rows = total - 2 * HALO
    plain = rate_reader(rows, (lon_ref, lat_ref))
    weighted = rate_reader(rows, (lon_ref, lat_ref, weight_ref))
    ends = jnp.zeros((4, TILE, LANES), jnp.float32)
    once_ref[:4] = ends
    once_ref[total + 4 :] = ends
    outside = jnp.zeros((HALO, TILE, LANES), jnp.float32)

    def one_tile(tile, carry):
        snap = pl.ds(pl.multiple_of(tile * TILE, TILE), TILE)

        def one_pass(load, rates, store):
            center = load(slice(4, 4 + total)).reshape(total * TILE, LANES)
            part = zonal_terms(hi_lo(center), main_ref[...]).reshape(total, TILE, LANES)
            stencil_rows(load, 0, total, part, rates, store)

        def store_once(at, value):
            once_ref[4 + at] = value

        def store_twice(at, value):
            twice_ref[at, snap] = value

        one_pass(lambda at: ext_ref[at, snap], plain, store_once)

        @pl.when(lax.axis_index("lat") == 0)
        def _():
            once_ref[4 : 4 + HALO] = outside

        @pl.when(lax.axis_index("lat") == lax.axis_size("lat") - 1)
        def _():
            once_ref[4 + HALO + rows : 4 + total] = outside

        one_pass(lambda at: once_ref[at], weighted, store_twice)
        return carry

    lax.fori_loop(0, snaps // TILE, one_tile, 0)
    outside = jnp.zeros((HALO, snaps, LANES), jnp.float32)
    twice_ref[:HALO] = outside
    twice_ref[HALO + rows :] = outside


def close_ends(strip_ref, span):
    for at in range(4):
        strip_ref[at] = pltpu.roll(strip_ref[span + at], STRIP, 1)
        strip_ref[span + 4 + at] = pltpu.roll(strip_ref[4 + at], LANES - STRIP, 1)


def rim_kernel(
    span,
    twice_ref,
    strip_ref,
    strip_rates_ref,
    first_ref,
    second_ref,
    edge_ref,
    again_ref,
    split_ref,
    gram_ref,
    outer_ref,
    side_ref,
    added_ref,
    rim_ref,
):
    both = split_ref.shape[1]
    snaps = both // 2
    half = span // 2
    lon_even = lax.axis_index("lon") % 2 == 0
    lane = lax.broadcasted_iota(jnp.int32, (TILE, LANES), 1)
    left = lane % STRIP < HALO
    rim = (lane < HALO) | (lane >= LANES - HALO)
    def strip_rate(kind, at):
        return jnp.concatenate([strip_rates_ref[kind, at]] * (TILE // 8), axis=0)

    def strip_stencil(source_ref, at, zonal):
        pairs = [
            source_ref[4 + at + offset] + source_ref[4 + at - offset] for offset in range(1, 5)
        ]
        return stencil_row(
            source_ref[4 + at], pairs, zonal, strip_rate(0, at), strip_rate(1, at)
        )

    for tile in range(0, snaps, TILE):
        snap = slice(tile, tile + TILE)
        for at in range(half):
            first, second = first_ref[at, snap], second_ref[at, snap]
            west = jnp.where(lon_even, second, first)
            east = jnp.where(lon_even, first, second)
            outer_ref[4 + at] = jnp.where(left, west, east)
            outer_ref[4 + half + at] = jnp.where(
                left, pltpu.roll(west, LANES - HALO, 1), pltpu.roll(east, HALO, 1)
            )
        close_ends(outer_ref, span)
        hi, lo = hi_lo(outer_ref[4 : 4 + span].reshape(span * TILE, LANES))
        own_hi, own_lo = hi_lo(strip_ref[:, snap].reshape(span * TILE, LANES))
        product = jnp.dot(
            jnp.concatenate([hi, lo, own_hi, own_lo], axis=1),
            edge_ref[...],
            preferred_element_type=jnp.float32,
        ).reshape(span, TILE, 4 * LANES)
        for at in range(span):
            zonal = product[at, :, :LANES] + product[at, :, LANES : 2 * LANES]
            side_ref[at] = strip_stencil(outer_ref, at, zonal)
            added_ref[4 + at] = strip_rate(0, at) * (
                product[at, :, 2 * LANES : 3 * LANES] + product[at, :, 3 * LANES :]
            )
        close_ends(added_ref, span)
        hi, lo = hi_lo(side_ref[...].reshape(span * TILE, LANES))
        own_hi, own_lo = hi_lo(added_ref[4 : 4 + span].reshape(span * TILE, LANES))
        part = zonal_terms([hi, lo, own_hi, own_lo], again_ref[...]).reshape(span, TILE, LANES)
        for at in range(span):
            rim_ref[at, snap] = strip_rate(2, at) * strip_stencil(added_ref, at, part[at])

    def finish(group, grams):
        begin = group * span
        shift = LANES - HALO - STRIP * group
        for pair in range(0, span, 2):
            rows_done = []
            for at in (pair, pair + 1):
                terms = []
                for tile in range(0, snaps, TILE):
                    snap = slice(tile, tile + TILE)
                    moved = pltpu.roll(rim_ref[at, snap], shift, 1)
                    value = twice_ref[begin + at, snap] + jnp.where(rim, moved, 0.0)
                    terms.append(hi_lo(value))
                row = jnp.concatenate(
                    [term[0] for term in terms] + [term[1] for term in terms], axis=0
                )
                split_ref[begin + at] = row
                rows_done.append(row)
            two = jnp.concatenate(rows_done, axis=1)
            grams = grams + lax.dot_general(
                two, two, (((1,), (1,)), ((), ())), preferred_element_type=jnp.float32
            )
        return grams

    grams = lax.fori_loop(0, GROUPS, finish, jnp.zeros((both, both), jnp.float32))
    gram = (
        grams[:snaps, :snaps]
        + grams[snaps:, snaps:]
        + (grams[:snaps, snaps:] + grams[snaps:, :snaps])
    )
    gram_ref[...] = jnp.concatenate([gram[at : at + 8] for at in range(0, snaps, 8)], axis=1)


def basis_kernel(root_count, gram_ref, split_ref, basis_ref, factor_ref, left_ref):
    snaps = basis_ref.shape[0]

    @pl.when(pl.program_id(0) == 0)
    def _():
        row = lax.broadcasted_iota(jnp.int32, (snaps, 2 * snaps), 0)
        col = lax.broadcasted_iota(jnp.int32, (snaps, 2 * snaps), 1)
        packed = jnp.sum(gram_ref[...], axis=0)
        gram = jnp.concatenate(
            [packed[:, at : at + snaps] for at in range(0, packed.shape[1], snaps)], axis=0
        )
        work = jnp.concatenate([gram, jnp.zeros((snaps, snaps), jnp.float32)], axis=1)
        work = jnp.where(col == row + snaps, 1.0, work)
        for step in range(0, snaps, PIVOTS):
            below = [
                jnp.broadcast_to(work[:, pivot : pivot + 1], work.shape)
                for pivot in range(step, step + PIVOTS)
            ]
            across = [work[pivot : pivot + 1, :] for pivot in range(step, step + PIVOTS)]
            for at in range(PIVOTS):
                pivot = step + at
                ratio = 1.0 / below[at][pivot : pivot + 1, :]
                rest = jnp.where(row > pivot, below[at], 0.0)
                work = work - (rest * ratio) * across[at]
                for later in range(at + 1, PIVOTS):
                    factor = below[later][pivot : pivot + 1, :] * ratio
                    below[later] = below[later] - rest * factor
                    across[later] = across[later] - factor * across[at]
        diagonal = jnp.sum(jnp.where(row == col, work, 0.0), axis=1, keepdims=True)
        work = work * lax.rsqrt(diagonal)
        upper = jnp.where(col >= row, work, 0.0)
        factor_ref[...] = upper[:, :snaps] / root_count
        hi, lo = hi_lo(work[:, snaps:] * root_count)
        left_ref[:snaps] = jnp.concatenate([hi, hi], axis=1)
        left_ref[snaps:] = jnp.concatenate([lo, jnp.zeros_like(lo)], axis=1)

    left = left_ref[...]
    start = pl.program_id(0) * basis_ref.shape[1] + HALO

    def body(at, carry):
        begin = pl.multiple_of(at * 16, 16)
        values = []
        for pair in range(8):
            row = start + begin + 2 * pair
            two = jnp.concatenate([split_ref[row], split_ref[row + 1]], axis=1)
            product = jnp.dot(left, two, preferred_element_type=jnp.float32)
            value = product[:snaps] + product[snaps:]
            values += [value[:, :LANES], value[:, LANES:]]
        turned = jnp.swapaxes(jnp.stack(values, axis=0), 0, 1)
        basis_ref[:, pl.ds(begin, 16), :] = turned.astype(jnp.bfloat16)
        return carry

    lax.fori_loop(0, basis_ref.shape[1] // 16, body, 0, unroll=8)


def pair_permutes(values, axis, periodic):
    count = lax.axis_size(axis)
    inner = [(i, i ^ 1) for i in range(count)]
    outer = []
    for i in range(1, count, 2):
        if periodic or i + 1 < count:
            outer += [(i, (i + 1) % count), ((i + 1) % count, i)]
    return lax.ppermute(values[0], axis, inner), lax.ppermute(values[1], axis, outer)


def gather_all(values):
    axes = ("lat", "lon")
    count = lax.axis_size(axes)
    return lax.all_to_all(jnp.broadcast_to(values, (count,) + values.shape), axes, 0, 0)


def whole(memory_space=pltpu.VMEM):
    return pl.BlockSpec(memory_space=memory_space)


def shards(field, lon_rate, lat_rate):
    snaps, rows, cols = field.shape
    total_rows = rows * lax.axis_size("lat")
    total_cells = total_rows * cols * lax.axis_size("lon")
    span = (rows + 2 * HALO) // GROUPS
    f32 = jnp.float32
    limits = pltpu.CompilerParams(vmem_limit_bytes=VMEM_BYTES)

    total = span * GROUPS
    ext = jax.ShapeDtypeStruct((total + 8, snaps, cols), f32)
    strip = jax.ShapeDtypeStruct((span, snaps, cols), f32)
    half = jax.ShapeDtypeStruct((span // 2, snaps, cols), f32)
    edge_rows = jax.ShapeDtypeStruct((snaps, HALO, cols), f32)
    first, second = pl.pallas_call(
        edge_kernel,
        in_specs=[whole()],
        out_specs=[whole()] * 2,
        out_shape=[edge_rows, edge_rows],
        compiler_params=limits,
        name="lat_messages",
    )(field)
    low, high = pair_permutes([first, second], "lat", False)
    weight = area_weight(total_rows)
    turned, packed, strip_rates = pl.pallas_call(
        functools.partial(strip_kernel, span),
        in_specs=[whole(pltpu.SMEM)] * 3 + [whole()],
        out_specs=[whole()] * 3,
        out_shape=[ext, strip, jax.ShapeDtypeStruct((3, span, 8, cols), f32)],
        compiler_params=limits,
        name="turn_and_pack",
    )(lon_rate, lat_rate, weight, field)
    turned, packed, first, second = pl.pallas_call(
        functools.partial(message_kernel, span),
        in_specs=[whole()] * 4,
        out_specs=[whole()] * 4,
        out_shape=[ext, strip, half, half],
        input_output_aliases={0: 0},
        compiler_params=limits,
        name="lon_messages",
    )(turned, packed, low, high)
    first, second = pair_permutes([first, second], "lon", True)

    main, edge, again = zonal_matrices()
    bf16 = jnp.bfloat16
    twice = pl.pallas_call(
        functools.partial(tile_kernel, span),
        in_specs=[whole(pltpu.SMEM)] * 3 + [whole()] * 2,
        out_specs=whole(),
        out_shape=jax.ShapeDtypeStruct((total, snaps, cols), f32),
        scratch_shapes=[pltpu.VMEM((total + 8, TILE, cols), f32)],
        compiler_params=limits,
        cost_estimate=pl.CostEstimate(
            flops=100 * snaps * rows * cols, bytes_accessed=8 * snaps * rows * cols, transcendentals=0
        ),
        name="both_passes",
    )(lon_rate, lat_rate, weight, turned, main)
    split, gram = pl.pallas_call(
        functools.partial(rim_kernel, span),
        in_specs=[whole()] * 7,
        out_specs=[whole(), whole()],
        out_shape=[
            jax.ShapeDtypeStruct((total, 2 * snaps, cols), bf16),
            jax.ShapeDtypeStruct((8, snaps // 8 * snaps), f32),
        ],
        scratch_shapes=[
            pltpu.VMEM((span + 8, TILE, cols), f32),
            pltpu.VMEM((span, TILE, cols), f32),
            pltpu.VMEM((span + 8, TILE, cols), f32),
            pltpu.VMEM((span, snaps, cols), f32),
        ],
        compiler_params=limits,
        name="rim_and_gram",
    )(twice, packed, strip_rates, first, second, edge, again)

    grams = gather_all(gram)
    block = 128
    basis, factor = pl.pallas_call(
        functools.partial(basis_kernel, math.sqrt(total_cells)),
        grid=(rows // block,),
        in_specs=[
            whole(),
            whole(),
        ],
        out_specs=[
            pl.BlockSpec((snaps, block, cols), lambda i: (0, i, 0)),
            pl.BlockSpec((snaps, snaps), lambda i: (0, 0)),
        ],
        out_shape=[
            jax.ShapeDtypeStruct((snaps, rows, cols), bf16),
            jax.ShapeDtypeStruct((snaps, snaps), f32),
        ],
        scratch_shapes=[
            pltpu.VMEM((2 * snaps, 2 * snaps), bf16),
        ],
        compiler_params=limits,
        name="factor_and_basis",
    )(grams, split)
    return (basis, factor)


def solution(mesh):
    return jax.shard_map(
        shards,
        mesh=mesh,
        in_specs=(P(None, "lat", "lon"), P(), P()),
        out_specs=(P(None, "lat", "lon"), P()),
        check_vma=False,
    )
```

```python
import functools
import math

import jax
import jax.numpy as jnp
import numpy as np
from jax import lax
from jax.experimental import pallas as pl
from jax.experimental.pallas import tpu as pltpu
from jax.sharding import PartitionSpec as P

stencil_weights = (-205.0 / 72.0, 8.0 / 5.0, -1.0 / 5.0, 8.0 / 315.0, -1.0 / 560.0)

HALO = 8
STRIP = 2 * HALO
LANES = 128
GROUPS = LANES // STRIP
TILE = 16
PIVOTS = 16
VMEM_BYTES = 24 * 1024 * 1024


def area_weight(total_rows):
    row_index = np.arange(total_rows).astype(np.float32)
    step = np.float32(180.0 / total_rows)
    latitude = np.float32(-90.0) + (row_index + np.float32(0.5)) * step
    return np.sqrt(np.cos(latitude * np.float32(math.pi / 180.0))).astype(np.float32)


def hi_lo(values):
    hi = values.astype(jnp.bfloat16)
    lo = (values - hi.astype(jnp.float32)).astype(jnp.bfloat16)
    return hi, lo


def band(in_cols, out_cols):
    offset = np.abs(np.asarray(in_cols)[:, None] - np.asarray(out_cols)[None, :])
    table = np.asarray(stencil_weights, np.float32)
    return np.where(offset <= 4, table[np.minimum(offset, 4)], np.float32(0.0)).astype(np.float32)


def two_terms(matrix):
    hi = matrix.astype(jnp.bfloat16)
    lo = (matrix - hi.astype(np.float32)).astype(jnp.bfloat16)
    return np.concatenate([hi, lo], axis=1)


def block_diagonal(matrix):
    return np.kron(np.eye(GROUPS, dtype=np.float32), matrix)


def zonal_matrices():
    own = np.arange(LANES)
    outer = np.concatenate([np.arange(-HALO, 0), LANES + np.arange(HALO)])
    inner = np.concatenate([np.arange(LANES - HALO, LANES), np.arange(HALO)])
    main = two_terms(band(own, own))
    near = band(outer, outer)
    far = band(inner, outer)
    inward = band(outer, inner)
    near[:HALO, HALO:] = near[HALO:, :HALO] = 0.0
    within = band(inner, inner)
    within[:HALO, HALO:] = within[HALO:, :HALO] = 0.0
    near, far, inward, within = [
        two_terms(block_diagonal(part)) for part in (near, far, inward, within)
    ]
    edge = np.concatenate([near, near, far, far], axis=0)
    again = np.concatenate([inward, inward, within, within], axis=0)
    inward = np.concatenate([inward, inward], axis=0)
    inward_only = np.concatenate([inward, np.zeros_like(inward)], axis=0)
    return np.concatenate([main, main], axis=0), np.concatenate([edge, inward_only], axis=1), again


def edge_kernel(field_ref, first_ref, second_ref):
    rows = field_ref.shape[1]
    lat_even = lax.axis_index("lat") % 2 == 0
    north, south = field_ref[:, :HALO], field_ref[:, rows - HALO :]
    first_ref[...] = jnp.where(lat_even, south, north)
    second_ref[...] = jnp.where(lat_even, north, south)


def strip_kernel(span, field_ref, ext_ref, strip_ref):
    snaps, rows, _ = field_ref.shape

    def turn(at, carry):
        begin = pl.multiple_of(at * 8, 8)
        for tile in range(0, snaps, 8):
            ext_ref[pl.ds(4 + HALO + begin, 8), tile : tile + 8] = jnp.swapaxes(
                field_ref[tile : tile + 8, pl.ds(begin, 8), :], 0, 1
            )
        return carry

    lax.fori_loop(0, rows // 8, turn, 0, unroll=4)
    ends = jnp.zeros((4 + HALO, snaps, LANES), jnp.float32)
    ext_ref[: 4 + HALO] = ends
    ext_ref[4 + HALO + rows :] = ends
    group_of = lax.broadcasted_iota(jnp.int32, (snaps, LANES), 1) // STRIP

    def pack(at, carry):
        packed = jnp.zeros((snaps, LANES), jnp.float32)
        for group in range(GROUPS):
            values = ext_ref[4 + group * span + at]
            moved = pltpu.roll(values, (HALO + STRIP * group) % LANES, 1)
            packed = jnp.where(group_of == group, moved, packed)
        strip_ref[at] = packed
        return carry

    lax.fori_loop(0, span, pack, 0, unroll=span // 2)


def message_kernel(
    span, ext_in_ref, strip_ref, low_ref, high_ref, ext_ref, full_ref, first_ref, second_ref
):
    snaps = strip_ref.shape[1]
    half = span // 2
    end = ext_ref.shape[0] - 4 - HALO
    lane = lax.broadcasted_iota(jnp.int32, (snaps, LANES), 1)
    lat_even = lax.axis_index("lat") % 2 == 0
    lon_even = lax.axis_index("lon") % 2 == 0
    full_ref[...] = strip_ref[...]
    for tile in range(0, snaps, 8):
        first = jnp.swapaxes(low_ref[tile : tile + 8], 0, 1)
        second = jnp.swapaxes(high_ref[tile : tile + 8], 0, 1)
        ext_ref[4 : 4 + HALO, tile : tile + 8] = jnp.where(lat_even, second, first)
        ext_ref[end : end + HALO, tile : tile + 8] = jnp.where(lat_even, first, second)
    for at in range(HALO):
        north, south = ext_ref[4 + at], ext_ref[end + at]
        full_ref[at] = jnp.where(lane < STRIP, pltpu.roll(north, HALO, 1), full_ref[at])
        last = span - HALO + at
        full_ref[last] = jnp.where(
            lane >= LANES - STRIP, pltpu.roll(south, LANES - HALO, 1), full_ref[last]
        )
    left = lane % STRIP < HALO
    for at in range(half):
        upper, lower = full_ref[at], full_ref[at + half]
        eastward = jnp.where(left, upper, pltpu.roll(lower, HALO, 1))
        westward = jnp.where(left, pltpu.roll(lower, LANES - HALO, 1), upper)
        first_ref[at] = jnp.where(lon_even, eastward, westward)
        second_ref[at] = jnp.where(lon_even, westward, eastward)


def stencil_row(center, pairs, zonal, zonal_rate, merid_rate, weight=None):
    merid = stencil_weights[1] * pairs[0]
    for offset in range(2, 5):
        merid = merid + stencil_weights[offset] * pairs[offset - 1]
    scale = 1.0 + stencil_weights[0] * merid_rate
    if weight is not None:
        scale, merid_rate, zonal_rate = scale * weight, merid_rate * weight, zonal_rate * weight
    return scale * center + merid_rate * merid + zonal_rate * zonal


def zonal_terms(parts, weights):
    product = jnp.dot(
        jnp.concatenate(parts, axis=1), weights, preferred_element_type=jnp.float32
    )
    return product[:, :LANES] + product[:, LANES:]


def rate_reader(rows, rates_refs):
    last = rows * lax.axis_size("lat") - 1
    origin = lax.axis_index("lat") * rows - HALO

    def read(at):
        row = jnp.clip(origin + at, 0, last)
        return [ref[row] for ref in rates_refs]

    return read


def stencil_rows(load, begin, span, part, rates, store):
    loaded = {}

    def row(at):
        if at not in loaded:
            loaded[at] = load(begin + at)
        return loaded[at]

    for at in range(span):
        here = at + 4
        pairs = [row(here + offset) + row(here - offset) for offset in range(1, 5)]
        store(at, stencil_row(row(here), pairs, part[at], *rates(begin + at)))


def tile_kernel(
    span, lon_ref, lat_ref, weight_ref, ext_ref, main_ref, twice_ref, strip_rates_ref, once_ref
):
    snaps = ext_ref.shape[1]
    total = span * GROUPS
    rows = total - 2 * HALO
    plain = rate_reader(rows, (lon_ref, lat_ref))
    weighted = rate_reader(rows, (lon_ref, lat_ref, weight_ref))
    ends = jnp.zeros((4, TILE, LANES), jnp.float32)
    once_ref[:4] = ends
    once_ref[total + 4 :] = ends
    outside = jnp.zeros((HALO, TILE, LANES), jnp.float32)

    def one_tile(tile, carry):
        snap = pl.ds(pl.multiple_of(tile * TILE, TILE), TILE)

        def one_pass(load, rates, store):
            center = load(slice(4, 4 + total)).reshape(total * TILE, LANES)
            part = zonal_terms(hi_lo(center), main_ref[...]).reshape(total, TILE, LANES)
            stencil_rows(load, 0, total, part, rates, store)

        def store_once(at, value):
            once_ref[4 + at] = value

        def store_twice(at, value):
            twice_ref[at, snap] = value

        one_pass(lambda at: ext_ref[at, snap], plain, store_once)

        @pl.when(lax.axis_index("lat") == 0)
        def _():
            once_ref[4 : 4 + HALO] = outside

        @pl.when(lax.axis_index("lat") == lax.axis_size("lat") - 1)
        def _():
            once_ref[4 + HALO + rows : 4 + total] = outside

        one_pass(lambda at: once_ref[at], weighted, store_twice)
        return carry

    lax.fori_loop(0, snaps // TILE, one_tile, 0)
    outside = jnp.zeros((HALO, snaps, LANES), jnp.float32)
    twice_ref[:HALO] = outside
    twice_ref[HALO + rows :] = outside
    lane_group = lax.broadcasted_iota(jnp.int32, (8, LANES), 1) // STRIP
    for at in range(span):
        values_at = [jnp.zeros((8, LANES), jnp.float32)] * 3
        for group in range(GROUPS):
            here = lane_group == group
            row = group * span + at
            values = weighted(row)
            if row < HALO or row >= HALO + rows:
                values[2] = 0.0
            values_at = [jnp.where(here, value, old) for value, old in zip(values, values_at)]
        for kind in range(3):
            strip_rates_ref[kind, at] = values_at[kind]


def close_ends(strip_ref, span):
    for at in range(4):
        strip_ref[at] = pltpu.roll(strip_ref[span + at], STRIP, 1)
        strip_ref[span + 4 + at] = pltpu.roll(strip_ref[4 + at], LANES - STRIP, 1)


def rim_kernel(
    span,
    twice_ref,
    strip_ref,
    strip_rates_ref,
    first_ref,
    second_ref,
    edge_ref,
    again_ref,
    split_ref,
    gram_ref,
    outer_ref,
    side_ref,
    added_ref,
    rim_ref,
):
    both = split_ref.shape[1]
    snaps = both // 2
    half = span // 2
    lon_even = lax.axis_index("lon") % 2 == 0
    lane = lax.broadcasted_iota(jnp.int32, (TILE, LANES), 1)
    left = lane % STRIP < HALO
    rim = (lane < HALO) | (lane >= LANES - HALO)
    def strip_rate(kind, at):
        return jnp.concatenate([strip_rates_ref[kind, at]] * (TILE // 8), axis=0)

    def strip_stencil(source_ref, at, zonal):
        pairs = [
            source_ref[4 + at + offset] + source_ref[4 + at - offset] for offset in range(1, 5)
        ]
        return stencil_row(
            source_ref[4 + at], pairs, zonal, strip_rate(0, at), strip_rate(1, at)
        )

    for tile in range(0, snaps, TILE):
        snap = slice(tile, tile + TILE)
        for at in range(half):
            first, second = first_ref[at, snap], second_ref[at, snap]
            west = jnp.where(lon_even, second, first)
            east = jnp.where(lon_even, first, second)
            outer_ref[4 + at] = jnp.where(left, west, east)
            outer_ref[4 + half + at] = jnp.where(
                left, pltpu.roll(west, LANES - HALO, 1), pltpu.roll(east, HALO, 1)
            )
        close_ends(outer_ref, span)
        hi, lo = hi_lo(outer_ref[4 : 4 + span].reshape(span * TILE, LANES))
        own_hi, own_lo = hi_lo(strip_ref[:, snap].reshape(span * TILE, LANES))
        product = jnp.dot(
            jnp.concatenate([hi, lo, own_hi, own_lo], axis=1),
            edge_ref[...],
            preferred_element_type=jnp.float32,
        ).reshape(span, TILE, 4 * LANES)
        for at in range(span):
            zonal = product[at, :, :LANES] + product[at, :, LANES : 2 * LANES]
            side_ref[at] = strip_stencil(outer_ref, at, zonal)
            added_ref[4 + at] = strip_rate(0, at) * (
                product[at, :, 2 * LANES : 3 * LANES] + product[at, :, 3 * LANES :]
            )
        close_ends(added_ref, span)
        hi, lo = hi_lo(side_ref[...].reshape(span * TILE, LANES))
        own_hi, own_lo = hi_lo(added_ref[4 : 4 + span].reshape(span * TILE, LANES))
        part = zonal_terms([hi, lo, own_hi, own_lo], again_ref[...]).reshape(span, TILE, LANES)
        for at in range(span):
            rim_ref[at, snap] = strip_rate(2, at) * strip_stencil(added_ref, at, part[at])

    def finish(group, grams):
        begin = group * span
        shift = LANES - HALO - STRIP * group
        for pair in range(0, span, 2):
            rows_done = []
            for at in (pair, pair + 1):
                terms = []
                for tile in range(0, snaps, TILE):
                    snap = slice(tile, tile + TILE)
                    moved = pltpu.roll(rim_ref[at, snap], shift, 1)
                    value = twice_ref[begin + at, snap] + jnp.where(rim, moved, 0.0)
                    terms.append(hi_lo(value))
                row = jnp.concatenate(
                    [term[0] for term in terms] + [term[1] for term in terms], axis=0
                )
                split_ref[begin + at] = row
                rows_done.append(row)
            two = jnp.concatenate(rows_done, axis=1)
            grams = grams + lax.dot_general(
                two, two, (((1,), (1,)), ((), ())), preferred_element_type=jnp.float32
            )
        return grams

    grams = lax.fori_loop(0, GROUPS, finish, jnp.zeros((both, both), jnp.float32))
    gram = (
        grams[:snaps, :snaps]
        + grams[snaps:, snaps:]
        + (grams[:snaps, snaps:] + grams[snaps:, :snaps])
    )
    gram_ref[...] = jnp.concatenate([gram[at : at + 8] for at in range(0, snaps, 8)], axis=1)


def basis_kernel(root_count, gram_ref, split_ref, basis_ref, factor_ref, left_ref):
    snaps = basis_ref.shape[0]

    @pl.when(pl.program_id(0) == 0)
    def _():
        row = lax.broadcasted_iota(jnp.int32, (snaps, 2 * snaps), 0)
        col = lax.broadcasted_iota(jnp.int32, (snaps, 2 * snaps), 1)
        packed = jnp.sum(gram_ref[...], axis=0)
        gram = jnp.concatenate(
            [packed[:, at : at + snaps] for at in range(0, packed.shape[1], snaps)], axis=0
        )
        work = jnp.concatenate([gram, jnp.zeros((snaps, snaps), jnp.float32)], axis=1)
        work = jnp.where(col == row + snaps, 1.0, work)
        for step in range(0, snaps, PIVOTS):
            below = [
                jnp.broadcast_to(work[:, pivot : pivot + 1], work.shape)
                for pivot in range(step, step + PIVOTS)
            ]
            across = [work[pivot : pivot + 1, :] for pivot in range(step, step + PIVOTS)]
            for at in range(PIVOTS):
                pivot = step + at
                ratio = 1.0 / below[at][pivot : pivot + 1, :]
                rest = jnp.where(row > pivot, below[at], 0.0)
                work = work - (rest * ratio) * across[at]
                for later in range(at + 1, PIVOTS):
                    factor = below[later][pivot : pivot + 1, :] * ratio
                    below[later] = below[later] - rest * factor
                    across[later] = across[later] - factor * across[at]
        diagonal = jnp.sum(jnp.where(row == col, work, 0.0), axis=1, keepdims=True)
        work = work * lax.rsqrt(diagonal)
        upper = jnp.where(col >= row, work, 0.0)
        factor_ref[...] = upper[:, :snaps] / root_count
        hi, lo = hi_lo(work[:, snaps:] * root_count)
        left_ref[:snaps] = jnp.concatenate([hi, hi], axis=1)
        left_ref[snaps:] = jnp.concatenate([lo, jnp.zeros_like(lo)], axis=1)

    left = left_ref[...]
    start = pl.program_id(0) * basis_ref.shape[1] + HALO

    def body(at, carry):
        begin = pl.multiple_of(at * 16, 16)
        values = []
        for pair in range(8):
            row = start + begin + 2 * pair
            two = jnp.concatenate([split_ref[row], split_ref[row + 1]], axis=1)
            product = jnp.dot(left, two, preferred_element_type=jnp.float32)
            value = product[:snaps] + product[snaps:]
            values += [value[:, :LANES], value[:, LANES:]]
        turned = jnp.swapaxes(jnp.stack(values, axis=0), 0, 1)
        basis_ref[:, pl.ds(begin, 16), :] = turned.astype(jnp.bfloat16)
        return carry

    lax.fori_loop(0, basis_ref.shape[1] // 16, body, 0, unroll=8)


def pair_permutes(values, axis, periodic):
    count = lax.axis_size(axis)
    inner = [(i, i ^ 1) for i in range(count)]
    outer = []
    for i in range(1, count, 2):
        if periodic or i + 1 < count:
            outer += [(i, (i + 1) % count), ((i + 1) % count, i)]
    return lax.ppermute(values[0], axis, inner), lax.ppermute(values[1], axis, outer)


def gather_all(values):
    axes = ("lat", "lon")
    count = lax.axis_size(axes)
    return lax.all_to_all(jnp.broadcast_to(values, (count,) + values.shape), axes, 0, 0)


def whole(memory_space=pltpu.VMEM):
    return pl.BlockSpec(memory_space=memory_space)


def shards(field, lon_rate, lat_rate):
    snaps, rows, cols = field.shape
    total_rows = rows * lax.axis_size("lat")
    total_cells = total_rows * cols * lax.axis_size("lon")
    span = (rows + 2 * HALO) // GROUPS
    f32 = jnp.float32
    limits = pltpu.CompilerParams(vmem_limit_bytes=VMEM_BYTES)

    total = span * GROUPS
    ext = jax.ShapeDtypeStruct((total + 8, snaps, cols), f32)
    strip = jax.ShapeDtypeStruct((span, snaps, cols), f32)
    half = jax.ShapeDtypeStruct((span // 2, snaps, cols), f32)
    edge_rows = jax.ShapeDtypeStruct((snaps, HALO, cols), f32)
    first, second = pl.pallas_call(
        edge_kernel,
        in_specs=[whole()],
        out_specs=[whole()] * 2,
        out_shape=[edge_rows, edge_rows],
        compiler_params=limits,
        name="lat_messages",
    )(field)
    low, high = pair_permutes([first, second], "lat", False)
    weight = area_weight(total_rows)
    turned, packed = pl.pallas_call(
        functools.partial(strip_kernel, span),
        in_specs=[whole()],
        out_specs=[whole()] * 2,
        out_shape=[ext, strip],
        compiler_params=limits,
        name="turn_and_pack",
    )(field)
    turned, packed, first, second = pl.pallas_call(
        functools.partial(message_kernel, span),
        in_specs=[whole()] * 4,
        out_specs=[whole()] * 4,
        out_shape=[ext, strip, half, half],
        input_output_aliases={0: 0},
        compiler_params=limits,
        name="lon_messages",
    )(turned, packed, low, high)
    first, second = pair_permutes([first, second], "lon", True)

    main, edge, again = zonal_matrices()
    bf16 = jnp.bfloat16
    twice, strip_rates = pl.pallas_call(
        functools.partial(tile_kernel, span),
        in_specs=[whole(pltpu.SMEM)] * 3 + [whole()] * 2,
        out_specs=[whole()] * 2,
        out_shape=[
            jax.ShapeDtypeStruct((total, snaps, cols), f32),
            jax.ShapeDtypeStruct((3, span, 8, cols), f32),
        ],
        scratch_shapes=[pltpu.VMEM((total + 8, TILE, cols), f32)],
        compiler_params=limits,
        cost_estimate=pl.CostEstimate(
            flops=100 * snaps * rows * cols, bytes_accessed=8 * snaps * rows * cols, transcendentals=0
        ),
        name="both_passes",
    )(lon_rate, lat_rate, weight, turned, main)
    split, gram = pl.pallas_call(
        functools.partial(rim_kernel, span),
        in_specs=[whole()] * 7,
        out_specs=[whole(), whole()],
        out_shape=[
            jax.ShapeDtypeStruct((total, 2 * snaps, cols), bf16),
            jax.ShapeDtypeStruct((8, snaps // 8 * snaps), f32),
        ],
        scratch_shapes=[
            pltpu.VMEM((span + 8, TILE, cols), f32),
            pltpu.VMEM((span, TILE, cols), f32),
            pltpu.VMEM((span + 8, TILE, cols), f32),
            pltpu.VMEM((span, snaps, cols), f32),
        ],
        compiler_params=limits,
        name="rim_and_gram",
    )(twice, packed, strip_rates, first, second, edge, again)

    grams = gather_all(gram)
    block = 128
    basis, factor = pl.pallas_call(
        functools.partial(basis_kernel, math.sqrt(total_cells)),
        grid=(rows // block,),
        in_specs=[
            whole(),
            whole(),
        ],
        out_specs=[
            pl.BlockSpec((snaps, block, cols), lambda i: (0, i, 0)),
            pl.BlockSpec((snaps, snaps), lambda i: (0, 0)),
        ],
        out_shape=[
            jax.ShapeDtypeStruct((snaps, rows, cols), bf16),
            jax.ShapeDtypeStruct((snaps, snaps), f32),
        ],
        scratch_shapes=[
            pltpu.VMEM((2 * snaps, 2 * snaps), bf16),
        ],
        compiler_params=limits,
        name="factor_and_basis",
    )(grams, split)
    return (basis, factor)


def solution(mesh):
    return jax.shard_map(
        shards,
        mesh=mesh,
        in_specs=(P(None, "lat", "lon"), P(), P()),
        out_specs=(P(None, "lat", "lon"), P()),
        check_vma=False,
    )
```

```python
import functools
import math

import jax
import jax.numpy as jnp
import numpy as np
from jax import lax
from jax.experimental import pallas as pl
from jax.experimental.pallas import tpu as pltpu
from jax.sharding import PartitionSpec as P

stencil_weights = (-205.0 / 72.0, 8.0 / 5.0, -1.0 / 5.0, 8.0 / 315.0, -1.0 / 560.0)

HALO = 8
STRIP = 2 * HALO
LANES = 128
GROUPS = LANES // STRIP
TILE = 16
PIVOTS = 16
VMEM_BYTES = 24 * 1024 * 1024


def area_weight(total_rows):
    row_index = np.arange(total_rows).astype(np.float32)
    step = np.float32(180.0 / total_rows)
    latitude = np.float32(-90.0) + (row_index + np.float32(0.5)) * step
    return np.sqrt(np.cos(latitude * np.float32(math.pi / 180.0))).astype(np.float32)


def hi_lo(values):
    hi = values.astype(jnp.bfloat16)
    lo = (values - hi.astype(jnp.float32)).astype(jnp.bfloat16)
    return hi, lo


def band(in_cols, out_cols):
    offset = np.abs(np.asarray(in_cols)[:, None] - np.asarray(out_cols)[None, :])
    table = np.asarray(stencil_weights, np.float32)
    return np.where(offset <= 4, table[np.minimum(offset, 4)], np.float32(0.0)).astype(np.float32)


def two_terms(matrix):
    hi = matrix.astype(jnp.bfloat16)
    lo = (matrix - hi.astype(np.float32)).astype(jnp.bfloat16)
    return np.concatenate([hi, lo], axis=1)


def block_diagonal(matrix):
    return np.kron(np.eye(GROUPS, dtype=np.float32), matrix)


def zonal_matrices():
    own = np.arange(LANES)
    outer = np.concatenate([np.arange(-HALO, 0), LANES + np.arange(HALO)])
    inner = np.concatenate([np.arange(LANES - HALO, LANES), np.arange(HALO)])
    main = two_terms(band(own, own))
    near = band(outer, outer)
    far = band(inner, outer)
    inward = band(outer, inner)
    near[:HALO, HALO:] = near[HALO:, :HALO] = 0.0
    within = band(inner, inner)
    within[:HALO, HALO:] = within[HALO:, :HALO] = 0.0
    near, far, inward, within = [
        two_terms(block_diagonal(part)) for part in (near, far, inward, within)
    ]
    edge = np.concatenate([near, near, far, far], axis=0)
    again = np.concatenate([inward, inward, within, within], axis=0)
    inward = np.concatenate([inward, inward], axis=0)
    inward_only = np.concatenate([inward, np.zeros_like(inward)], axis=0)
    return np.concatenate([main, main], axis=0), np.concatenate([edge, inward_only], axis=1), again


def strip_kernel(span, field_ref, ext_ref, strip_ref):
    snaps, rows, _ = field_ref.shape

    def turn(at, carry):
        begin = pl.multiple_of(at * 8, 8)
        for tile in range(0, snaps, 8):
            ext_ref[pl.ds(4 + HALO + begin, 8), tile : tile + 8] = jnp.swapaxes(
                field_ref[tile : tile + 8, pl.ds(begin, 8), :], 0, 1
            )
        return carry

    lax.fori_loop(0, rows // 8, turn, 0, unroll=4)
    ends = jnp.zeros((4 + HALO, snaps, LANES), jnp.float32)
    ext_ref[: 4 + HALO] = ends
    ext_ref[4 + HALO + rows :] = ends
    group_of = lax.broadcasted_iota(jnp.int32, (snaps, LANES), 1) // STRIP

    def pack(at, carry):
        packed = jnp.zeros((snaps, LANES), jnp.float32)
        for group in range(GROUPS):
            values = ext_ref[4 + group * span + at]
            moved = pltpu.roll(values, (HALO + STRIP * group) % LANES, 1)
            packed = jnp.where(group_of == group, moved, packed)
        strip_ref[at] = packed
        return carry

    lax.fori_loop(0, span, pack, 0, unroll=span // 2)


def message_kernel(
    span, ext_in_ref, strip_ref, low_ref, high_ref, ext_ref, full_ref, first_ref, second_ref
):
    snaps = strip_ref.shape[1]
    half = span // 2
    end = ext_ref.shape[0] - 4 - HALO
    lane = lax.broadcasted_iota(jnp.int32, (snaps, LANES), 1)
    lat = lax.axis_index("lat")
    last_lat = lax.axis_size("lat") - 1
    lat_even = lat % 2 == 0
    lon_even = lax.axis_index("lon") % 2 == 0
    full_ref[...] = strip_ref[...]
    for tile in range(0, snaps, 8):
        first = jnp.swapaxes(low_ref[tile : tile + 8], 0, 1)
        second = jnp.swapaxes(high_ref[tile : tile + 8], 0, 1)
        north = jnp.where(lat_even, second, first)
        south = jnp.where(lat_even, first, second)
        ext_ref[4 : 4 + HALO, tile : tile + 8] = jnp.where(lat == 0, 0.0, north)
        ext_ref[end : end + HALO, tile : tile + 8] = jnp.where(lat == last_lat, 0.0, south)
    for at in range(HALO):
        north, south = ext_ref[4 + at], ext_ref[end + at]
        full_ref[at] = jnp.where(lane < STRIP, pltpu.roll(north, HALO, 1), full_ref[at])
        last = span - HALO + at
        full_ref[last] = jnp.where(
            lane >= LANES - STRIP, pltpu.roll(south, LANES - HALO, 1), full_ref[last]
        )
    left = lane % STRIP < HALO
    for at in range(half):
        upper, lower = full_ref[at], full_ref[at + half]
        eastward = jnp.where(left, upper, pltpu.roll(lower, HALO, 1))
        westward = jnp.where(left, pltpu.roll(lower, LANES - HALO, 1), upper)
        first_ref[at] = jnp.where(lon_even, eastward, westward)
        second_ref[at] = jnp.where(lon_even, westward, eastward)


def stencil_row(center, pairs, zonal, zonal_rate, merid_rate, weight=None):
    merid = stencil_weights[1] * pairs[0]
    for offset in range(2, 5):
        merid = merid + stencil_weights[offset] * pairs[offset - 1]
    scale = 1.0 + stencil_weights[0] * merid_rate
    if weight is not None:
        scale, merid_rate, zonal_rate = scale * weight, merid_rate * weight, zonal_rate * weight
    return scale * center + merid_rate * merid + zonal_rate * zonal


def zonal_terms(parts, weights):
    product = jnp.dot(
        jnp.concatenate(parts, axis=1), weights, preferred_element_type=jnp.float32
    )
    return product[:, :LANES] + product[:, LANES:]


def rate_reader(rows, rates_refs):
    last = rows * lax.axis_size("lat") - 1
    origin = lax.axis_index("lat") * rows - HALO

    def read(at):
        row = jnp.clip(origin + at, 0, last)
        return [ref[row] for ref in rates_refs]

    return read


def stencil_rows(load, begin, span, part, rates, store):
    loaded = {}

    def row(at):
        if at not in loaded:
            loaded[at] = load(begin + at)
        return loaded[at]

    for at in range(span):
        here = at + 4
        pairs = [row(here + offset) + row(here - offset) for offset in range(1, 5)]
        store(at, stencil_row(row(here), pairs, part[at], *rates(begin + at)))


def tile_kernel(
    span, lon_ref, lat_ref, weight_ref, ext_ref, main_ref, twice_ref, strip_rates_ref, once_ref
):
    snaps = ext_ref.shape[1]
    total = span * GROUPS
    rows = total - 2 * HALO
    plain = rate_reader(rows, (lon_ref, lat_ref))
    weighted = rate_reader(rows, (lon_ref, lat_ref, weight_ref))
    ends = jnp.zeros((4, TILE, LANES), jnp.float32)
    once_ref[:4] = ends
    once_ref[total + 4 :] = ends
    outside = jnp.zeros((HALO, TILE, LANES), jnp.float32)

    def one_tile(tile, carry):
        snap = pl.ds(pl.multiple_of(tile * TILE, TILE), TILE)

        def one_pass(load, rates, store):
            center = load(slice(4, 4 + total)).reshape(total * TILE, LANES)
            part = zonal_terms(hi_lo(center), main_ref[...]).reshape(total, TILE, LANES)
            stencil_rows(load, 0, total, part, rates, store)

        def store_once(at, value):
            once_ref[4 + at] = value

        def store_twice(at, value):
            twice_ref[at, snap] = value

        one_pass(lambda at: ext_ref[at, snap], plain, store_once)

        @pl.when(lax.axis_index("lat") == 0)
        def _():
            once_ref[4 : 4 + HALO] = outside

        @pl.when(lax.axis_index("lat") == lax.axis_size("lat") - 1)
        def _():
            once_ref[4 + HALO + rows : 4 + total] = outside

        one_pass(lambda at: once_ref[at], weighted, store_twice)
        return carry

    lax.fori_loop(0, snaps // TILE, one_tile, 0)
    outside = jnp.zeros((HALO, snaps, LANES), jnp.float32)
    twice_ref[:HALO] = outside
    twice_ref[HALO + rows :] = outside
    lane_group = lax.broadcasted_iota(jnp.int32, (8, LANES), 1) // STRIP
    for at in range(span):
        values_at = [jnp.zeros((8, LANES), jnp.float32)] * 3
        for group in range(GROUPS):
            here = lane_group == group
            row = group * span + at
            values = weighted(row)
            if row < HALO or row >= HALO + rows:
                values[2] = 0.0
            values_at = [jnp.where(here, value, old) for value, old in zip(values, values_at)]
        for kind in range(3):
            strip_rates_ref[kind, at] = values_at[kind]


def close_ends(strip_ref, span):
    for at in range(4):
        strip_ref[at] = pltpu.roll(strip_ref[span + at], STRIP, 1)
        strip_ref[span + 4 + at] = pltpu.roll(strip_ref[4 + at], LANES - STRIP, 1)


def rim_kernel(
    span,
    twice_ref,
    strip_ref,
    strip_rates_ref,
    first_ref,
    second_ref,
    edge_ref,
    again_ref,
    split_ref,
    gram_ref,
    outer_ref,
    side_ref,
    added_ref,
    rim_ref,
):
    both = split_ref.shape[1]
    snaps = both // 2
    half = span // 2
    lon_even = lax.axis_index("lon") % 2 == 0
    lane = lax.broadcasted_iota(jnp.int32, (TILE, LANES), 1)
    left = lane % STRIP < HALO
    rim = (lane < HALO) | (lane >= LANES - HALO)
    def strip_rate(kind, at):
        return jnp.concatenate([strip_rates_ref[kind, at]] * (TILE // 8), axis=0)

    def strip_stencil(source_ref, at, zonal):
        pairs = [
            source_ref[4 + at + offset] + source_ref[4 + at - offset] for offset in range(1, 5)
        ]
        return stencil_row(
            source_ref[4 + at], pairs, zonal, strip_rate(0, at), strip_rate(1, at)
        )

    for tile in range(0, snaps, TILE):
        snap = slice(tile, tile + TILE)
        for at in range(half):
            first, second = first_ref[at, snap], second_ref[at, snap]
            west = jnp.where(lon_even, second, first)
            east = jnp.where(lon_even, first, second)
            outer_ref[4 + at] = jnp.where(left, west, east)
            outer_ref[4 + half + at] = jnp.where(
                left, pltpu.roll(west, LANES - HALO, 1), pltpu.roll(east, HALO, 1)
            )
        close_ends(outer_ref, span)
        hi, lo = hi_lo(outer_ref[4 : 4 + span].reshape(span * TILE, LANES))
        own_hi, own_lo = hi_lo(strip_ref[:, snap].reshape(span * TILE, LANES))
        product = jnp.dot(
            jnp.concatenate([hi, lo, own_hi, own_lo], axis=1),
            edge_ref[...],
            preferred_element_type=jnp.float32,
        ).reshape(span, TILE, 4 * LANES)
        for at in range(span):
            zonal = product[at, :, :LANES] + product[at, :, LANES : 2 * LANES]
            side_ref[at] = strip_stencil(outer_ref, at, zonal)
            added_ref[4 + at] = strip_rate(0, at) * (
                product[at, :, 2 * LANES : 3 * LANES] + product[at, :, 3 * LANES :]
            )
        close_ends(added_ref, span)
        hi, lo = hi_lo(side_ref[...].reshape(span * TILE, LANES))
        own_hi, own_lo = hi_lo(added_ref[4 : 4 + span].reshape(span * TILE, LANES))
        part = zonal_terms([hi, lo, own_hi, own_lo], again_ref[...]).reshape(span, TILE, LANES)
        for at in range(span):
            rim_ref[at, snap] = strip_rate(2, at) * strip_stencil(added_ref, at, part[at])

    def finish(group, grams):
        begin = group * span
        shift = LANES - HALO - STRIP * group
        for pair in range(0, span, 2):
            rows_done = []
            for at in (pair, pair + 1):
                terms = []
                for tile in range(0, snaps, TILE):
                    snap = slice(tile, tile + TILE)
                    moved = pltpu.roll(rim_ref[at, snap], shift, 1)
                    value = twice_ref[begin + at, snap] + jnp.where(rim, moved, 0.0)
                    terms.append(hi_lo(value))
                row = jnp.concatenate(
                    [term[0] for term in terms] + [term[1] for term in terms], axis=0
                )
                split_ref[begin + at] = row
                rows_done.append(row)
            two = jnp.concatenate(rows_done, axis=1)
            grams = grams + lax.dot_general(
                two, two, (((1,), (1,)), ((), ())), preferred_element_type=jnp.float32
            )
        return grams

    grams = lax.fori_loop(0, GROUPS, finish, jnp.zeros((both, both), jnp.float32))
    gram = (
        grams[:snaps, :snaps]
        + grams[snaps:, snaps:]
        + (grams[:snaps, snaps:] + grams[snaps:, :snaps])
    )
    gram_ref[...] = jnp.concatenate([gram[at : at + 8] for at in range(0, snaps, 8)], axis=1)


def basis_kernel(root_count, gram_ref, split_ref, basis_ref, factor_ref, left_ref):
    snaps = basis_ref.shape[0]

    @pl.when(pl.program_id(0) == 0)
    def _():
        row = lax.broadcasted_iota(jnp.int32, (snaps, 2 * snaps), 0)
        col = lax.broadcasted_iota(jnp.int32, (snaps, 2 * snaps), 1)
        packed = jnp.sum(gram_ref[...], axis=0)
        gram = jnp.concatenate(
            [packed[:, at : at + snaps] for at in range(0, packed.shape[1], snaps)], axis=0
        )
        work = jnp.concatenate([gram, jnp.zeros((snaps, snaps), jnp.float32)], axis=1)
        work = jnp.where(col == row + snaps, 1.0, work)
        for step in range(0, snaps, PIVOTS):
            below = [
                jnp.broadcast_to(work[:, pivot : pivot + 1], work.shape)
                for pivot in range(step, step + PIVOTS)
            ]
            across = [work[pivot : pivot + 1, :] for pivot in range(step, step + PIVOTS)]
            for at in range(PIVOTS):
                pivot = step + at
                ratio = 1.0 / below[at][pivot : pivot + 1, :]
                rest = jnp.where(row > pivot, below[at], 0.0)
                work = work - (rest * ratio) * across[at]
                for later in range(at + 1, PIVOTS):
                    factor = below[later][pivot : pivot + 1, :] * ratio
                    below[later] = below[later] - rest * factor
                    across[later] = across[later] - factor * across[at]
        diagonal = jnp.sum(jnp.where(row == col, work, 0.0), axis=1, keepdims=True)
        work = work * lax.rsqrt(diagonal)
        upper = jnp.where(col >= row, work, 0.0)
        factor_ref[...] = upper[:, :snaps] / root_count
        hi, lo = hi_lo(work[:, snaps:] * root_count)
        left_ref[:snaps] = jnp.concatenate([hi, hi], axis=1)
        left_ref[snaps:] = jnp.concatenate([lo, jnp.zeros_like(lo)], axis=1)

    left = left_ref[...]
    start = pl.program_id(0) * basis_ref.shape[1] + HALO

    def body(at, carry):
        begin = pl.multiple_of(at * 16, 16)
        values = []
        for pair in range(8):
            row = start + begin + 2 * pair
            two = jnp.concatenate([split_ref[row], split_ref[row + 1]], axis=1)
            product = jnp.dot(left, two, preferred_element_type=jnp.float32)
            value = product[:snaps] + product[snaps:]
            values += [value[:, :LANES], value[:, LANES:]]
        turned = jnp.swapaxes(jnp.stack(values, axis=0), 0, 1)
        basis_ref[:, pl.ds(begin, 16), :] = turned.astype(jnp.bfloat16)
        return carry

    lax.fori_loop(0, basis_ref.shape[1] // 16, body, 0, unroll=8)


def pair_permutes(values, axis):
    count = lax.axis_size(axis)
    inner = [(i, i ^ 1) for i in range(count)]
    outer = [(i, (i + 1 if i % 2 else i - 1) % count) for i in range(count)]
    return lax.ppermute(values[0], axis, inner), lax.ppermute(values[1], axis, outer)


def gather_all(values):
    axes = ("lat", "lon")
    count = lax.axis_size(axes)
    return lax.all_to_all(jnp.broadcast_to(values, (count,) + values.shape), axes, 0, 0)


def whole(memory_space=pltpu.VMEM):
    return pl.BlockSpec(memory_space=memory_space)


def shards(field, lon_rate, lat_rate):
    snaps, rows, cols = field.shape
    total_rows = rows * lax.axis_size("lat")
    total_cells = total_rows * cols * lax.axis_size("lon")
    span = (rows + 2 * HALO) // GROUPS
    f32 = jnp.float32
    limits = pltpu.CompilerParams(vmem_limit_bytes=VMEM_BYTES)

    total = span * GROUPS
    ext = jax.ShapeDtypeStruct((total + 8, snaps, cols), f32)
    strip = jax.ShapeDtypeStruct((span, snaps, cols), f32)
    half = jax.ShapeDtypeStruct((span // 2, snaps, cols), f32)
    weight = area_weight(total_rows)
    begin = jnp.where(lax.axis_index("lat") % 2 == 0, rows - HALO, 0)
    low, high = pair_permutes(
        [
            lax.dynamic_slice_in_dim(field, start, HALO, axis=1)
            for start in (begin, rows - HALO - begin)
        ],
        "lat",
    )
    turned, packed = pl.pallas_call(
        functools.partial(strip_kernel, span),
        in_specs=[whole()],
        out_specs=[whole()] * 2,
        out_shape=[ext, strip],
        compiler_params=limits,
        name="turn_and_pack",
    )(field)
    turned, packed, first, second = pl.pallas_call(
        functools.partial(message_kernel, span),
        in_specs=[whole()] * 4,
        out_specs=[whole()] * 4,
        out_shape=[ext, strip, half, half],
        input_output_aliases={0: 0},
        compiler_params=limits,
        name="lon_messages",
    )(turned, packed, low, high)
    first, second = pair_permutes([first, second], "lon")

    main, edge, again = zonal_matrices()
    bf16 = jnp.bfloat16
    twice, strip_rates = pl.pallas_call(
        functools.partial(tile_kernel, span),
        in_specs=[whole(pltpu.SMEM)] * 3 + [whole()] * 2,
        out_specs=[whole()] * 2,
        out_shape=[
            jax.ShapeDtypeStruct((total, snaps, cols), f32),
            jax.ShapeDtypeStruct((3, span, 8, cols), f32),
        ],
        scratch_shapes=[pltpu.VMEM((total + 8, TILE, cols), f32)],
        compiler_params=limits,
        cost_estimate=pl.CostEstimate(
            flops=100 * snaps * rows * cols, bytes_accessed=8 * snaps * rows * cols, transcendentals=0
        ),
        name="both_passes",
    )(lon_rate, lat_rate, weight, turned, main)
    split, gram = pl.pallas_call(
        functools.partial(rim_kernel, span),
        in_specs=[whole()] * 7,
        out_specs=[whole(), whole()],
        out_shape=[
            jax.ShapeDtypeStruct((total, 2 * snaps, cols), bf16),
            jax.ShapeDtypeStruct((8, snaps // 8 * snaps), f32),
        ],
        scratch_shapes=[
            pltpu.VMEM((span + 8, TILE, cols), f32),
            pltpu.VMEM((span, TILE, cols), f32),
            pltpu.VMEM((span + 8, TILE, cols), f32),
            pltpu.VMEM((span, snaps, cols), f32),
        ],
        compiler_params=limits,
        name="rim_and_gram",
    )(twice, packed, strip_rates, first, second, edge, again)

    grams = gather_all(gram)
    block = 128
    basis, factor = pl.pallas_call(
        functools.partial(basis_kernel, math.sqrt(total_cells)),
        grid=(rows // block,),
        in_specs=[
            whole(),
            whole(),
        ],
        out_specs=[
            pl.BlockSpec((snaps, block, cols), lambda i: (0, i, 0)),
            pl.BlockSpec((snaps, snaps), lambda i: (0, 0)),
        ],
        out_shape=[
            jax.ShapeDtypeStruct((snaps, rows, cols), bf16),
            jax.ShapeDtypeStruct((snaps, snaps), f32),
        ],
        scratch_shapes=[
            pltpu.VMEM((2 * snaps, 2 * snaps), bf16),
        ],
        compiler_params=limits,
        name="factor_and_basis",
    )(grams, split)
    return (basis, factor)


def solution(mesh):
    return jax.shard_map(
        shards,
        mesh=mesh,
        in_specs=(P(None, "lat", "lon"), P(), P()),
        out_specs=(P(None, "lat", "lon"), P()),
        check_vma=False,
    )
```

```python
import functools
import math

import jax
import jax.numpy as jnp
import numpy as np
from jax import lax
from jax.experimental import pallas as pl
from jax.experimental.pallas import tpu as pltpu
from jax.sharding import PartitionSpec as P

stencil_weights = (-205.0 / 72.0, 8.0 / 5.0, -1.0 / 5.0, 8.0 / 315.0, -1.0 / 560.0)

HALO = 8
STRIP = 2 * HALO
LANES = 128
GROUPS = LANES // STRIP
TILE = 16
PIVOTS = 16
VMEM_BYTES = 24 * 1024 * 1024


def area_weight(total_rows):
    row_index = np.arange(total_rows).astype(np.float32)
    step = np.float32(180.0 / total_rows)
    latitude = np.float32(-90.0) + (row_index + np.float32(0.5)) * step
    return np.sqrt(np.cos(latitude * np.float32(math.pi / 180.0))).astype(np.float32)


def hi_lo(values):
    hi = values.astype(jnp.bfloat16)
    lo = (values - hi.astype(jnp.float32)).astype(jnp.bfloat16)
    return hi, lo


def band(in_cols, out_cols):
    offset = np.abs(np.asarray(in_cols)[:, None] - np.asarray(out_cols)[None, :])
    table = np.asarray(stencil_weights, np.float32)
    return np.where(offset <= 4, table[np.minimum(offset, 4)], np.float32(0.0)).astype(np.float32)


def two_terms(matrix):
    hi = matrix.astype(jnp.bfloat16)
    lo = (matrix - hi.astype(np.float32)).astype(jnp.bfloat16)
    return np.concatenate([hi, lo], axis=1)


def block_diagonal(matrix):
    return np.kron(np.eye(GROUPS, dtype=np.float32), matrix)


def zonal_matrices():
    own = np.arange(LANES)
    outer = np.concatenate([np.arange(-HALO, 0), LANES + np.arange(HALO)])
    inner = np.concatenate([np.arange(LANES - HALO, LANES), np.arange(HALO)])
    main = two_terms(band(own, own))
    near = band(outer, outer)
    far = band(inner, outer)
    inward = band(outer, inner)
    near[:HALO, HALO:] = near[HALO:, :HALO] = 0.0
    within = band(inner, inner)
    within[:HALO, HALO:] = within[HALO:, :HALO] = 0.0
    near, far, inward, within = [
        two_terms(block_diagonal(part)) for part in (near, far, inward, within)
    ]
    edge = np.concatenate([near, near, far, far], axis=0)
    again = np.concatenate([inward, inward, within, within], axis=0)
    inward = np.concatenate([inward, inward], axis=0)
    inward_only = np.concatenate([inward, np.zeros_like(inward)], axis=0)
    return np.concatenate([main, main], axis=0), np.concatenate([edge, inward_only], axis=1), again


def strip_kernel(span, field_ref, ext_ref, strip_ref):
    snaps, rows, _ = field_ref.shape

    def turn(at, carry):
        begin = pl.multiple_of(at * 8, 8)
        for tile in range(0, snaps, 8):
            ext_ref[pl.ds(4 + HALO + begin, 8), tile : tile + 8] = jnp.swapaxes(
                field_ref[tile : tile + 8, pl.ds(begin, 8), :], 0, 1
            )
        return carry

    lax.fori_loop(0, rows // 8, turn, 0, unroll=4)
    ends = jnp.zeros((4 + HALO, snaps, LANES), jnp.float32)
    ext_ref[: 4 + HALO] = ends
    ext_ref[4 + HALO + rows :] = ends
    group_of = lax.broadcasted_iota(jnp.int32, (snaps, LANES), 1) // STRIP

    def pack(at, carry):
        packed = jnp.zeros((snaps, LANES), jnp.float32)
        for group in range(GROUPS):
            values = ext_ref[4 + group * span + at]
            moved = pltpu.roll(values, (HALO + STRIP * group) % LANES, 1)
            packed = jnp.where(group_of == group, moved, packed)
        strip_ref[at] = packed
        return carry

    lax.fori_loop(0, span, pack, 0, unroll=span // 2)


def message_kernel(
    span, ext_in_ref, strip_ref, low_ref, high_ref, ext_ref, full_ref, first_ref, second_ref
):
    snaps = strip_ref.shape[1]
    half = span // 2
    end = ext_ref.shape[0] - 4 - HALO
    lane = lax.broadcasted_iota(jnp.int32, (snaps, LANES), 1)
    lat = lax.axis_index("lat")
    last_lat = lax.axis_size("lat") - 1
    lat_even = lat % 2 == 0
    lon_even = lax.axis_index("lon") % 2 == 0
    full_ref[...] = strip_ref[...]
    for tile in range(0, snaps, 8):
        first = jnp.swapaxes(low_ref[tile : tile + 8], 0, 1)
        second = jnp.swapaxes(high_ref[tile : tile + 8], 0, 1)
        north = jnp.where(lat_even, second, first)
        south = jnp.where(lat_even, first, second)
        ext_ref[4 : 4 + HALO, tile : tile + 8] = jnp.where(lat == 0, 0.0, north)
        ext_ref[end : end + HALO, tile : tile + 8] = jnp.where(lat == last_lat, 0.0, south)
    for at in range(HALO):
        north, south = ext_ref[4 + at], ext_ref[end + at]
        full_ref[at] = jnp.where(lane < STRIP, pltpu.roll(north, HALO, 1), full_ref[at])
        last = span - HALO + at
        full_ref[last] = jnp.where(
            lane >= LANES - STRIP, pltpu.roll(south, LANES - HALO, 1), full_ref[last]
        )
    left = lane % STRIP < HALO
    for at in range(half):
        upper, lower = full_ref[at], full_ref[at + half]
        eastward = jnp.where(left, upper, pltpu.roll(lower, HALO, 1))
        westward = jnp.where(left, pltpu.roll(lower, LANES - HALO, 1), upper)
        first_ref[at] = jnp.where(lon_even, eastward, westward)
        second_ref[at] = jnp.where(lon_even, westward, eastward)


def stencil_row(center, pairs, zonal, zonal_rate, merid_rate, weight=None):
    merid = stencil_weights[1] * pairs[0]
    for offset in range(2, 5):
        merid = merid + stencil_weights[offset] * pairs[offset - 1]
    scale = 1.0 + stencil_weights[0] * merid_rate
    if weight is not None:
        scale, merid_rate, zonal_rate = scale * weight, merid_rate * weight, zonal_rate * weight
    return scale * center + merid_rate * merid + zonal_rate * zonal


def zonal_terms(parts, weights):
    product = jnp.dot(
        jnp.concatenate(parts, axis=1), weights, preferred_element_type=jnp.float32
    )
    return product[:, :LANES] + product[:, LANES:]


def rate_reader(rows, rates_refs):
    last = rows * lax.axis_size("lat") - 1
    origin = lax.axis_index("lat") * rows - HALO

    def read(at):
        row = jnp.clip(origin + at, 0, last)
        return [ref[row] for ref in rates_refs]

    return read


def stencil_rows(load, begin, span, part, rates, store):
    loaded = {}

    def row(at):
        if at not in loaded:
            loaded[at] = load(begin + at)
        return loaded[at]

    for at in range(span):
        here = at + 4
        pairs = [row(here + offset) + row(here - offset) for offset in range(1, 5)]
        store(at, stencil_row(row(here), pairs, part[at], *rates(begin + at)))


def tile_kernel(
    span, lon_ref, lat_ref, weight_ref, ext_ref, main_ref, twice_ref, strip_rates_ref, once_ref
):
    snaps = ext_ref.shape[1]
    total = span * GROUPS
    rows = total - 2 * HALO
    plain = rate_reader(rows, (lon_ref, lat_ref))
    weighted = rate_reader(rows, (lon_ref, lat_ref, weight_ref))
    ends = jnp.zeros((4, TILE, LANES), jnp.float32)
    once_ref[:4] = ends
    once_ref[total + 4 :] = ends
    outside = jnp.zeros((HALO, TILE, LANES), jnp.float32)

    def one_tile(tile, carry):
        snap = pl.ds(pl.multiple_of(tile * TILE, TILE), TILE)

        def one_pass(load, rates, store):
            center = load(slice(4, 4 + total)).reshape(total * TILE, LANES)
            part = zonal_terms(hi_lo(center), main_ref[...]).reshape(total, TILE, LANES)
            stencil_rows(load, 0, total, part, rates, store)

        def store_once(at, value):
            once_ref[4 + at] = value

        def store_twice(at, value):
            twice_ref[at, snap] = value

        one_pass(lambda at: ext_ref[at, snap], plain, store_once)

        @pl.when(lax.axis_index("lat") == 0)
        def _():
            once_ref[4 : 4 + HALO] = outside

        @pl.when(lax.axis_index("lat") == lax.axis_size("lat") - 1)
        def _():
            once_ref[4 + HALO + rows : 4 + total] = outside

        one_pass(lambda at: once_ref[at], weighted, store_twice)
        return carry

    lax.fori_loop(0, snaps // TILE, one_tile, 0)
    outside = jnp.zeros((HALO, snaps, LANES), jnp.float32)
    twice_ref[:HALO] = outside
    twice_ref[HALO + rows :] = outside
    lane_group = lax.broadcasted_iota(jnp.int32, (8, LANES), 1) // STRIP
    for at in range(span):
        values_at = [jnp.zeros((8, LANES), jnp.float32)] * 3
        for group in range(GROUPS):
            here = lane_group == group
            row = group * span + at
            values = weighted(row)
            if row < HALO or row >= HALO + rows:
                values[2] = 0.0
            values_at = [jnp.where(here, value, old) for value, old in zip(values, values_at)]
        for kind in range(3):
            strip_rates_ref[kind, at] = values_at[kind]


def close_ends(strip_ref, span):
    for at in range(4):
        strip_ref[at] = pltpu.roll(strip_ref[span + at], STRIP, 1)
        strip_ref[span + 4 + at] = pltpu.roll(strip_ref[4 + at], LANES - STRIP, 1)


def rim_kernel(
    span,
    twice_ref,
    strip_ref,
    strip_rates_ref,
    first_ref,
    second_ref,
    edge_ref,
    again_ref,
    split_ref,
    gram_ref,
    outer_ref,
    side_ref,
    added_ref,
    rim_ref,
):
    both = split_ref.shape[1]
    snaps = both // 2
    half = span // 2
    lon_even = lax.axis_index("lon") % 2 == 0
    lane = lax.broadcasted_iota(jnp.int32, (TILE, LANES), 1)
    left = lane % STRIP < HALO
    rim = (lane < HALO) | (lane >= LANES - HALO)
    def strip_rate(kind, at):
        return jnp.concatenate([strip_rates_ref[kind, at]] * (TILE // 8), axis=0)

    def strip_stencil(source_ref, at, zonal):
        pairs = [
            source_ref[4 + at + offset] + source_ref[4 + at - offset] for offset in range(1, 5)
        ]
        return stencil_row(
            source_ref[4 + at], pairs, zonal, strip_rate(0, at), strip_rate(1, at)
        )

    for tile in range(0, snaps, TILE):
        snap = slice(tile, tile + TILE)
        for at in range(half):
            first, second = first_ref[at, snap], second_ref[at, snap]
            west = jnp.where(lon_even, second, first)
            east = jnp.where(lon_even, first, second)
            outer_ref[4 + at] = jnp.where(left, west, east)
            outer_ref[4 + half + at] = jnp.where(
                left, pltpu.roll(west, LANES - HALO, 1), pltpu.roll(east, HALO, 1)
            )
        close_ends(outer_ref, span)
        hi, lo = hi_lo(outer_ref[4 : 4 + span].reshape(span * TILE, LANES))
        own_hi, own_lo = hi_lo(strip_ref[:, snap].reshape(span * TILE, LANES))
        product = jnp.dot(
            jnp.concatenate([hi, lo, own_hi, own_lo], axis=1),
            edge_ref[...],
            preferred_element_type=jnp.float32,
        ).reshape(span, TILE, 4 * LANES)
        for at in range(span):
            zonal = product[at, :, :LANES] + product[at, :, LANES : 2 * LANES]
            side_ref[at] = strip_stencil(outer_ref, at, zonal)
            added_ref[4 + at] = strip_rate(0, at) * (
                product[at, :, 2 * LANES : 3 * LANES] + product[at, :, 3 * LANES :]
            )
        close_ends(added_ref, span)
        hi, lo = hi_lo(side_ref[...].reshape(span * TILE, LANES))
        own_hi, own_lo = hi_lo(added_ref[4 : 4 + span].reshape(span * TILE, LANES))
        part = zonal_terms([hi, lo, own_hi, own_lo], again_ref[...]).reshape(span, TILE, LANES)
        for at in range(span):
            rim_ref[at, snap] = strip_rate(2, at) * strip_stencil(added_ref, at, part[at])

    def finish(group, grams):
        begin = group * span
        shift = LANES - HALO - STRIP * group
        for pair in range(0, span, 2):
            rows_done = []
            for at in (pair, pair + 1):
                terms = []
                for tile in range(0, snaps, TILE):
                    snap = slice(tile, tile + TILE)
                    moved = pltpu.roll(rim_ref[at, snap], shift, 1)
                    value = twice_ref[begin + at, snap] + jnp.where(rim, moved, 0.0)
                    terms.append(hi_lo(value))
                row = jnp.concatenate(
                    [term[0] for term in terms] + [term[1] for term in terms], axis=0
                )
                split_ref[begin + at] = row
                rows_done.append(row)
            two = jnp.concatenate(rows_done, axis=1)
            grams = grams + lax.dot_general(
                two, two, (((1,), (1,)), ((), ())), preferred_element_type=jnp.float32
            )
        return grams

    grams = lax.fori_loop(0, GROUPS, finish, jnp.zeros((both, both), jnp.float32), unroll=4)
    gram = (
        grams[:snaps, :snaps]
        + grams[snaps:, snaps:]
        + (grams[:snaps, snaps:] + grams[snaps:, :snaps])
    )
    gram_ref[...] = jnp.concatenate([gram[at : at + 8] for at in range(0, snaps, 8)], axis=1)


def basis_kernel(root_count, gram_ref, split_ref, basis_ref, factor_ref, left_ref):
    snaps = basis_ref.shape[0]

    @pl.when(pl.program_id(0) == 0)
    def _():
        row = lax.broadcasted_iota(jnp.int32, (snaps, 2 * snaps), 0)
        col = lax.broadcasted_iota(jnp.int32, (snaps, 2 * snaps), 1)
        packed = jnp.sum(gram_ref[...], axis=0)
        gram = jnp.concatenate(
            [packed[:, at : at + snaps] for at in range(0, packed.shape[1], snaps)], axis=0
        )
        work = jnp.concatenate([gram, jnp.zeros((snaps, snaps), jnp.float32)], axis=1)
        work = jnp.where(col == row + snaps, 1.0, work)
        for step in range(0, snaps, PIVOTS):
            below = [
                jnp.broadcast_to(work[:, pivot : pivot + 1], work.shape)
                for pivot in range(step, step + PIVOTS)
            ]
            across = [work[pivot : pivot + 1, :] for pivot in range(step, step + PIVOTS)]
            for at in range(PIVOTS):
                pivot = step + at
                ratio = 1.0 / below[at][pivot : pivot + 1, :]
                rest = jnp.where(row > pivot, below[at], 0.0)
                work = work - (rest * ratio) * across[at]
                for later in range(at + 1, PIVOTS):
                    factor = below[later][pivot : pivot + 1, :] * ratio
                    below[later] = below[later] - rest * factor
                    across[later] = across[later] - factor * across[at]
        diagonal = jnp.sum(jnp.where(row == col, work, 0.0), axis=1, keepdims=True)
        work = work * lax.rsqrt(diagonal)
        upper = jnp.where(col >= row, work, 0.0)
        factor_ref[...] = upper[:, :snaps] / root_count
        hi, lo = hi_lo(work[:, snaps:] * root_count)
        left_ref[:snaps] = jnp.concatenate([hi, hi], axis=1)
        left_ref[snaps:] = jnp.concatenate([lo, jnp.zeros_like(lo)], axis=1)

    left = left_ref[...]
    start = pl.program_id(0) * basis_ref.shape[1] + HALO

    def body(at, carry):
        begin = pl.multiple_of(at * 16, 16)
        values = []
        for pair in range(8):
            row = start + begin + 2 * pair
            two = jnp.concatenate([split_ref[row], split_ref[row + 1]], axis=1)
            product = jnp.dot(left, two, preferred_element_type=jnp.float32)
            value = product[:snaps] + product[snaps:]
            values += [value[:, :LANES], value[:, LANES:]]
        turned = jnp.swapaxes(jnp.stack(values, axis=0), 0, 1)
        basis_ref[:, pl.ds(begin, 16), :] = turned.astype(jnp.bfloat16)
        return carry

    lax.fori_loop(0, basis_ref.shape[1] // 16, body, 0, unroll=8)


def pair_permutes(values, axis):
    count = lax.axis_size(axis)
    inner = [(i, i ^ 1) for i in range(count)]
    outer = [(i, (i + 1 if i % 2 else i - 1) % count) for i in range(count)]
    return lax.ppermute(values[0], axis, inner), lax.ppermute(values[1], axis, outer)


def gather_all(values):
    axes = ("lat", "lon")
    count = lax.axis_size(axes)
    return lax.all_to_all(jnp.broadcast_to(values, (count,) + values.shape), axes, 0, 0)


def whole(memory_space=pltpu.VMEM):
    return pl.BlockSpec(memory_space=memory_space)


def shards(field, lon_rate, lat_rate):
    snaps, rows, cols = field.shape
    total_rows = rows * lax.axis_size("lat")
    total_cells = total_rows * cols * lax.axis_size("lon")
    span = (rows + 2 * HALO) // GROUPS
    f32 = jnp.float32
    limits = pltpu.CompilerParams(vmem_limit_bytes=VMEM_BYTES)

    total = span * GROUPS
    ext = jax.ShapeDtypeStruct((total + 8, snaps, cols), f32)
    strip = jax.ShapeDtypeStruct((span, snaps, cols), f32)
    half = jax.ShapeDtypeStruct((span // 2, snaps, cols), f32)
    weight = area_weight(total_rows)
    begin = jnp.where(lax.axis_index("lat") % 2 == 0, rows - HALO, 0)
    low, high = pair_permutes(
        [
            lax.dynamic_slice_in_dim(field, start, HALO, axis=1)
            for start in (begin, rows - HALO - begin)
        ],
        "lat",
    )
    turned, packed = pl.pallas_call(
        functools.partial(strip_kernel, span),
        in_specs=[whole()],
        out_specs=[whole()] * 2,
        out_shape=[ext, strip],
        compiler_params=limits,
        name="turn_and_pack",
    )(field)
    turned, packed, first, second = pl.pallas_call(
        functools.partial(message_kernel, span),
        in_specs=[whole()] * 4,
        out_specs=[whole()] * 4,
        out_shape=[ext, strip, half, half],
        input_output_aliases={0: 0},
        compiler_params=limits,
        name="lon_messages",
    )(turned, packed, low, high)
    first, second = pair_permutes([first, second], "lon")

    main, edge, again = zonal_matrices()
    bf16 = jnp.bfloat16
    twice, strip_rates = pl.pallas_call(
        functools.partial(tile_kernel, span),
        in_specs=[whole(pltpu.SMEM)] * 3 + [whole()] * 2,
        out_specs=[whole()] * 2,
        out_shape=[
            jax.ShapeDtypeStruct((total, snaps, cols), f32),
            jax.ShapeDtypeStruct((3, span, 8, cols), f32),
        ],
        scratch_shapes=[pltpu.VMEM((total + 8, TILE, cols), f32)],
        compiler_params=limits,
        cost_estimate=pl.CostEstimate(
            flops=100 * snaps * rows * cols, bytes_accessed=8 * snaps * rows * cols, transcendentals=0
        ),
        name="both_passes",
    )(lon_rate, lat_rate, weight, turned, main)
    split, gram = pl.pallas_call(
        functools.partial(rim_kernel, span),
        in_specs=[whole()] * 7,
        out_specs=[whole(), whole()],
        out_shape=[
            jax.ShapeDtypeStruct((total, 2 * snaps, cols), bf16),
            jax.ShapeDtypeStruct((8, snaps // 8 * snaps), f32),
        ],
        scratch_shapes=[
            pltpu.VMEM((span + 8, TILE, cols), f32),
            pltpu.VMEM((span, TILE, cols), f32),
            pltpu.VMEM((span + 8, TILE, cols), f32),
            pltpu.VMEM((span, snaps, cols), f32),
        ],
        compiler_params=limits,
        name="rim_and_gram",
    )(twice, packed, strip_rates, first, second, edge, again)

    grams = gather_all(gram)
    block = 128
    basis, factor = pl.pallas_call(
        functools.partial(basis_kernel, math.sqrt(total_cells)),
        grid=(rows // block,),
        in_specs=[
            whole(),
            whole(),
        ],
        out_specs=[
            pl.BlockSpec((snaps, block, cols), lambda i: (0, i, 0)),
            pl.BlockSpec((snaps, snaps), lambda i: (0, 0)),
        ],
        out_shape=[
            jax.ShapeDtypeStruct((snaps, rows, cols), bf16),
            jax.ShapeDtypeStruct((snaps, snaps), f32),
        ],
        scratch_shapes=[
            pltpu.VMEM((2 * snaps, 2 * snaps), bf16),
        ],
        compiler_params=limits,
        name="factor_and_basis",
    )(grams, split)
    return (basis, factor)


def solution(mesh):
    return jax.shard_map(
        shards,
        mesh=mesh,
        in_specs=(P(None, "lat", "lon"), P(), P()),
        out_specs=(P(None, "lat", "lon"), P()),
        check_vma=False,
    )
```

```python
import functools
import math

import jax
import jax.numpy as jnp
import numpy as np
from jax import lax
from jax.experimental import pallas as pl
from jax.experimental.pallas import tpu as pltpu
from jax.sharding import PartitionSpec as P

stencil_weights = (-205.0 / 72.0, 8.0 / 5.0, -1.0 / 5.0, 8.0 / 315.0, -1.0 / 560.0)

HALO = 8
STRIP = 2 * HALO
LANES = 128
GROUPS = LANES // STRIP
TILE = 16
PIVOTS = 16
VMEM_BYTES = 24 * 1024 * 1024


def area_weight(total_rows):
    row_index = np.arange(total_rows).astype(np.float32)
    step = np.float32(180.0 / total_rows)
    latitude = np.float32(-90.0) + (row_index + np.float32(0.5)) * step
    return np.sqrt(np.cos(latitude * np.float32(math.pi / 180.0))).astype(np.float32)


def hi_lo(values):
    hi = values.astype(jnp.bfloat16)
    lo = (values - hi.astype(jnp.float32)).astype(jnp.bfloat16)
    return hi, lo


def band(in_cols, out_cols):
    offset = np.abs(np.asarray(in_cols)[:, None] - np.asarray(out_cols)[None, :])
    table = np.asarray(stencil_weights, np.float32)
    return np.where(offset <= 4, table[np.minimum(offset, 4)], np.float32(0.0)).astype(np.float32)


def two_terms(matrix):
    hi = matrix.astype(jnp.bfloat16)
    lo = (matrix - hi.astype(np.float32)).astype(jnp.bfloat16)
    return np.concatenate([hi, lo], axis=1)


def block_diagonal(matrix):
    return np.kron(np.eye(GROUPS, dtype=np.float32), matrix)


def zonal_matrices():
    own = np.arange(LANES)
    outer = np.concatenate([np.arange(-HALO, 0), LANES + np.arange(HALO)])
    inner = np.concatenate([np.arange(LANES - HALO, LANES), np.arange(HALO)])
    main = two_terms(band(own, own))
    near = band(outer, outer)
    far = band(inner, outer)
    inward = band(outer, inner)
    near[:HALO, HALO:] = near[HALO:, :HALO] = 0.0
    within = band(inner, inner)
    within[:HALO, HALO:] = within[HALO:, :HALO] = 0.0
    near, far, inward, within = [
        two_terms(block_diagonal(part)) for part in (near, far, inward, within)
    ]
    edge = np.concatenate([near, near, far, far], axis=0)
    again = np.concatenate([inward, inward, within, within], axis=0)
    inward = np.concatenate([inward, inward], axis=0)
    inward_only = np.concatenate([inward, np.zeros_like(inward)], axis=0)
    return np.concatenate([main, main], axis=0), np.concatenate([edge, inward_only], axis=1), again


def strip_kernel(span, field_ref, ext_ref, strip_ref):
    snaps, rows, _ = field_ref.shape

    def turn(at, carry):
        begin = pl.multiple_of(at * 8, 8)
        for tile in range(0, snaps, 8):
            ext_ref[pl.ds(4 + HALO + begin, 8), tile : tile + 8] = jnp.swapaxes(
                field_ref[tile : tile + 8, pl.ds(begin, 8), :], 0, 1
            )
        return carry

    lax.fori_loop(0, rows // 8, turn, 0, unroll=16)
    ends = jnp.zeros((4 + HALO, snaps, LANES), jnp.float32)
    ext_ref[: 4 + HALO] = ends
    ext_ref[4 + HALO + rows :] = ends
    group_of = lax.broadcasted_iota(jnp.int32, (snaps, LANES), 1) // STRIP

    def pack(at, carry):
        packed = jnp.zeros((snaps, LANES), jnp.float32)
        for group in range(GROUPS):
            values = ext_ref[4 + group * span + at]
            moved = pltpu.roll(values, (HALO + STRIP * group) % LANES, 1)
            packed = jnp.where(group_of == group, moved, packed)
        strip_ref[at] = packed
        return carry

    lax.fori_loop(0, span, pack, 0, unroll=span)


def message_kernel(
    span, ext_in_ref, strip_ref, low_ref, high_ref, ext_ref, full_ref, first_ref, second_ref
):
    snaps = strip_ref.shape[1]
    half = span // 2
    end = ext_ref.shape[0] - 4 - HALO
    lane = lax.broadcasted_iota(jnp.int32, (snaps, LANES), 1)
    lat = lax.axis_index("lat")
    last_lat = lax.axis_size("lat") - 1
    lat_even = lat % 2 == 0
    lon_even = lax.axis_index("lon") % 2 == 0
    full_ref[...] = strip_ref[...]
    for tile in range(0, snaps, 8):
        first = jnp.swapaxes(low_ref[tile : tile + 8], 0, 1)
        second = jnp.swapaxes(high_ref[tile : tile + 8], 0, 1)
        north = jnp.where(lat_even, second, first)
        south = jnp.where(lat_even, first, second)
        ext_ref[4 : 4 + HALO, tile : tile + 8] = jnp.where(lat == 0, 0.0, north)
        ext_ref[end : end + HALO, tile : tile + 8] = jnp.where(lat == last_lat, 0.0, south)
    for at in range(HALO):
        north, south = ext_ref[4 + at], ext_ref[end + at]
        full_ref[at] = jnp.where(lane < STRIP, pltpu.roll(north, HALO, 1), full_ref[at])
        last = span - HALO + at
        full_ref[last] = jnp.where(
            lane >= LANES - STRIP, pltpu.roll(south, LANES - HALO, 1), full_ref[last]
        )
    left = lane % STRIP < HALO
    for at in range(half):
        upper, lower = full_ref[at], full_ref[at + half]
        eastward = jnp.where(left, upper, pltpu.roll(lower, HALO, 1))
        westward = jnp.where(left, pltpu.roll(lower, LANES - HALO, 1), upper)
        first_ref[at] = jnp.where(lon_even, eastward, westward)
        second_ref[at] = jnp.where(lon_even, westward, eastward)


def stencil_row(center, pairs, zonal, zonal_rate, merid_rate, weight=None):
    merid = stencil_weights[1] * pairs[0]
    for offset in range(2, 5):
        merid = merid + stencil_weights[offset] * pairs[offset - 1]
    scale = 1.0 + stencil_weights[0] * merid_rate
    if weight is not None:
        scale, merid_rate, zonal_rate = scale * weight, merid_rate * weight, zonal_rate * weight
    return scale * center + merid_rate * merid + zonal_rate * zonal


def zonal_terms(parts, weights):
    product = jnp.dot(
        jnp.concatenate(parts, axis=1), weights, preferred_element_type=jnp.float32
    )
    return product[:, :LANES] + product[:, LANES:]


def rate_reader(rows, rates_refs):
    last = rows * lax.axis_size("lat") - 1
    origin = lax.axis_index("lat") * rows - HALO

    def read(at):
        row = jnp.clip(origin + at, 0, last)
        return [ref[row] for ref in rates_refs]

    return read


def stencil_rows(load, begin, span, part, rates, store):
    loaded = {}

    def row(at):
        if at not in loaded:
            loaded[at] = load(begin + at)
        return loaded[at]

    for at in range(span):
        here = at + 4
        pairs = [row(here + offset) + row(here - offset) for offset in range(1, 5)]
        store(at, stencil_row(row(here), pairs, part[at], *rates(begin + at)))


def tile_kernel(
    span, lon_ref, lat_ref, weight_ref, ext_ref, main_ref, twice_ref, strip_rates_ref, once_ref
):
    snaps = ext_ref.shape[1]
    total = span * GROUPS
    rows = total - 2 * HALO
    plain = rate_reader(rows, (lon_ref, lat_ref))
    weighted = rate_reader(rows, (lon_ref, lat_ref, weight_ref))
    ends = jnp.zeros((4, TILE, LANES), jnp.float32)
    once_ref[:4] = ends
    once_ref[total + 4 :] = ends
    outside = jnp.zeros((HALO, TILE, LANES), jnp.float32)

    def one_tile(tile, carry):
        snap = pl.ds(pl.multiple_of(tile * TILE, TILE), TILE)

        def one_pass(load, rates, store):
            center = load(slice(4, 4 + total)).reshape(total * TILE, LANES)
            part = zonal_terms(hi_lo(center), main_ref[...]).reshape(total, TILE, LANES)
            stencil_rows(load, 0, total, part, rates, store)

        def store_once(at, value):
            once_ref[4 + at] = value

        def store_twice(at, value):
            twice_ref[at, snap] = value

        one_pass(lambda at: ext_ref[at, snap], plain, store_once)

        @pl.when(lax.axis_index("lat") == 0)
        def _():
            once_ref[4 : 4 + HALO] = outside

        @pl.when(lax.axis_index("lat") == lax.axis_size("lat") - 1)
        def _():
            once_ref[4 + HALO + rows : 4 + total] = outside

        one_pass(lambda at: once_ref[at], weighted, store_twice)
        return carry

    lax.fori_loop(0, snaps // TILE, one_tile, 0, unroll=True)
    outside = jnp.zeros((HALO, snaps, LANES), jnp.float32)
    twice_ref[:HALO] = outside
    twice_ref[HALO + rows :] = outside
    lane_group = lax.broadcasted_iota(jnp.int32, (8, LANES), 1) // STRIP
    for at in range(span):
        values_at = [jnp.zeros((8, LANES), jnp.float32)] * 3
        for group in range(GROUPS):
            here = lane_group == group
            row = group * span + at
            values = weighted(row)
            if row < HALO or row >= HALO + rows:
                values[2] = 0.0
            values_at = [jnp.where(here, value, old) for value, old in zip(values, values_at)]
        for kind in range(3):
            strip_rates_ref[kind, at] = values_at[kind]


def close_ends(strip_ref, span):
    for at in range(4):
        strip_ref[at] = pltpu.roll(strip_ref[span + at], STRIP, 1)
        strip_ref[span + 4 + at] = pltpu.roll(strip_ref[4 + at], LANES - STRIP, 1)


def rim_kernel(
    span,
    twice_ref,
    strip_ref,
    strip_rates_ref,
    first_ref,
    second_ref,
    edge_ref,
    again_ref,
    split_ref,
    gram_ref,
    outer_ref,
    side_ref,
    added_ref,
    rim_ref,
):
    both = split_ref.shape[1]
    snaps = both // 2
    half = span // 2
    lon_even = lax.axis_index("lon") % 2 == 0
    lane = lax.broadcasted_iota(jnp.int32, (TILE, LANES), 1)
    left = lane % STRIP < HALO
    rim = (lane < HALO) | (lane >= LANES - HALO)
    def strip_rate(kind, at):
        return jnp.concatenate([strip_rates_ref[kind, at]] * (TILE // 8), axis=0)

    def strip_stencil(source_ref, at, zonal):
        pairs = [
            source_ref[4 + at + offset] + source_ref[4 + at - offset] for offset in range(1, 5)
        ]
        return stencil_row(
            source_ref[4 + at], pairs, zonal, strip_rate(0, at), strip_rate(1, at)
        )

    for tile in range(0, snaps, TILE):
        snap = slice(tile, tile + TILE)
        for at in range(half):
            first, second = first_ref[at, snap], second_ref[at, snap]
            west = jnp.where(lon_even, second, first)
            east = jnp.where(lon_even, first, second)
            outer_ref[4 + at] = jnp.where(left, west, east)
            outer_ref[4 + half + at] = jnp.where(
                left, pltpu.roll(west, LANES - HALO, 1), pltpu.roll(east, HALO, 1)
            )
        close_ends(outer_ref, span)
        hi, lo = hi_lo(outer_ref[4 : 4 + span].reshape(span * TILE, LANES))
        own_hi, own_lo = hi_lo(strip_ref[:, snap].reshape(span * TILE, LANES))
        product = jnp.dot(
            jnp.concatenate([hi, lo, own_hi, own_lo], axis=1),
            edge_ref[...],
            preferred_element_type=jnp.float32,
        ).reshape(span, TILE, 4 * LANES)
        for at in range(span):
            zonal = product[at, :, :LANES] + product[at, :, LANES : 2 * LANES]
            side_ref[at] = strip_stencil(outer_ref, at, zonal)
            added_ref[4 + at] = strip_rate(0, at) * (
                product[at, :, 2 * LANES : 3 * LANES] + product[at, :, 3 * LANES :]
            )
        close_ends(added_ref, span)
        hi, lo = hi_lo(side_ref[...].reshape(span * TILE, LANES))
        own_hi, own_lo = hi_lo(added_ref[4 : 4 + span].reshape(span * TILE, LANES))
        part = zonal_terms([hi, lo, own_hi, own_lo], again_ref[...]).reshape(span, TILE, LANES)
        for at in range(span):
            rim_ref[at, snap] = strip_rate(2, at) * strip_stencil(added_ref, at, part[at])

    def finish(group, grams):
        begin = group * span
        shift = LANES - HALO - STRIP * group
        for pair in range(0, span, 2):
            rows_done = []
            for at in (pair, pair + 1):
                terms = []
                for tile in range(0, snaps, TILE):
                    snap = slice(tile, tile + TILE)
                    moved = pltpu.roll(rim_ref[at, snap], shift, 1)
                    value = twice_ref[begin + at, snap] + jnp.where(rim, moved, 0.0)
                    terms.append(hi_lo(value))
                row = jnp.concatenate(
                    [term[0] for term in terms] + [term[1] for term in terms], axis=0
                )
                split_ref[begin + at] = row
                rows_done.append(row)
            two = jnp.concatenate(rows_done, axis=1)
            grams = grams + lax.dot_general(
                two, two, (((1,), (1,)), ((), ())), preferred_element_type=jnp.float32
            )
        return grams

    grams = lax.fori_loop(0, GROUPS, finish, jnp.zeros((both, both), jnp.float32), unroll=4)
    gram = (
        grams[:snaps, :snaps]
        + grams[snaps:, snaps:]
        + (grams[:snaps, snaps:] + grams[snaps:, :snaps])
    )
    gram_ref[...] = jnp.concatenate([gram[at : at + 8] for at in range(0, snaps, 8)], axis=1)


def basis_kernel(root_count, gram_ref, split_ref, basis_ref, factor_ref, left_ref):
    snaps = basis_ref.shape[0]

    @pl.when(pl.program_id(0) == 0)
    def _():
        row = lax.broadcasted_iota(jnp.int32, (snaps, 2 * snaps), 0)
        col = lax.broadcasted_iota(jnp.int32, (snaps, 2 * snaps), 1)
        packed = jnp.sum(gram_ref[...], axis=0)
        gram = jnp.concatenate(
            [packed[:, at : at + snaps] for at in range(0, packed.shape[1], snaps)], axis=0
        )
        work = jnp.concatenate([gram, jnp.zeros((snaps, snaps), jnp.float32)], axis=1)
        work = jnp.where(col == row + snaps, 1.0, work)
        for step in range(0, snaps, PIVOTS):
            below = [
                jnp.broadcast_to(work[:, pivot : pivot + 1], work.shape)
                for pivot in range(step, step + PIVOTS)
            ]
            across = [work[pivot : pivot + 1, :] for pivot in range(step, step + PIVOTS)]
            for at in range(PIVOTS):
                pivot = step + at
                ratio = 1.0 / below[at][pivot : pivot + 1, :]
                rest = jnp.where(row > pivot, below[at], 0.0)
                work = work - (rest * ratio) * across[at]
                for later in range(at + 1, PIVOTS):
                    factor = below[later][pivot : pivot + 1, :] * ratio
                    below[later] = below[later] - rest * factor
                    across[later] = across[later] - factor * across[at]
        diagonal = jnp.sum(jnp.where(row == col, work, 0.0), axis=1, keepdims=True)
        work = work * lax.rsqrt(diagonal)
        upper = jnp.where(col >= row, work, 0.0)
        factor_ref[...] = upper[:, :snaps] / root_count
        hi, lo = hi_lo(work[:, snaps:] * root_count)
        left_ref[:snaps] = jnp.concatenate([hi, hi], axis=1)
        left_ref[snaps:] = jnp.concatenate([lo, jnp.zeros_like(lo)], axis=1)

    left = left_ref[...]
    start = pl.program_id(0) * basis_ref.shape[1] + HALO

    def body(at, carry):
        begin = pl.multiple_of(at * 16, 16)
        values = []
        for pair in range(8):
            row = start + begin + 2 * pair
            two = jnp.concatenate([split_ref[row], split_ref[row + 1]], axis=1)
            product = jnp.dot(left, two, preferred_element_type=jnp.float32)
            value = product[:snaps] + product[snaps:]
            values += [value[:, :LANES], value[:, LANES:]]
        turned = jnp.swapaxes(jnp.stack(values, axis=0), 0, 1)
        basis_ref[:, pl.ds(begin, 16), :] = turned.astype(jnp.bfloat16)
        return carry

    lax.fori_loop(0, basis_ref.shape[1] // 16, body, 0, unroll=8)


def pair_permutes(values, axis):
    count = lax.axis_size(axis)
    inner = [(i, i ^ 1) for i in range(count)]
    outer = [(i, (i + 1 if i % 2 else i - 1) % count) for i in range(count)]
    return lax.ppermute(values[0], axis, inner), lax.ppermute(values[1], axis, outer)


def gather_all(values):
    axes = ("lat", "lon")
    count = lax.axis_size(axes)
    return lax.all_to_all(jnp.broadcast_to(values, (count,) + values.shape), axes, 0, 0)


def whole(memory_space=pltpu.VMEM):
    return pl.BlockSpec(memory_space=memory_space)


def shards(field, lon_rate, lat_rate):
    snaps, rows, cols = field.shape
    total_rows = rows * lax.axis_size("lat")
    total_cells = total_rows * cols * lax.axis_size("lon")
    span = (rows + 2 * HALO) // GROUPS
    f32 = jnp.float32
    limits = pltpu.CompilerParams(vmem_limit_bytes=VMEM_BYTES)

    total = span * GROUPS
    ext = jax.ShapeDtypeStruct((total + 8, snaps, cols), f32)
    strip = jax.ShapeDtypeStruct((span, snaps, cols), f32)
    half = jax.ShapeDtypeStruct((span // 2, snaps, cols), f32)
    weight = area_weight(total_rows)
    begin = jnp.where(lax.axis_index("lat") % 2 == 0, rows - HALO, 0)
    low, high = pair_permutes(
        [
            lax.dynamic_slice_in_dim(field, start, HALO, axis=1)
            for start in (begin, rows - HALO - begin)
        ],
        "lat",
    )
    turned, packed = pl.pallas_call(
        functools.partial(strip_kernel, span),
        in_specs=[whole()],
        out_specs=[whole()] * 2,
        out_shape=[ext, strip],
        compiler_params=limits,
        name="turn_and_pack",
    )(field)
    turned, packed, first, second = pl.pallas_call(
        functools.partial(message_kernel, span),
        in_specs=[whole()] * 4,
        out_specs=[whole()] * 4,
        out_shape=[ext, strip, half, half],
        input_output_aliases={0: 0},
        compiler_params=limits,
        name="lon_messages",
    )(turned, packed, low, high)
    first, second = pair_permutes([first, second], "lon")

    main, edge, again = zonal_matrices()
    bf16 = jnp.bfloat16
    twice, strip_rates = pl.pallas_call(
        functools.partial(tile_kernel, span),
        in_specs=[whole(pltpu.SMEM)] * 3 + [whole()] * 2,
        out_specs=[whole()] * 2,
        out_shape=[
            jax.ShapeDtypeStruct((total, snaps, cols), f32),
            jax.ShapeDtypeStruct((3, span, 8, cols), f32),
        ],
        scratch_shapes=[pltpu.VMEM((total + 8, TILE, cols), f32)],
        compiler_params=limits,
        cost_estimate=pl.CostEstimate(
            flops=100 * snaps * rows * cols, bytes_accessed=8 * snaps * rows * cols, transcendentals=0
        ),
        name="both_passes",
    )(lon_rate, lat_rate, weight, turned, main)
    split, gram = pl.pallas_call(
        functools.partial(rim_kernel, span),
        in_specs=[whole()] * 7,
        out_specs=[whole(), whole()],
        out_shape=[
            jax.ShapeDtypeStruct((total, 2 * snaps, cols), bf16),
            jax.ShapeDtypeStruct((8, snaps // 8 * snaps), f32),
        ],
        scratch_shapes=[
            pltpu.VMEM((span + 8, TILE, cols), f32),
            pltpu.VMEM((span, TILE, cols), f32),
            pltpu.VMEM((span + 8, TILE, cols), f32),
            pltpu.VMEM((span, snaps, cols), f32),
        ],
        compiler_params=limits,
        name="rim_and_gram",
    )(twice, packed, strip_rates, first, second, edge, again)

    grams = gather_all(gram)
    block = 128
    basis, factor = pl.pallas_call(
        functools.partial(basis_kernel, math.sqrt(total_cells)),
        grid=(rows // block,),
        in_specs=[
            whole(),
            whole(),
        ],
        out_specs=[
            pl.BlockSpec((snaps, block, cols), lambda i: (0, i, 0)),
            pl.BlockSpec((snaps, snaps), lambda i: (0, 0)),
        ],
        out_shape=[
            jax.ShapeDtypeStruct((snaps, rows, cols), bf16),
            jax.ShapeDtypeStruct((snaps, snaps), f32),
        ],
        scratch_shapes=[
            pltpu.VMEM((2 * snaps, 2 * snaps), bf16),
        ],
        compiler_params=limits,
        name="factor_and_basis",
    )(grams, split)
    return (basis, factor)


def solution(mesh):
    return jax.shard_map(
        shards,
        mesh=mesh,
        in_specs=(P(None, "lat", "lon"), P(), P()),
        out_specs=(P(None, "lat", "lon"), P()),
        check_vma=False,
    )
```
